32 devices in a mesh: dp: 4 (over y, core), fsdp: 8 (over z, x).
Axes of the slice: x: 2, y: 2, z: 4, core: 2. Of those that a mesh axis runs over, the one named last changes fastest.
Arguments:
- frames: bfloat16 [16384, 768], P(('dp', 'fsdp')), may hold values from -6 to 6
- lengths: int32 [32, 2], P(('dp', 'fsdp')), may hold values from 0 to 512, as said below
- query_weight: bfloat16 [768, 768], P(('dp', 'fsdp')), may hold values from -0.21875 to 0.21875
- query_bias: bfloat16 [768], P(('dp', 'fsdp')), may hold values from -3 to 3
- key_weight: bfloat16 [768, 768], P(('dp', 'fsdp')), may hold values from -0.21875 to 0.21875
- value_weight: bfloat16 [768, 768], P(('dp', 'fsdp')), may hold values from -0.21875 to 0.21875
- value_bias: bfloat16 [768], P(('dp', 'fsdp')), may hold values from -3 to 3
- output_weight: bfloat16 [768, 768], P(('dp', 'fsdp')), may hold values from -2.5 to 2.5
- output_bias: bfloat16 [768], P(('dp', 'fsdp')), may hold values from -3 to 3
- first_gain: bfloat16 [768], P(('dp', 'fsdp')), may hold values from 0.5 to 1.5
- first_shift: bfloat16 [768], P(('dp', 'fsdp')), may hold values from -3 to 3
- inner_weight: bfloat16 [768, 3072], P(('dp', 'fsdp')), may hold values from -0.21875 to 0.21875
- inner_bias: bfloat16 [3072], P(('dp', 'fsdp')), may hold values from -3 to 3
- outer_weight: bfloat16 [3072, 768], P(('dp', 'fsdp')), may hold values from -0.109375 to 0.109375
- outer_bias: bfloat16 [768], P(('dp', 'fsdp')), may hold values from -3 to 3
- second_gain: bfloat16 [768], P(('dp', 'fsdp')), may hold values from 0.5 to 1.5
- second_shift: bfloat16 [768], P(('dp', 'fsdp')), may hold values from -3 to 3
- grad_out: bfloat16 [16384, 768], P(('dp', 'fsdp')), may hold values from -6 to 6
Outputs:
- layer_out: bfloat16 [16384, 768], P(('dp', 'fsdp'))
- frames_grad: bfloat16 [16384, 768], P(('dp', 'fsdp'))
- query_weight_grad: float32 [768, 768], P(('dp', 'fsdp'))
- query_bias_grad: float32 [768], P(('dp', 'fsdp'))
- key_weight_grad: float32 [768, 768], P(('dp', 'fsdp'))
- value_weight_grad: float32 [768, 768], P(('dp', 'fsdp'))
- value_bias_grad: float32 [768], P(('dp', 'fsdp'))
- output_weight_grad: float32 [768, 768], P(('dp', 'fsdp'))
- output_bias_grad: float32 [768], P(('dp', 'fsdp'))
- first_gain_grad: float32 [768], P(('dp', 'fsdp'))
- first_shift_grad: float32 [768], P(('dp', 'fsdp'))
- inner_weight_grad: float32 [768, 3072], P(('dp', 'fsdp'))
- inner_bias_grad: float32 [3072], P(('dp', 'fsdp'))
- outer_weight_grad: float32 [3072, 768], P(('dp', 'fsdp'))
- outer_bias_grad: float32 [768], P(('dp', 'fsdp'))
- second_gain_grad: float32 [768], P(('dp', 'fsdp'))
- second_shift_grad: float32 [768], P(('dp', 'fsdp'))
The draws below stay inside these ranges and needn't reach their ends.
Inputs may be any that keep to these rules, and one draw needn't show every extreme that they name: `lengths`: row b holds block b's two utterances: slot 0 has 100 to 512 frames, slot 1 has 0 (empty) up to 512 minus slot 0; the block's remaining slots are padding. In one block, drawn from the seed, slot 0 fills all 512 slots.
All inputs are finite; a program needn't handle non-finite values.
Results may differ from the reference program's by a relative error of at most 0.015.
Values may be sent and summed in bfloat16 or wider, within the bound.
A program may use at most 192 MiB of HBM per device.

```python
import jax
import jax.numpy as jnp
from jax import lax

D = 768
HEADS = 12
HEAD_DIM = 64
FF = 3072
FRAMES_DEV = 512
LEN_MIN = 100
NUM_SHARDS = 32
FRAMES = 16384


def draw_lengths(key, part):
    key = jax.random.fold_in(key, 11)
    first_key, second_key, chosen_key = jax.random.split(key, 3)
    first_len = jax.random.randint(first_key, (NUM_SHARDS,), LEN_MIN, FRAMES_DEV + 1)
    second_len = jax.random.randint(second_key, (NUM_SHARDS,), 0, FRAMES_DEV - first_len + 1)
    chosen = jax.random.randint(chosen_key, (), 0, NUM_SHARDS)
    places = jnp.arange(NUM_SHARDS)
    first_len = jnp.where(places == chosen, FRAMES_DEV, first_len)
    second_len = jnp.where(places == chosen, 0, second_len)
    return jnp.stack([first_len, second_len], axis=1).astype(jnp.int32)


def levels(rng, extent, cuts, smallest, top_value):
    def one(position, shards_of):
        steps = jax.random.uniform(jax.random.fold_in(jax.random.fold_in(rng, 6), position), (shards_of,), jnp.float32, smallest / len(cuts), top_value / len(cuts))
        return jnp.repeat(jnp.exp(steps), extent[position] // shards_of).reshape((-1,) + (1,) * (len(extent) - position - 1))

    factor_of = one(*cuts[0])
    for cut in cuts[1:]:
        factor_of = factor_of * one(*cut)
    return factor_of


def centred(key, dims, scale, bound, pieces=(), held_as=jnp.bfloat16):
    array = scale * jax.random.normal(key, dims, jnp.float32)
    if pieces:
        array = array * levels(key, dims, pieces, -0.22, 0.18)
    return jnp.clip(array, -bound, bound).astype(held_as)


def setup_inputs(seed: int = 0) -> dict:
    arg_keys = jax.random.split(jax.random.key(seed), 19)
    return {
        "frames": centred(arg_keys[0], (FRAMES, D), 1.0, 6.0, ((0, 32),)),
        "lengths": draw_lengths(jax.random.fold_in(arg_keys[18], 71), 0),
        "query_weight": centred(arg_keys[2], (D, D), D ** -0.5, 0.21875, ((0, 32),)),
        "query_bias": centred(arg_keys[3], (D,), 0.5, 3.0, ((0, 32),)),
        "key_weight": centred(arg_keys[4], (D, D), D ** -0.5, 0.21875, ((0, 32),)),
        "value_weight": centred(arg_keys[5], (D, D), D ** -0.5, 0.21875, ((0, 32),)),
        "value_bias": centred(arg_keys[6], (D,), 0.5, 3.0, ((0, 32),)),
        "output_weight": centred(arg_keys[7], (D, D), (D // 128) ** -0.5, 2.5, ((0, 32),)),
        "output_bias": centred(arg_keys[8], (D,), 0.5, 3.0, ((0, 32),)),
        "first_gain": jnp.clip(1.0 + 0.1 * jax.random.normal(arg_keys[9], (D,), jnp.float32), 0.5, 1.5).astype(jnp.bfloat16),
        "first_shift": centred(arg_keys[10], (D,), 0.5, 3.0, ((0, 32),)),
        "inner_weight": centred(arg_keys[11], (D, FF), D ** -0.5, 0.21875, ((0, 32),)),
        "inner_bias": centred(arg_keys[12], (FF,), 0.5, 3.0, ((0, 32),)),
        "outer_weight": centred(arg_keys[13], (FF, D), FF ** -0.5, 0.109375, ((0, 32),)),
        "outer_bias": centred(arg_keys[14], (D,), 0.5, 3.0, ((0, 32),)),
        "second_gain": jnp.clip(1.0 + 0.1 * jax.random.normal(arg_keys[15], (D,), jnp.float32), 0.5, 1.5).astype(jnp.bfloat16),
        "second_shift": centred(arg_keys[16], (D,), 0.5, 3.0, ((0, 32),)),
        "grad_out": centred(arg_keys[17], (FRAMES, D), 1.0, 6.0, ((0, 32),)),
    }


@jax.custom_vjp
def low(v):
    return lax.optimization_barrier(v.astype(jnp.bfloat16)).astype(jnp.float32)

@jax.custom_vjp
def low_back(v):
    return v

def low_keep(v):
    return (low(v), None)

def low_pass(kept, grad):
    return (grad,)

def back_keep(v):
    return (v, None)

def back_low(kept, grad):
    return (low(grad),)
low.defvjp(low_keep, low_pass)
low_back.defvjp(back_keep, back_low)
HIGHEST = lax.Precision.HIGHEST

def layer_norm(values, gain_vec, shift_vec):
    center = values - lax.optimization_barrier(jnp.mean(values, axis=-1, keepdims=True))
    spread = lax.optimization_barrier(jnp.mean(center * center, axis=-1, keepdims=True))
    return center * lax.rsqrt(spread + 1e-05) * gain_vec + shift_vec

def exact_gelu(values):
    return jax.nn.gelu(values, approximate=False)

def layer_block(frame_block, utt_lengths, params):
    query_mat, query_vec, key_mat, value_mat, value_vec, output_mat, output_vec, first_scale, first_offset, inner_mat, inner_vec, outer_mat, outer_vec, second_scale, second_offset = params
    places = jnp.arange(FRAMES_DEV, dtype=jnp.int32)
    bounds = jnp.cumsum(utt_lengths).astype(jnp.int32)
    groups = lax.optimization_barrier(jnp.sum((places[:, None] >= bounds[None, :]).astype(jnp.int32), axis=1)).astype(jnp.int32)
    live_mask = (places < bounds[-1]).astype(jnp.float32)
    allowed = groups[:, None] == groups[None, :]
    score_scale = HEAD_DIM ** (-0.5)
    queries = low(low_back(jnp.dot(frame_block, query_mat, precision=HIGHEST) + query_vec))
    keyset = low(low_back(jnp.dot(frame_block, key_mat, precision=HIGHEST)))
    valueset = low(low_back(jnp.dot(frame_block, value_mat, precision=HIGHEST) + value_vec))
    queries = queries.reshape(FRAMES_DEV, HEADS, HEAD_DIM)
    keyset = keyset.reshape(FRAMES_DEV, HEADS, HEAD_DIM)
    valueset = valueset.reshape(FRAMES_DEV, HEADS, HEAD_DIM)
    scores = low_back(jnp.einsum('qhd,khd->hqk', queries, keyset, precision=HIGHEST) * score_scale)
    scores = jnp.where(allowed[None], scores, -1e+30)
    row_max = lax.optimization_barrier(jnp.max(scores, axis=-1, keepdims=True))
    raw_weights = jnp.exp(scores - row_max)
    attn_prob = raw_weights / lax.optimization_barrier(jnp.sum(raw_weights, axis=-1, keepdims=True))
    context = jnp.einsum('hqk,khd->qhd', low(attn_prob), valueset, precision=HIGHEST)
    context = low(low_back(context.reshape(FRAMES_DEV, HEADS * HEAD_DIM)))
    attn_out = low_back(jnp.dot(context, output_mat, precision=HIGHEST) + output_vec)
    hidden = layer_norm(frame_block + attn_out, first_scale, first_offset)
    inner_pre = low_back(jnp.dot(low(hidden), inner_mat, precision=HIGHEST) + inner_vec)
    active = low(exact_gelu(inner_pre))
    outer_out = low_back(jnp.dot(active, outer_mat, precision=HIGHEST) + outer_vec)
    return layer_norm(hidden + outer_out, second_scale, second_offset) * live_mask[:, None]

def reference(frames, lengths, query_weight, query_bias, key_weight, value_weight, value_bias, output_weight, output_bias, first_gain, first_shift, inner_weight, inner_bias, outer_weight, outer_bias, second_gain, second_shift, grad_out):
    params = tuple((item.astype(jnp.float32) for item in (query_weight, query_bias, key_weight, value_weight, value_bias, output_weight, output_bias, first_gain, first_shift, inner_weight, inner_bias, outer_weight, outer_bias, second_gain, second_shift)))
    blocks = frames.astype(jnp.float32).reshape(NUM_SHARDS, FRAMES_DEV, D)
    block_step = jax.checkpoint(layer_block)

    def forward(block_set, param_set):
        return lax.map(lambda item: block_step(item[0], item[1], param_set), (block_set, lengths))
    outputs, pull = jax.vjp(forward, blocks, params)
    block_grads, param_grads = pull(grad_out.astype(jnp.float32).reshape(NUM_SHARDS, FRAMES_DEV, D))
    return (outputs.reshape(FRAMES_DEV * NUM_SHARDS, D).astype(jnp.bfloat16), block_grads.reshape(FRAMES_DEV * NUM_SHARDS, D).astype(jnp.bfloat16), param_grads[0], param_grads[1], param_grads[2], param_grads[3], param_grads[4], param_grads[5], param_grads[6], param_grads[7], param_grads[8], param_grads[9], param_grads[10], param_grads[11], param_grads[12], param_grads[13], param_grads[14])
```

```python
import jax
import jax.numpy as jnp
from jax import lax
from jax.sharding import PartitionSpec as P

HEADS = 12


def layer_norm(values, gain_vec, shift_vec):
    center = values - jnp.mean(values, axis=-1, keepdims=True)
    spread = jnp.mean(center * center, axis=-1, keepdims=True)
    return center * lax.rsqrt(spread + 1e-05) * gain_vec + shift_vec


def exact_gelu(values):
    return jax.nn.gelu(values, approximate=False)


def matmul(left_side, right_side):
    return jnp.dot(left_side, right_side, preferred_element_type=jnp.float32)


def matmul_tn(left_side, right_side):
    return lax.dot_general(
        left_side, right_side, (((0,), (0,)), ((), ())), preferred_element_type=jnp.float32
    )


def matmul_nt(left_side, right_side):
    return lax.dot_general(
        left_side, right_side, (((1,), (1,)), ((), ())), preferred_element_type=jnp.float32
    )


def column_sums(values):
    return jnp.sum(values.astype(jnp.float32), axis=0)


def block_scores(query_block, key_heads, group_block, groups, score_scale):
    raw_scores = (
        jnp.einsum("qhd,khd->hqk", query_block, key_heads, preferred_element_type=jnp.float32)
        * score_scale
    )
    allowed = group_block[:, None] == groups[None, :]
    return jnp.where(allowed[None], raw_scores, -1e30)


def per_device(
    frames,
    lengths,
    query_weight,
    query_bias,
    key_weight,
    value_weight,
    value_bias,
    output_weight,
    output_bias,
    first_gain,
    first_shift,
    inner_weight,
    inner_bias,
    outer_weight,
    outer_bias,
    second_gain,
    second_shift,
    grad_out,
):
    frame_count = frames.shape[0]
    model_width = frames.shape[1]
    head_size = model_width // HEADS
    score_scale = head_size ** (-0.5)
    places = jnp.arange(frame_count, dtype=jnp.int32)
    bounds = jnp.stack([lengths[0, 0], lengths[0, 0] + lengths[0, 1]])
    groups = jnp.sum((places[:, None] >= bounds[None, :]).astype(jnp.int32), axis=1)
    live_mask = (places < bounds[-1]).astype(jnp.float32)
    gathered = (
        lax.all_gather(query_weight, ("dp", "fsdp"), axis=0, tiled=True),
        lax.all_gather(query_bias, ("dp", "fsdp"), axis=0, tiled=True),
        lax.all_gather(key_weight, ("dp", "fsdp"), axis=0, tiled=True),
        lax.all_gather(value_weight, ("dp", "fsdp"), axis=0, tiled=True),
        lax.all_gather(value_bias, ("dp", "fsdp"), axis=0, tiled=True),
        lax.all_gather(output_weight, ("dp", "fsdp"), axis=0, tiled=True),
        lax.all_gather(output_bias, ("dp", "fsdp"), axis=0, tiled=True),
        lax.all_gather(first_gain, ("dp", "fsdp"), axis=0, tiled=True),
        lax.all_gather(first_shift, ("dp", "fsdp"), axis=0, tiled=True),
        lax.all_gather(inner_weight, ("dp", "fsdp"), axis=0, tiled=True),
        lax.all_gather(inner_bias, ("dp", "fsdp"), axis=0, tiled=True),
        lax.all_gather(outer_weight, ("dp", "fsdp"), axis=0, tiled=True),
        lax.all_gather(outer_bias, ("dp", "fsdp"), axis=0, tiled=True),
        lax.all_gather(second_gain, ("dp", "fsdp"), axis=0, tiled=True),
        lax.all_gather(second_shift, ("dp", "fsdp"), axis=0, tiled=True),
    )
    (
        query_mat,
        query_vec,
        key_mat,
        value_mat,
        value_vec,
        output_mat,
        output_vec,
        first_scale,
        first_offset,
        inner_mat,
        inner_vec,
        outer_mat,
        outer_vec,
        second_scale,
        second_offset,
    ) = gathered
    query_rows = (matmul(frames, query_mat) + query_vec.astype(jnp.float32)).astype(jnp.bfloat16)
    key_rows = matmul(frames, key_mat).astype(jnp.bfloat16)
    value_rows = (matmul(frames, value_mat) + value_vec.astype(jnp.float32)).astype(jnp.bfloat16)
    query_heads = query_rows.reshape(frame_count, HEADS, head_size)
    key_heads = key_rows.reshape(frame_count, HEADS, head_size)
    value_heads = value_rows.reshape(frame_count, HEADS, head_size)
    scores = block_scores(query_heads, key_heads, groups, groups, score_scale)
    row_max = jnp.max(scores, axis=-1, keepdims=True)
    raw_weights = jnp.exp(scores - row_max)
    row_total = jnp.sum(raw_weights, axis=-1, keepdims=True)
    attn_prob = raw_weights / row_total
    log_totals = row_max + jnp.log(row_total)
    context_parts = jnp.einsum(
        "hqk,khd->qhd",
        attn_prob.astype(jnp.bfloat16),
        value_heads,
        preferred_element_type=jnp.float32,
    )
    context_rows = context_parts.reshape(frame_count, model_width).astype(jnp.bfloat16)
    frames_float = frames.astype(jnp.float32)
    resid_one = frames_float + matmul(context_rows, output_mat) + output_vec.astype(jnp.float32)
    hidden, first_pull = jax.vjp(
        layer_norm, resid_one, first_scale.astype(jnp.float32), first_offset.astype(jnp.float32)
    )
    hidden_low = hidden.astype(jnp.bfloat16)
    inner_pre = matmul(hidden_low, inner_mat) + inner_vec.astype(jnp.float32)
    active, gelu_pull = jax.vjp(exact_gelu, inner_pre)
    active_low = active.astype(jnp.bfloat16)
    outer_out = matmul(active_low, outer_mat) + outer_vec.astype(jnp.float32)
    normed_out, second_pull = jax.vjp(
        layer_norm,
        hidden + outer_out,
        second_scale.astype(jnp.float32),
        second_offset.astype(jnp.float32),
    )
    layer_out = (normed_out * live_mask[:, None]).astype(jnp.bfloat16)
    grad_top = grad_out.astype(jnp.float32) * live_mask[:, None]
    grad_two, second_gain_grad, second_shift_grad = second_pull(grad_top)
    grad_outer = grad_two.astype(jnp.bfloat16)
    outer_mat_grad = matmul_tn(active_low, grad_outer)
    outer_vec_grad = column_sums(grad_outer)
    (grad_inner,) = gelu_pull(matmul_nt(grad_outer, outer_mat))
    grad_inner_low = grad_inner.astype(jnp.bfloat16)
    inner_mat_grad = matmul_tn(hidden_low, grad_inner_low)
    inner_vec_grad = column_sums(grad_inner_low)
    grad_hidden = grad_two + matmul_nt(grad_inner_low, inner_mat)
    grad_one, first_gain_grad, first_shift_grad = first_pull(grad_hidden)
    grad_attn = grad_one.astype(jnp.bfloat16)
    output_mat_grad = matmul_tn(context_rows, grad_attn)
    output_vec_grad = column_sums(grad_attn)
    grad_context = (
        matmul_nt(grad_attn, output_mat).astype(jnp.bfloat16).reshape(frame_count, HEADS, head_size)
    )
    scores = block_scores(query_heads, key_heads, groups, groups, score_scale)
    attn_prob = jnp.exp(scores - log_totals)
    grad_prob = jnp.einsum(
        "qhd,khd->hqk", grad_context, value_heads, preferred_element_type=jnp.float32
    )
    inner_sum = jnp.sum(attn_prob * grad_prob, axis=-1, keepdims=True)
    grad_scores = (attn_prob * (grad_prob - inner_sum)).astype(jnp.bfloat16)
    query_grad_parts = (
        jnp.einsum("hqk,khd->qhd", grad_scores, key_heads, preferred_element_type=jnp.float32)
        * score_scale
    )
    key_grad_sum = (
        jnp.einsum("hqk,qhd->khd", grad_scores, query_heads, preferred_element_type=jnp.float32)
        * score_scale
    )
    value_grad_sum = jnp.einsum(
        "hqk,qhd->khd",
        attn_prob.astype(jnp.bfloat16),
        grad_context,
        preferred_element_type=jnp.float32,
    )
    grad_query = query_grad_parts.reshape(frame_count, model_width).astype(jnp.bfloat16)
    grad_key = key_grad_sum.reshape(frame_count, model_width).astype(jnp.bfloat16)
    grad_value = value_grad_sum.reshape(frame_count, model_width).astype(jnp.bfloat16)
    query_mat_grad = matmul_tn(frames, grad_query)
    query_vec_grad = column_sums(grad_query)
    key_mat_grad = matmul_tn(frames, grad_key)
    value_mat_grad = matmul_tn(frames, grad_value)
    value_vec_grad = column_sums(grad_value)
    frames_grad = (
        grad_one
        + matmul_nt(grad_query, query_mat)
        + matmul_nt(grad_key, key_mat)
        + matmul_nt(grad_value, value_mat)
    ).astype(jnp.bfloat16)
    shares = (
        lax.psum_scatter(query_mat_grad, ("dp", "fsdp"), scatter_dimension=0, tiled=True),
        lax.psum_scatter(query_vec_grad, ("dp", "fsdp"), scatter_dimension=0, tiled=True),
        lax.psum_scatter(key_mat_grad, ("dp", "fsdp"), scatter_dimension=0, tiled=True),
        lax.psum_scatter(value_mat_grad, ("dp", "fsdp"), scatter_dimension=0, tiled=True),
        lax.psum_scatter(value_vec_grad, ("dp", "fsdp"), scatter_dimension=0, tiled=True),
        lax.psum_scatter(output_mat_grad, ("dp", "fsdp"), scatter_dimension=0, tiled=True),
        lax.psum_scatter(output_vec_grad, ("dp", "fsdp"), scatter_dimension=0, tiled=True),
        lax.psum_scatter(first_gain_grad, ("dp", "fsdp"), scatter_dimension=0, tiled=True),
        lax.psum_scatter(first_shift_grad, ("dp", "fsdp"), scatter_dimension=0, tiled=True),
        lax.psum_scatter(inner_mat_grad, ("dp", "fsdp"), scatter_dimension=0, tiled=True),
        lax.psum_scatter(inner_vec_grad, ("dp", "fsdp"), scatter_dimension=0, tiled=True),
        lax.psum_scatter(outer_mat_grad, ("dp", "fsdp"), scatter_dimension=0, tiled=True),
        lax.psum_scatter(outer_vec_grad, ("dp", "fsdp"), scatter_dimension=0, tiled=True),
        lax.psum_scatter(second_gain_grad, ("dp", "fsdp"), scatter_dimension=0, tiled=True),
        lax.psum_scatter(second_shift_grad, ("dp", "fsdp"), scatter_dimension=0, tiled=True),
    )
    return (
        layer_out,
        frames_grad,
        shares[0],
        shares[1],
        shares[2],
        shares[3],
        shares[4],
        shares[5],
        shares[6],
        shares[7],
        shares[8],
        shares[9],
        shares[10],
        shares[11],
        shares[12],
        shares[13],
        shares[14],
    )


def solution(mesh):
    in_specs = (
        P(("dp", "fsdp"), None),
        P(("dp", "fsdp"), None),
        P(("dp", "fsdp"), None),
        P(("dp", "fsdp")),
        P(("dp", "fsdp"), None),
        P(("dp", "fsdp"), None),
        P(("dp", "fsdp")),
        P(("dp", "fsdp"), None),
        P(("dp", "fsdp")),
        P(("dp", "fsdp")),
        P(("dp", "fsdp")),
        P(("dp", "fsdp"), None),
        P(("dp", "fsdp")),
        P(("dp", "fsdp"), None),
        P(("dp", "fsdp")),
        P(("dp", "fsdp")),
        P(("dp", "fsdp")),
        P(("dp", "fsdp"), None),
    )
    out_specs = (
        P(("dp", "fsdp"), None),
        P(("dp", "fsdp"), None),
        P(("dp", "fsdp"), None),
        P(("dp", "fsdp")),
        P(("dp", "fsdp"), None),
        P(("dp", "fsdp"), None),
        P(("dp", "fsdp")),
        P(("dp", "fsdp"), None),
        P(("dp", "fsdp")),
        P(("dp", "fsdp")),
        P(("dp", "fsdp")),
        P(("dp", "fsdp"), None),
        P(("dp", "fsdp")),
        P(("dp", "fsdp"), None),
        P(("dp", "fsdp")),
        P(("dp", "fsdp")),
        P(("dp", "fsdp")),
    )
    return jax.shard_map(
        per_device, mesh=mesh, in_specs=in_specs, out_specs=out_specs, check_vma=False
    )
```

```python
import functools
from types import SimpleNamespace

import jax
import jax.numpy as jnp
from jax import lax
from jax.experimental import pallas as pl
from jax.experimental.pallas import tpu as pltpu
from jax.sharding import PartitionSpec as P

HEADS = 12


def layer_norm(values, gain_vec, shift_vec):
    center = values - jnp.mean(values, axis=-1, keepdims=True)
    spread = jnp.mean(center * center, axis=-1, keepdims=True)
    return center * lax.rsqrt(spread + 1e-05) * gain_vec + shift_vec


def exact_gelu(values):
    return jax.nn.gelu(values, approximate=False)


def matmul(left_side, right_side):
    return jnp.dot(left_side, right_side, preferred_element_type=jnp.float32)


def matmul_tn(left_side, right_side):
    return lax.dot_general(
        left_side, right_side, (((0,), (0,)), ((), ())), preferred_element_type=jnp.float32
    )


def matmul_nt(left_side, right_side):
    return lax.dot_general(
        left_side, right_side, (((1,), (1,)), ((), ())), preferred_element_type=jnp.float32
    )


def column_sums(values):
    return jnp.sum(values.astype(jnp.float32), axis=0)


def block_scores(query_block, key_heads, group_block, groups, score_scale):
    raw_scores = (
        jnp.einsum("qhd,khd->hqk", query_block, key_heads, preferred_element_type=jnp.float32)
        * score_scale
    )
    allowed = group_block[:, None] == groups[None, :]
    return jnp.where(allowed[None], raw_scores, -1e30)


def general_device(
    frames,
    lengths,
    query_weight,
    query_bias,
    key_weight,
    value_weight,
    value_bias,
    output_weight,
    output_bias,
    first_gain,
    first_shift,
    inner_weight,
    inner_bias,
    outer_weight,
    outer_bias,
    second_gain,
    second_shift,
    grad_out,
):
    frame_count = frames.shape[0]
    model_width = frames.shape[1]
    head_size = model_width // HEADS
    score_scale = head_size ** (-0.5)
    places = jnp.arange(frame_count, dtype=jnp.int32)
    bounds = jnp.stack([lengths[0, 0], lengths[0, 0] + lengths[0, 1]])
    groups = jnp.sum((places[:, None] >= bounds[None, :]).astype(jnp.int32), axis=1)
    live_mask = (places < bounds[-1]).astype(jnp.float32)
    gathered = (
        lax.all_gather(query_weight, ("dp", "fsdp"), axis=0, tiled=True),
        lax.all_gather(query_bias, ("dp", "fsdp"), axis=0, tiled=True),
        lax.all_gather(key_weight, ("dp", "fsdp"), axis=0, tiled=True),
        lax.all_gather(value_weight, ("dp", "fsdp"), axis=0, tiled=True),
        lax.all_gather(value_bias, ("dp", "fsdp"), axis=0, tiled=True),
        lax.all_gather(output_weight, ("dp", "fsdp"), axis=0, tiled=True),
        lax.all_gather(output_bias, ("dp", "fsdp"), axis=0, tiled=True),
        lax.all_gather(first_gain, ("dp", "fsdp"), axis=0, tiled=True),
        lax.all_gather(first_shift, ("dp", "fsdp"), axis=0, tiled=True),
        lax.all_gather(inner_weight, ("dp", "fsdp"), axis=0, tiled=True),
        lax.all_gather(inner_bias, ("dp", "fsdp"), axis=0, tiled=True),
        lax.all_gather(outer_weight, ("dp", "fsdp"), axis=0, tiled=True),
        lax.all_gather(outer_bias, ("dp", "fsdp"), axis=0, tiled=True),
        lax.all_gather(second_gain, ("dp", "fsdp"), axis=0, tiled=True),
        lax.all_gather(second_shift, ("dp", "fsdp"), axis=0, tiled=True),
    )
    (
        query_mat,
        query_vec,
        key_mat,
        value_mat,
        value_vec,
        output_mat,
        output_vec,
        first_scale,
        first_offset,
        inner_mat,
        inner_vec,
        outer_mat,
        outer_vec,
        second_scale,
        second_offset,
    ) = gathered
    query_rows = (matmul(frames, query_mat) + query_vec.astype(jnp.float32)).astype(jnp.bfloat16)
    key_rows = matmul(frames, key_mat).astype(jnp.bfloat16)
    value_rows = (matmul(frames, value_mat) + value_vec.astype(jnp.float32)).astype(jnp.bfloat16)
    query_heads = query_rows.reshape(frame_count, HEADS, head_size)
    key_heads = key_rows.reshape(frame_count, HEADS, head_size)
    value_heads = value_rows.reshape(frame_count, HEADS, head_size)
    scores = block_scores(query_heads, key_heads, groups, groups, score_scale)
    row_max = jnp.max(scores, axis=-1, keepdims=True)
    raw_weights = jnp.exp(scores - row_max)
    row_total = jnp.sum(raw_weights, axis=-1, keepdims=True)
    attn_prob = raw_weights / row_total
    log_totals = row_max + jnp.log(row_total)
    context_parts = jnp.einsum(
        "hqk,khd->qhd",
        attn_prob.astype(jnp.bfloat16),
        value_heads,
        preferred_element_type=jnp.float32,
    )
    context_rows = context_parts.reshape(frame_count, model_width).astype(jnp.bfloat16)
    frames_float = frames.astype(jnp.float32)
    resid_one = frames_float + matmul(context_rows, output_mat) + output_vec.astype(jnp.float32)
    hidden, first_pull = jax.vjp(
        layer_norm, resid_one, first_scale.astype(jnp.float32), first_offset.astype(jnp.float32)
    )
    hidden_low = hidden.astype(jnp.bfloat16)
    inner_pre = matmul(hidden_low, inner_mat) + inner_vec.astype(jnp.float32)
    active, gelu_pull = jax.vjp(exact_gelu, inner_pre)
    active_low = active.astype(jnp.bfloat16)
    outer_out = matmul(active_low, outer_mat) + outer_vec.astype(jnp.float32)
    normed_out, second_pull = jax.vjp(
        layer_norm,
        hidden + outer_out,
        second_scale.astype(jnp.float32),
        second_offset.astype(jnp.float32),
    )
    layer_out = (normed_out * live_mask[:, None]).astype(jnp.bfloat16)
    grad_top = grad_out.astype(jnp.float32) * live_mask[:, None]
    grad_two, second_gain_grad, second_shift_grad = second_pull(grad_top)
    grad_outer = grad_two.astype(jnp.bfloat16)
    outer_mat_grad = matmul_tn(active_low, grad_outer)
    outer_vec_grad = column_sums(grad_outer)
    (grad_inner,) = gelu_pull(matmul_nt(grad_outer, outer_mat))
    grad_inner_low = grad_inner.astype(jnp.bfloat16)
    inner_mat_grad = matmul_tn(hidden_low, grad_inner_low)
    inner_vec_grad = column_sums(grad_inner_low)
    grad_hidden = grad_two + matmul_nt(grad_inner_low, inner_mat)
    grad_one, first_gain_grad, first_shift_grad = first_pull(grad_hidden)
    grad_attn = grad_one.astype(jnp.bfloat16)
    output_mat_grad = matmul_tn(context_rows, grad_attn)
    output_vec_grad = column_sums(grad_attn)
    grad_context = (
        matmul_nt(grad_attn, output_mat).astype(jnp.bfloat16).reshape(frame_count, HEADS, head_size)
    )
    scores = block_scores(query_heads, key_heads, groups, groups, score_scale)
    attn_prob = jnp.exp(scores - log_totals)
    grad_prob = jnp.einsum(
        "qhd,khd->hqk", grad_context, value_heads, preferred_element_type=jnp.float32
    )
    inner_sum = jnp.sum(attn_prob * grad_prob, axis=-1, keepdims=True)
    grad_scores = (attn_prob * (grad_prob - inner_sum)).astype(jnp.bfloat16)
    query_grad_parts = (
        jnp.einsum("hqk,khd->qhd", grad_scores, key_heads, preferred_element_type=jnp.float32)
        * score_scale
    )
    key_grad_sum = (
        jnp.einsum("hqk,qhd->khd", grad_scores, query_heads, preferred_element_type=jnp.float32)
        * score_scale
    )
    value_grad_sum = jnp.einsum(
        "hqk,qhd->khd",
        attn_prob.astype(jnp.bfloat16),
        grad_context,
        preferred_element_type=jnp.float32,
    )
    grad_query = query_grad_parts.reshape(frame_count, model_width).astype(jnp.bfloat16)
    grad_key = key_grad_sum.reshape(frame_count, model_width).astype(jnp.bfloat16)
    grad_value = value_grad_sum.reshape(frame_count, model_width).astype(jnp.bfloat16)
    query_mat_grad = matmul_tn(frames, grad_query)
    query_vec_grad = column_sums(grad_query)
    key_mat_grad = matmul_tn(frames, grad_key)
    value_mat_grad = matmul_tn(frames, grad_value)
    value_vec_grad = column_sums(grad_value)
    frames_grad = (
        grad_one
        + matmul_nt(grad_query, query_mat)
        + matmul_nt(grad_key, key_mat)
        + matmul_nt(grad_value, value_mat)
    ).astype(jnp.bfloat16)
    shares = (
        lax.psum_scatter(query_mat_grad, ("dp", "fsdp"), scatter_dimension=0, tiled=True),
        lax.psum_scatter(query_vec_grad, ("dp", "fsdp"), scatter_dimension=0, tiled=True),
        lax.psum_scatter(key_mat_grad, ("dp", "fsdp"), scatter_dimension=0, tiled=True),
        lax.psum_scatter(value_mat_grad, ("dp", "fsdp"), scatter_dimension=0, tiled=True),
        lax.psum_scatter(value_vec_grad, ("dp", "fsdp"), scatter_dimension=0, tiled=True),
        lax.psum_scatter(output_mat_grad, ("dp", "fsdp"), scatter_dimension=0, tiled=True),
        lax.psum_scatter(output_vec_grad, ("dp", "fsdp"), scatter_dimension=0, tiled=True),
        lax.psum_scatter(first_gain_grad, ("dp", "fsdp"), scatter_dimension=0, tiled=True),
        lax.psum_scatter(first_shift_grad, ("dp", "fsdp"), scatter_dimension=0, tiled=True),
        lax.psum_scatter(inner_mat_grad, ("dp", "fsdp"), scatter_dimension=0, tiled=True),
        lax.psum_scatter(inner_vec_grad, ("dp", "fsdp"), scatter_dimension=0, tiled=True),
        lax.psum_scatter(outer_mat_grad, ("dp", "fsdp"), scatter_dimension=0, tiled=True),
        lax.psum_scatter(outer_vec_grad, ("dp", "fsdp"), scatter_dimension=0, tiled=True),
        lax.psum_scatter(second_gain_grad, ("dp", "fsdp"), scatter_dimension=0, tiled=True),
        lax.psum_scatter(second_shift_grad, ("dp", "fsdp"), scatter_dimension=0, tiled=True),
    )
    return (
        layer_out,
        frames_grad,
        shares[0],
        shares[1],
        shares[2],
        shares[3],
        shares[4],
        shares[5],
        shares[6],
        shares[7],
        shares[8],
        shares[9],
        shares[10],
        shares[11],
        shares[12],
        shares[13],
        shares[14],
    )


MESH = pl.DeviceIdType.MESH
NZ = 4
LANES = 128


class Net:
    def __init__(self):
        dp, fs = lax.axis_index("dp"), lax.axis_index("fsdp")
        self.y, self.c = lax.div(dp, 2), lax.rem(dp, 2)
        self.z, self.x = lax.div(fs, 2), lax.rem(fs, 2)

    def dev(self, y=None, c=None, z=None, x=None):
        y = self.y if y is None else y
        c = self.c if c is None else c
        z = self.z if z is None else z
        x = self.x if x is None else x
        return (y * 2 + c, z * 2 + x)

    def across(self, dim):
        if dim == "x":
            return self.dev(x=1 - self.x)
        if dim == "y":
            return self.dev(y=1 - self.y)
        return self.dev(c=1 - self.c)

    def barrier(self):
        bar = pltpu.get_barrier_semaphore()

        def tell(device):
            pl.semaphore_signal(bar, inc=1, device_id=device, device_id_type=MESH)

        for dim in "xyc":
            tell(self.across(dim))
        for k in range(1, NZ):
            tell(self.dev(z=lax.rem(self.z + k, NZ)))
        pl.semaphore_wait(bar, 3 + NZ - 1)


class Way:
    def __init__(self, net, region, order, sems, unit):
        self.net, self.region, self.order = net, region, order
        self.send, self.recv, self.unit = sems[0], sems[1], unit

    def copy(self, src, dst, slot, device):
        return pltpu.make_async_remote_copy(
            src_ref=src, dst_ref=dst, send_sem=self.send.at[self.unit, slot],
            recv_sem=self.recv.at[self.unit, slot], device_id=device, device_id_type=MESH)

    def part(self, have="", **at):
        n = self.net
        for d in "yzx":
            at.setdefault(d, None if d in have else getattr(n, d))
        return self.region(at["y"], n.c, at["z"], at["x"])

    def flip(self, *dims):
        return {d: 1 - getattr(self.net, d) for d in dims}

    def behind(self, k):
        return lax.rem(self.net.z + NZ - k, NZ)

    def ahead(self, k):
        return lax.rem(self.net.z + k, NZ)


class Gather(Way):
    def along(self, k, have):
        part = self.part(have)
        return self.copy(part, part, k - 1, self.net.dev(z=self.ahead(k)))

    def came(self, k, have):
        part = self.part(have, z=self.behind(k))
        return self.copy(part, part, k - 1, self.net.dev(z=self.behind(k)))

    def over(self, slot, d, have, **at):
        part = self.part(have, **at)
        return self.copy(part, part, slot, self.net.across(d))

    def sibling(self):
        part = self.region(None, self.net.c, None, None)
        return self.copy(part, part, 6, self.net.across("c"))

    def stages(self):
        first, d2, d3 = self.order
        zs = range(1, NZ)

        def start_a():
            for k in zs:
                self.along(k, "").start()

        def start_b():
            for k in zs:
                self.came(k, "").wait_recv()
            self.over(3, d2, "z").start()
            self.over(4, d3, "z").start()

        def start_c():
            self.over(3, d2, "z").wait_recv()
            self.over(5, d3, "z", **self.flip(d2)).start()

        def start_d():
            self.over(4, d3, "z").wait_recv()
            self.over(5, d3, "z", **self.flip(d2)).wait_recv()
            self.sibling().start()

        def start_e():
            self.sibling().wait_recv()

        def end():
            for k in zs:
                self.along(k, "").wait_send()
            self.over(3, d2, "z").wait_send()
            self.over(4, d3, "z").wait_send()
            self.over(5, d3, "z", **self.flip(d2)).wait_send()
            self.sibling().wait_send()

        if first == "z":
            return dict(a=start_a, b=start_b, c=start_c, d=start_d, e=start_e, f=end)

        have = first

        def begin_a():
            self.over(3, first, "").start()

        def begin_b():
            self.over(3, first, "").wait_recv()
            for k in zs:
                self.along(k, have).start()

        def begin_c():
            for k in zs:
                self.came(k, have).wait_recv()
            self.over(4, d3, have + "z").start()

        def begin_d():
            self.over(4, d3, have + "z").wait_recv()
            self.sibling().start()

        def finish():
            self.over(3, first, "").wait_send()
            for k in zs:
                self.along(k, have).wait_send()
            self.over(4, d3, have + "z").wait_send()
            self.sibling().wait_send()

        return dict(a=begin_a, b=begin_b, c=begin_c, d=begin_d, e=start_e, f=finish)


class Scatter(Way):
    def __init__(self, net, region, order, sems, unit, landing, line):
        super().__init__(net, region, order, sems, unit)
        self.landing, self.line = landing, line

    def sibling(self, core):
        part = self.region(None, core, None, None)
        return self.copy(part, part, 6, self.net.across("c"))

    def sibling_out(self):
        return self.sibling(1 - self.net.c)

    def sibling_in(self):
        return self.sibling(self.net.c)

    def over(self, k, d, slot, *dims):
        return self.copy(self.part("z", **self.flip(*dims)), self.landing(k), slot, self.net.across(d))

    def first(self):
        return self.over(0, self.order[2], 4, self.order[2], self.order[1])

    def second(self):
        return self.over(1, self.order[2], 5, self.order[2])

    def third(self):
        return self.over(2, self.order[1], 3, self.order[1])

    def along(self, k):
        ahead = self.ahead(k)
        return self.copy(self.part(z=ahead), self.line(k), k - 1, self.net.dev(z=ahead))

    @staticmethod
    def add(part, came):
        part[...] = (part[...].astype(jnp.float32) + came[...].astype(jnp.float32)).astype(part.dtype)

    def spread(self):
        self.first().start()
        self.second().start()

    def fold_first(self):
        self.first().wait_recv()
        self.add(self.part("z", **self.flip(self.order[1])), self.landing(0))
        self.third().start()

    def fold_second(self):
        self.second().wait_recv()
        self.add(self.part("z"), self.landing(1))

    def fold_third(self):
        self.third().wait_recv()
        self.add(self.part("z"), self.landing(2))
        for k in range(1, NZ):
            self.along(k).start()

    def total(self):
        out = self.part()[...].astype(jnp.float32)
        for k in range(1, NZ):
            self.along(k).wait_recv()
            out = out + self.line(k)[...].astype(jnp.float32)
        return out

    def stages(self):
        return dict(s=self.spread, t=self.fold_first, u=self.fold_second, v=self.fold_third)

    def finish(self):
        self.sibling_out().wait_send()
        for one in (self.first(), self.second(), self.third()):
            one.wait_send()
        for k in range(1, NZ):
            self.along(k).wait_send()


def region_square(ref):
    pair, half = ref.shape[2] // NZ, ref.shape[3] // 2

    def region(y, c, z, x):
        rows = pl.ds(0, pair * NZ) if z is None else pl.ds(pl.multiple_of(z * pair, 16), pair)
        cols = pl.ds(0, half * 2) if x is None else pl.ds(pl.multiple_of(x * half, LANES), half)
        return ref.at[pl.ds(0, 2) if y is None else y, c, rows, cols]

    return region


def region_lead(ref, start, size):
    run = ref.shape[4] // 2

    def region(y, c, z, x):
        rows = pl.ds(0, 2 * run) if x is None else pl.ds(pl.multiple_of(x * run, 16), run)
        high, low = (pl.ds(0, 2), pl.ds(0, 2)) if z is None else (lax.div(z, 2), lax.rem(z, 2))
        return ref.at[pl.ds(0, 2) if y is None else y, c, high, low, rows, pl.ds(start, size)]

    return region


def region_small(ref):
    def region(y, c, z, x):
        return ref.at[pl.ds(0, 2) if y is None else y, c, pl.ds(0, NZ) if z is None else z, pl.ds(0, 2) if x is None else x]

    return region


UNITS = range(13)
GATHER = ("zxy", "zyx", "zxy", "zyx", "zxy", "zyx", "zxy", "zyx", "zxy", "zyx", "zxy", "zyx", "zxy")
SCATTER = ("zxy", "zyx", "zxy", "zyx", "zxy", "zyx", "zxy", "zyx", "zxy", "zyx", "zxy", "zyx", "zxy")
OUTER = ((0, 256), (256, 256), (512, 128), (640, 128))


def mm(left, right):
    return jnp.dot(left, right, preferred_element_type=jnp.float32)


def mm_nt(left, right):
    return lax.dot_general(left, right, (((1,), (1,)), ((), ())), preferred_element_type=jnp.float32)


def mm_tn(left, right):
    return lax.dot_general(left, right, (((0,), (0,)), ((), ())), preferred_element_type=jnp.float32)


def eights(block):
    return jnp.sum(block.reshape(block.shape[0] // 8, 8, block.shape[1]), axis=0)


STEP = 64
F32, BF16 = jnp.float32, jnp.bfloat16


def layer_kernel(names, *refs):
    r = SimpleNamespace(**dict(zip(names, refs, strict=True)))
    net = Net()
    frame_count, width = r.frames.shape
    half = width // 2
    lead = r.wq.shape[0]
    pair = 2 * lead
    own_rows = pl.ds(pl.multiple_of(net.z * pair, 16), pair)
    own_cols = pl.ds(pl.multiple_of(net.x * half, LANES), half)
    w8, w2 = r.w8, r.w2
    g2 = r.g2

    x_in = pltpu.make_async_copy(r.frames, r.xbuf, r.isem.at[0])
    g_in = pltpu.make_async_copy(r.grad_out, r.gbuf, r.isem.at[1])
    x_in.start()
    g_in.start()
    net.barrier()

    gather, scatter = [], []
    for i in UNITS:
        cols = OUTER[i - 8] if 8 <= i < 12 else None
        if i < 8:
            region = region_square(w8.at[i])
            to = region_square(w2.at[i // 2, i % 2]) if i < 3 else region
            landing = lambda k, i=i: r.land8.at[i, k]
            line = lambda k, i=i: r.line8.at[i, k - 1]
        elif cols:
            region, to = region_lead(w2, *cols), region_lead(g2, *cols)
            landing = lambda k, cols=cols: r.land2.at[k, :, :, :, pl.ds(*cols)]
            line = lambda k, cols=cols: r.line2.at[k - 1, :, pl.ds(*cols)]
        else:
            region = region_small(r.small)
        gather.append(Gather(net, region, GATHER[i], (r.gs, r.gr), i).stages())
        if i < 12:
            scatter.append(Scatter(net, to, SCATTER[i], (r.ss, r.sr), i, landing, line))

    def shard(u):
        if u < 4:
            return (r.wq, r.wk, r.wv, r.wo)[u][...]
        return r.wi[:, (u - 4) * width:(u - 3) * width]

    def swap(u):
        return pltpu.make_async_remote_copy(
            src_ref=r.xs.at[u], dst_ref=r.xr.at[u], send_sem=r.xss.at[u], recv_sem=r.xrs.at[u],
            device_id=net.across("x"), device_id_type=MESH)

    def offer(u):
        v = shard(u).astype(F32)
        theirs = jnp.where(net.x == 0, v[:, half:], v[:, :half])
        r.xs[u] = jnp.concatenate([theirs, jnp.zeros((8, half), F32)], axis=0).astype(BF16)
        swap(u).start()

    def merge(u):
        swap(u).wait_recv()
        v = shard(u).astype(F32)
        mine = jnp.where(net.x == 0, v[:, :half], v[:, half:])
        came = r.xr[u].astype(F32)[:lead]
        first, second = jnp.where(net.x == 0, mine, came), jnp.where(net.x == 0, came, mine)
        w8[u, net.y, net.c, own_rows, own_cols] = jnp.concatenate([first, second], axis=0).astype(BF16)

    def place():
        for k in range(4):
            offer(k)
        pack = r.pack
        pack[...] = jnp.zeros_like(pack)
        for row, one in enumerate((r.bq, None, r.bv, r.bo, r.g1, r.s1, r.b2, r.gg2, r.s2, r.bi1)):
            if one is not None:
                size = one.shape[0]
                pack[row:row + 1, :size] = one[...].astype(F32).reshape(1, size)
        r.small[net.y, net.c, net.z, net.x] = pack[...].astype(BF16)
        w2[net.y, net.c, lax.div(net.z, 2), lax.rem(net.z, 2), pl.ds(pl.multiple_of(net.x * 4 * lead, 16), 4 * lead), :] = (
            r.wouter[...])
        for k in range(4, 8):
            offer(k)

    l0 = r.lengths[0, 0]
    l1 = l0 + r.lengths[0, 1]
    vec, bi, gsm, cs = r.vec, r.bi, r.gsm, r.cs
    fa, q3, e12 = r.fa, r.q3, r.e12
    act, gp, act_t = r.act, r.gp, r.act_t

    def loop(body, step=STEP, total=frame_count):
        def one(i, carry):
            body(pl.ds(pl.multiple_of(i * step, step), step))
            return carry

        lax.fori_loop(0, total // step, one, 0)

    def groups(shape, dim, start=0):
        place = lax.broadcasted_iota(jnp.int32, shape, dim) + start
        return (place >= l0).astype(jnp.int32) + (place >= l1).astype(jnp.int32)

    def masks():
        shape = (frame_count, LANES)
        lane = lax.broadcasted_iota(jnp.int32, shape, 1)
        group = groups(shape, 0)
        for e in range(2):
            spare = lane - (1 - e) * (LANES // 2)
            inside = (spare >= 0) & (spare < 3)
            r.mq[e] = jnp.where(inside & (spare != group), -1e30, 0.0).astype(BF16)
            r.mk[e] = jnp.where(inside & (spare == group), 1.0, 0.0).astype(BF16)

    def vectors():
        got = r.small[...].reshape(32 * 16, LANES)
        lane = lax.broadcasted_iota(jnp.int32, (LANES, width), 0)
        col = lax.broadcasted_iota(jnp.int32, (LANES, width), 1)
        tile = jnp.where((lane < lead) & (lane == lax.rem(col, lead)), 1.0, 0.0).astype(BF16)
        wide = mm(got, tile).reshape(32, 16, width)
        owner = lax.broadcasted_iota(jnp.int32, wide.shape, 0)
        place = lax.div(lax.broadcasted_iota(jnp.int32, wide.shape, 2), lead)
        vec[...] = jnp.sum(jnp.where(owner == place, wide, 0.0), axis=0)
        inner = got.astype(F32).reshape(32, 16, LANES)[:, 9, :].astype(BF16)
        for c in range(4):
            lane = lax.broadcasted_iota(jnp.int32, (LANES, width), 0)
            col = lax.broadcasted_iota(jnp.int32, (LANES, width), 1) + c * width
            tile = jnp.where((lane < 4 * lead) & (lane == lax.rem(col, 4 * lead)), 1.0, 0.0).astype(BF16)
            wide = mm(inner, tile)
            owner = lax.broadcasted_iota(jnp.int32, wide.shape, 0)
            place = lax.div(lax.broadcasted_iota(jnp.int32, wide.shape, 1) + c * width, 4 * lead)
            bi[c] = jnp.sum(jnp.where(owner == place, wide, 0.0), axis=0, keepdims=True)

    def square(u):
        return w8[u].reshape(width, width)

    def project(u):
        rows = mm(r.xbuf[...], square(u)) + vec[pl.ds(u, 1), :]
        q3[u] = (rows * 0.125 if u == 0 else rows).astype(BF16)

    def head_lanes(shape, e):
        return lax.div(lax.broadcasted_iota(jnp.int32, shape, 1), LANES // 2) == e

    ROWS = 256

    def attend(p):
        cols = pl.ds(pl.multiple_of(p * LANES, LANES), LANES)
        sides = []
        for e in range(2):
            mine = head_lanes((frame_count, LANES), e)
            keys = jnp.where(mine, q3[1, :, cols], r.mk[e])
            vals = jnp.where(mine, q3[2, :, cols], jnp.ones((), BF16))
            sides.append((keys, vals))
        for i in range(frame_count // ROWS):
            rows = pl.ds(i * ROWS, ROWS)
            outs = []
            for e in range(2):
                keys, vals = sides[e]
                mine = head_lanes((ROWS, LANES), e)
                query = jnp.where(mine, q3[0, rows, cols], r.mq[e, rows, :])
                scores = mm_nt(query, keys)
                top = jnp.max(scores, axis=1, keepdims=True)
                weights = jnp.exp(scores - top).astype(BF16)
                e12[2 * p + e, rows, :] = weights
                outs.append(mm(weights, vals))
            low = head_lanes((ROWS, LANES), 0)
            over = jnp.where(low, outs[0], outs[1])
            under = pltpu.roll(jnp.where(low, outs[1], outs[0]), LANES // 2, 1)
            inverse = 1.0 / under
            r.linv[rows, cols] = inverse
            r.ctx[rows, cols] = (over * inverse).astype(BF16)

    def heads(body, first, last):
        def one(i, carry):
            body(i)
            return carry

        lax.fori_loop(first, last, one, 0)

    def norm_one():
        fa[...] = mm(r.ctx[...], square(3))
        r.ctx_t[...] = jnp.transpose(r.ctx[...]).reshape(r.ctx_t.shape)

        def body(rows):
            v = r.xbuf[rows, :].astype(F32) + fa[rows, :] + vec[3:4, :]
            center = v - jnp.mean(v, axis=1, keepdims=True)
            scale = lax.rsqrt(jnp.mean(center * center, axis=1, keepdims=True) + 1e-05)
            normed = center * scale
            r.n1[rows, :] = normed
            r.r1[rows, :] = jnp.broadcast_to(scale, (STEP, LANES))
            r.low[rows, :] = (normed * vec[4:5, :] + vec[5:6, :]).astype(BF16)

        loop(body)
        r.hid_t[...] = jnp.transpose(r.low[...]).reshape(r.hid_t.shape)

    def feed(c):
        fa[...] = mm(r.low[...], square(4 + c))

        def body(rows):
            v = fa[rows, :] + bi[c]
            phi = 0.5 + 0.5 * lax.erf(v * 0.7071067811865476)
            bell = jnp.exp(v * v * -0.5) * 0.3989422804014327
            act[c, rows, :] = (v * phi).astype(BF16)
            gp[c, rows, :] = (phi + v * bell).astype(BF16)

        loop(body, 32)
        act_t[c // 2, c % 2] = jnp.transpose(act[c])

    def block(ref, c):
        return ref[c // 2, c % 2].reshape(width, width)

    def feed_out(k):
        start, size = OUTER[k]
        cols = slice(start, start + size)
        total = None
        for c in range(4):
            one = mm(act[c], w2[c // 2, c % 2, :, :, :, cols].reshape(width, size))
            total = one if total is None else total + one
        fa[:, cols] = total

    def fold(slot, row):
        gsm[row:row + 1, :] = jnp.sum(cs[slot], axis=0, keepdims=True)

    def norm_two():
        g_in.wait()
        cs[...] = jnp.zeros_like(cs)

        def body(rows):
            hidden = r.n1[rows, :] * vec[4:5, :] + vec[5:6, :]
            v = hidden + fa[rows, :] + vec[6:7, :]
            center = v - jnp.mean(v, axis=1, keepdims=True)
            scale = lax.rsqrt(jnp.mean(center * center, axis=1, keepdims=True) + 1e-05)
            normed = center * scale
            place = lax.broadcasted_iota(jnp.int32, normed.shape, 0) + rows.start
            live = jnp.where(place < l1, 1.0, 0.0)
            r.xbuf[rows, :] = ((normed * vec[7:8, :] + vec[8:9, :]) * live).astype(BF16)
            top = r.gbuf[rows, :].astype(F32) * live
            e = top * vec[7:8, :]
            d = e - jnp.mean(e, axis=1, keepdims=True) - normed * jnp.mean(e * normed, axis=1, keepdims=True)
            d = d * scale
            r.d2[rows, :] = d
            low = d.astype(BF16)
            r.low[rows, :] = low
            cs[0] += eights(top * normed)
            cs[1] += eights(top)
            cs[2] += eights(low.astype(F32))

        loop(body)
        fold(0, 7)
        fold(1, 8)
        fold(2, 6)

    layer_out = pltpu.make_async_copy(r.xbuf, r.layer_out, r.isem.at[0])
    frames_out = pltpu.make_async_copy(r.gbuf, r.frames_grad, r.isem.at[1])

    def back_feed(c):
        fa[...] = mm_nt(r.low[...], block(w2, c))
        cs[0] = jnp.zeros_like(cs[0])

        def body(rows):
            low = (fa[rows, :] * gp[c, rows, :].astype(F32)).astype(BF16)
            gp[c, rows, :] = low
            cs[0] += eights(low.astype(F32))

        loop(body)
        fold(0, 9 + c)

    def grad_square(u, left, right, own):
        core = net.c if own else 1 - net.c
        to = w2.at[u // 2, u % 2] if u < 3 else w8.at[u]
        rows = mm(left[:, core].reshape(2 * pair * NZ, frame_count), right()).reshape(2, pair * NZ, width)
        if own:
            scatter[u].sibling_in().wait_recv()
            rows = rows + to[:, core].astype(F32)
        to[:, core] = rows.astype(BF16)

    def grad_outer(i, own):
        core = net.c if own else 1 - net.c
        start, size = OUTER[i - 8]
        cols = pl.ds(start, size)
        left = act_t[:, core].reshape(2 * width, frame_count)
        rows = mm(left, r.low[:, cols]).reshape((2,) + g2.shape[2:5] + (size,))
        if own:
            scatter[i].sibling_in().wait_recv()
            rows = rows + g2[:, core, :, :, :, cols].astype(F32)
        g2[:, core, :, :, :, cols] = rows.astype(BF16)

    def back_hidden():
        def one(c, carry):
            got = mm_nt(gp[c], w8[4 + c].reshape(width, width))

            @pl.when(c == 0)
            def _():
                fa[...] = got

            @pl.when(c > 0)
            def _():
                fa[...] += got

            return carry

        lax.fori_loop(0, 4, one, 0)

    def back_norm_one():
        cs[...] = jnp.zeros_like(cs)

        def body(rows):
            d = r.d2[rows, :] + fa[rows, :]
            normed = r.n1[rows, :]
            e = d * vec[4:5, :]
            cs[0] += eights(d * normed)
            cs[1] += eights(d)
            d = e - jnp.mean(e, axis=1, keepdims=True) - normed * jnp.mean(e * normed, axis=1, keepdims=True)
            d = d * r.r1[rows, 0:1]
            r.d2[rows, :] = d
            low = d.astype(BF16)
            r.low[rows, :] = low
            cs[2] += eights(low.astype(F32))

        loop(body)
        fold(0, 4)
        fold(1, 5)
        fold(2, 3)

    def back_context():
        act[3] = mm_nt(r.low[...], square(3)).astype(BF16)

    def back_attend(p):
        cols = pl.ds(pl.multiple_of(p * LANES, LANES), LANES)
        shape = (frame_count, LANES)
        low = head_lanes(shape, 0)
        scaled = (act[3, :, cols].astype(F32) * r.linv[:, cols]).astype(BF16)
        product = scaled.astype(F32) * r.ctx[:, cols].astype(F32)
        lane = lax.broadcasted_iota(jnp.int32, shape, 1)
        k2, v2, q2 = q3[1, :, cols], q3[2, :, cols], q3[0, :, cols]
        dq, dk, dv = [], [], []
        for e in range(2):
            mine = head_lanes(shape, e)
            spare = lane - (1 - e) * (LANES // 2)
            dot = jnp.sum(jnp.where(mine, product, 0.0), axis=1, keepdims=True)
            high = dot.astype(BF16).astype(F32)
            extra = jnp.where(spare == 0, high, jnp.where(spare == 1, dot - high, 0.0)).astype(BF16)
            left = jnp.where(mine, scaled, extra)
            minus = jnp.where((spare == 0) | (spare == 1), -1.0, 0.0).astype(BF16)
            right = jnp.where(mine, v2, minus)
            for i in range(frame_count // ROWS):
                part = slice(i * ROWS, (i + 1) * ROWS)
                r.ds[e, part, :] = (e12[2 * p + e, part, :].astype(F32) * mm_nt(left[part], right)).astype(BF16)
            dq.append(mm(r.ds[e], k2))
            dk.append(mm_tn(r.ds[e], q2))
            dv.append(mm_tn(e12[2 * p + e], scaled))
        act[0, :, cols] = (jnp.where(low, dq[0], dq[1]) * 0.125).astype(BF16)
        act[1, :, cols] = jnp.where(low, dk[0], dk[1]).astype(BF16)
        act[2, :, cols] = jnp.where(low, dv[0], dv[1]).astype(BF16)

    def bias_sums():
        cs[...] = jnp.zeros_like(cs)

        def body(rows):
            cs[0] += eights(act[0, rows, :].astype(F32))
            cs[1] += eights(act[2, rows, :].astype(F32))

        loop(body)
        fold(0, 0)
        fold(1, 2)
        gsm[1:2, :] = jnp.zeros((1, width), F32)
        gsm[13:16, :] = jnp.zeros((3, width), F32)

    def back_frames():
        fa[...] = r.d2[...] + mm_nt(act[0], square(0))
        fa[...] += mm_nt(act[1], square(1))
        layer_out.wait()
        r.gbuf[...] = (fa[...] + mm_nt(act[2], square(2))).astype(BF16)
        frames_out.start()

    def small_copy(k, device):
        return pltpu.make_async_remote_copy(
            src_ref=r.sm.at[k], dst_ref=r.sl.at[k], send_sem=r.sms.at[k], recv_sem=r.smr.at[k],
            device_id=device, device_id_type=MESH)

    def small_step(k):
        if k == 0:
            r.sm[0] = gsm[...]
        else:
            r.sm[k] = r.sm[k - 1] + r.sl[k - 1]
        if k < 3:
            small_copy(k, net.across("cyx"[k])).start()

    def small_wait(k):
        small_copy(k, net.across("cyx"[k])).wait_recv()

    def small_line(k):
        return pltpu.make_async_remote_copy(
            src_ref=r.sm.at[3], dst_ref=r.sl.at[2 + k], send_sem=r.sms.at[2 + k], recv_sem=r.smr.at[2 + k],
            device_id=net.dev(z=lax.rem(net.z + k, NZ)), device_id_type=MESH)

    def small_total():
        for k in range(1, NZ):
            small_line(k).wait_recv()
        whole = r.sm[3] + r.sl[3] + r.sl[4] + r.sl[5]
        index = (net.y * 2 + net.c) * 2 * NZ + net.z * 2 + net.x
        turned = pltpu.roll(whole, lax.rem(width - index * lead, width), 1)
        row = lax.broadcasted_iota(jnp.int32, (16, width), 0)
        block = lax.div(index, 8)
        inner = jnp.sum(jnp.where(row == 9 + block, whole, 0.0), axis=0, keepdims=True)
        inner = pltpu.roll(jnp.broadcast_to(inner, (8, width)), lax.rem(width - lax.rem(index, 8) * 4 * lead, width), 1)
        r.gsmall[0:8, :] = turned[0:8, :LANES]
        r.gsmall[8:16, :] = jnp.where(row[:8, :LANES] == 0, turned[8:9, :LANES], inner[:, :LANES])

    def swap_back(u):
        return pltpu.make_async_remote_copy(
            src_ref=r.ys.at[u], dst_ref=r.yr.at[u], send_sem=r.yss.at[u], recv_sem=r.yrs.at[u],
            device_id=net.across("x"), device_id_type=MESH)

    def out_of(u):
        if u < 4:
            return (r.gwq, r.gwk, r.gwv, r.gwo)[u], 0
        return r.gwi, (u - 4) * width

    def total_square(u):
        r.f8[...] = scatter[u].total()
        out, start = out_of(u)
        mine, theirs = pl.multiple_of(net.x * lead, 8), pl.multiple_of((1 - net.x) * lead, 8)
        r.ys[u] = r.f8[pl.ds(theirs, lead), :]
        swap_back(u).start()
        out[:, pl.ds(pl.multiple_of(start + net.x * half, LANES), half)] = r.f8[pl.ds(mine, lead), :]

    def last_square(u):
        swap_back(u).wait_recv()
        out, start = out_of(u)
        out[:, pl.ds(pl.multiple_of(start + (1 - net.x) * half, LANES), half)] = r.yr[u]

    def total_outer(i):
        r.gwouter[:, pl.ds(*OUTER[i - 8])] = scatter[i].total()

    def unit(i, left=None, right=None):
        steps = SimpleNamespace(**gather[i])
        if i == len(UNITS) - 1:
            return steps
        way, square = scatter[i], i < 8

        def half_of(own):
            if square:
                grad_square(i, left, right, own)
            else:
                grad_outer(i, own)

        def away():
            half_of(False)
            way.sibling_out().start()

        def home():
            half_of(True)
            way.spread()

        steps.away, steps.home = away, home
        steps.t, steps.u, steps.v = way.fold_first, way.fold_second, way.fold_third
        if square:
            steps.p = functools.partial(merge, i)
            steps.x, steps.y = functools.partial(total_square, i), functools.partial(last_square, i)
        else:
            steps.x = functools.partial(total_outer, i)
        return steps

    def give(k):
        pl.semaphore_signal(r.free.at[k], inc=1, device_id=net.across("c"), device_id_type=MESH)

    def take(k):
        pl.semaphore_wait(r.free.at[k], 1)

    def turn():
        x_in.wait()
        r.xt[...] = jnp.transpose(r.xbuf[...]).reshape(r.xt.shape)

    def gather_end():
        for one in gather:
            one["f"]()

    def small(k):
        if k > 0:
            small_wait(k - 1)
        small_step(k)
        if k == 3:
            for one in range(1, NZ):
                small_line(one).start()

    def end():
        for one in scatter:
            one.finish()
        for u in range(8):
            swap(u).wait_send()
            swap_back(u).wait_send()
        for k in range(3):
            small_copy(k, net.across("cyx"[k])).wait_send()
        for k in range(1, NZ):
            small_line(k).wait_send()
        frames_out.wait()

    def go(*steps):
        for step in steps:
            step()

    q, k, v = (unit(u, r.xt, lambda u=u: act[u]) for u in range(3))
    o = unit(3, r.ctx_t, lambda: r.low[...])
    i0, i1, i2, i3 = (unit(4 + u, r.hid_t, lambda u=u: gp[u]) for u in range(4))
    w0, w1, w2_, w3 = (unit(8 + u) for u in range(4))
    s = unit(12)
    place()
    go(s.a, q.p, k.p, q.a, k.a, v.p, o.p)
    masks()
    turn()
    go(s.b, s.c, s.d, q.b, k.b, v.a, o.a, s.e)
    vectors()
    go(i0.p, i1.p, q.c, k.c, v.b, o.b, i0.a, i1.a, q.d, k.d, i2.p, i3.p)
    go(v.c, o.c, i0.b, i1.b, i2.a, i3.a, q.e, k.e, v.d, o.d)
    project(0)
    project(1)
    go(i0.c, i1.c, i2.b, i3.b, w0.a, w1.a, v.e, o.e, i0.d, i1.d)
    project(2)
    heads(attend, 0, 2)
    go(i2.c, i3.c, w0.b, w1.b, w2_.a, w3.a, i0.e, i1.e, i2.d, i3.d)
    heads(attend, 2, 4)
    heads(attend, 4, 6)
    norm_one()
    go(w0.c, w1.c, w2_.b, w3.b, i2.e, i3.e, w0.d, w1.d)
    feed(0)
    feed(1)
    go(w2_.c, w3.c, w0.e, w1.e)
    feed(2)
    feed(3)
    feed_out(0)
    feed_out(1)
    go(w2_.d, w3.d, w2_.e)
    feed_out(2)
    go(w3.e)
    feed_out(3)
    norm_two()
    layer_out.start()
    go(w0.away, w1.away, w0.home, w1.home, w2_.away, w2_.home, w3.away, w3.home)
    gather_end()
    back_feed(0)
    back_feed(1)
    back_feed(2)
    back_feed(3)
    give(0)
    go(w0.t, w1.t, w0.u, w1.u)
    back_hidden()
    give(1)
    go(w2_.t, w3.t, w2_.u, w3.u)
    take(1)
    go(i0.away, i1.away, i0.home, i1.home, w0.v, w1.v, i2.away, i3.away, i2.home, i3.home)
    back_norm_one()
    back_context()
    give(2)
    go(w2_.v, w3.v)
    take(2)
    go(o.away, o.home, i0.t, i1.t, i0.u, i1.u, w0.x, w1.x, i2.t, i3.t, i2.u, i3.u)
    heads(back_attend, 0, 2)
    go(w2_.x, w3.x, o.t, i0.v, i1.v, o.u)
    heads(back_attend, 2, 4)
    go(i2.v, i3.v, i0.x, i1.x)
    heads(back_attend, 4, 6)
    take(0)
    go(q.away, k.away, q.home, k.home, v.away, v.home)
    bias_sums()
    small(0)
    go(i2.x, i3.x, o.v, q.t, k.t, v.t)
    back_frames()
    small(1)
    go(q.u, k.u, v.u)
    small(2)
    go(o.x, q.v, k.v, v.v)
    small(3)
    go(q.x, k.x, v.x)
    small_total()
    go(i0.y, i1.y, i2.y, i3.y, o.y, q.y, k.y, v.y)
    end()


def kernel_device(
    frames, lengths, query_weight, query_bias, key_weight, value_weight, value_bias, output_weight, output_bias,
    first_gain, first_shift, inner_weight, inner_bias, outer_weight, outer_bias, second_gain, second_shift, grad_out,
):
    count, width = frames.shape
    lead = query_weight.shape[0]
    pair, half = 2 * lead, width // 2
    vmem, hbm = pl.BlockSpec(memory_space=pltpu.VMEM), pl.BlockSpec(memory_space=pl.ANY)
    smem = pl.BlockSpec(memory_space=pltpu.SMEM)
    args = dict(
        frames=(hbm, frames), grad_out=(hbm, grad_out), lengths=(smem, lengths), wq=(vmem, query_weight),
        wk=(vmem, key_weight), wv=(vmem, value_weight), wo=(vmem, output_weight), wi=(vmem, inner_weight),
        wouter=(vmem, outer_weight), bq=(vmem, query_bias), bv=(vmem, value_bias), bo=(vmem, output_bias),
        g1=(vmem, first_gain), s1=(vmem, first_shift), b2=(vmem, outer_bias), gg2=(vmem, second_gain),
        s2=(vmem, second_shift), bi1=(vmem, inner_bias))
    shape = jax.ShapeDtypeStruct
    outs = dict(
        layer_out=(hbm, shape((count, width), BF16)), frames_grad=(hbm, shape((count, width), BF16)),
        gwq=(vmem, shape((lead, width), F32)), gwk=(vmem, shape((lead, width), F32)),
        gwv=(vmem, shape((lead, width), F32)), gwo=(vmem, shape((lead, width), F32)),
        gwi=(vmem, shape(inner_weight.shape, F32)), gwouter=(vmem, shape(outer_weight.shape, F32)),
        gsmall=(vmem, shape((16, LANES), F32)))
    dma = pltpu.SemaphoreType.DMA
    big = (count, width)
    square = (2, 2, pair * NZ, width)
    turned = (2, 2, pair * NZ, count)
    lead_shape = (2, 2, 2, 2, 8 * lead, width)
    scratch = dict(
        w8=((8,) + square, BF16), w2=(lead_shape, BF16), g2=(lead_shape, BF16), small=((2, 2, NZ, 2, 16, LANES), BF16),
        land8=((8, 3, pair * NZ, half), BF16), line8=((8, NZ - 1, pair, half), BF16),
        land2=((3, 2, 2, 4 * lead, width), BF16), line2=((NZ - 1, 4 * lead, width), BF16),
        pack=((16, LANES), F32), xs=((8, lead + 8, half), BF16), xr=((8, lead + 8, half), BF16),
        ys=((8, lead, half), F32), yr=((8, lead, half), F32), xbuf=(big, BF16), gbuf=(big, BF16), q3=((3,) + big, BF16),
        e12=((HEADS, count, count), BF16), linv=(big, F32), ctx=(big, BF16), xt=(turned, BF16), ctx_t=(turned, BF16),
        hid_t=(turned, BF16), low=(big, BF16), n1=(big, F32), r1=((count, LANES), F32), act=((4,) + big, BF16),
        gp=((4,) + big, BF16), act_t=((2, 2, width, count), BF16), fa=(big, F32), d2=(big, F32),
        ds=((2, count, count), BF16), mq=((2, count, LANES), BF16), mk=((2, count, LANES), BF16), vec=((16, width), F32),
        bi=((4, 1, width), F32), gsm=((16, width), F32), cs=((3, 8, width), F32), sm=((4, 16, width), F32),
        sl=((6, 16, width), F32), f8=((pair, half), F32))
    scratch = {k: pltpu.VMEM(*v) for k, v in scratch.items()}
    scratch.update(
        gs=dma((13, 7)), gr=dma((13, 7)), ss=dma((12, 7)), sr=dma((12, 7)), xss=dma((8,)), xrs=dma((8,)), yss=dma((8,)),
        yrs=dma((8,)), sms=dma((6,)), smr=dma((6,)), isem=dma((2,)), free=pltpu.SemaphoreType.REGULAR((3,)))
    got = pl.pallas_call(
        functools.partial(layer_kernel, (*args, *outs, *scratch)),
        out_shape=[o[1] for o in outs.values()],
        in_specs=[a[0] for a in args.values()],
        out_specs=[o[0] for o in outs.values()],
        scratch_shapes=list(scratch.values()),
        compiler_params=pltpu.CompilerParams(collective_id=0, has_side_effects=True, vmem_limit_bytes=VMEM_BYTES),
    )(*(a[1] for a in args.values()))

    bias, wide = shape((lead,), F32), shape((4 * lead,), F32)
    vectors = {3: bias, 6: bias, 8: bias, 9: bias, 10: bias, 12: wide, 14: bias, 15: bias, 16: bias}
    row_of = {3: 0, 6: 2, 8: 3, 9: 4, 10: 5, 12: 9, 14: 6, 15: 7, 16: 8}
    places = [i for i in range(17) if i not in vectors]

    def publish(*refs):
        came, small, out = refs[:8], refs[8], refs[9:]
        for a, i in zip(came, places, strict=True):
            out[i][...] = a[...]
        for i, row in row_of.items():
            size = vectors[i].shape[0]
            out[i][...] = small[row:row + 1, :size].reshape(size)

    whole = dict(zip(places, (o[1] for o in list(outs.values())[:8]), strict=True))
    return tuple(pl.pallas_call(
        publish,
        out_shape=[vectors[i] if i in vectors else whole[i] for i in range(17)],
        in_specs=[vmem] * 9,
        out_specs=[vmem] * 17,
    )(*got))


VMEM_BYTES = 63 << 20


def solution(mesh):
    split = P(("dp", "fsdp"))
    rows = P(("dp", "fsdp"), None)
    in_specs = (
        rows, rows, rows, split, rows, rows, split, rows, split, split, split, rows, split, rows, split, split, split, rows,
    )
    out_specs = (
        rows, rows, rows, split, rows, rows, split, rows, split, split, split, rows, split, rows, split, split, split,
    )
    fits = mesh.shape["dp"] == 4 and mesh.shape["fsdp"] == 2 * NZ

    def per_device(frames, lengths, query_weight, *rest):
        lead, width = query_weight.shape
        good = fits and lead % 8 == 0 and 4 * lead <= LANES and width == 768
        run = kernel_device if good else general_device
        return run(frames, lengths, query_weight, *rest)

    return jax.shard_map(per_device, mesh=mesh, in_specs=in_specs, out_specs=out_specs, check_vma=False)
```

```python
import functools
from types import SimpleNamespace

import jax
import jax.numpy as jnp
from jax import lax
from jax.experimental import pallas as pl
from jax.experimental.pallas import tpu as pltpu
from jax.sharding import PartitionSpec as P

HEADS = 12


def layer_norm(values, gain_vec, shift_vec):
    center = values - jnp.mean(values, axis=-1, keepdims=True)
    spread = jnp.mean(center * center, axis=-1, keepdims=True)
    return center * lax.rsqrt(spread + 1e-05) * gain_vec + shift_vec


def exact_gelu(values):
    return jax.nn.gelu(values, approximate=False)


def matmul(left_side, right_side):
    return jnp.dot(left_side, right_side, preferred_element_type=jnp.float32)


def matmul_tn(left_side, right_side):
    return lax.dot_general(
        left_side, right_side, (((0,), (0,)), ((), ())), preferred_element_type=jnp.float32
    )


def matmul_nt(left_side, right_side):
    return lax.dot_general(
        left_side, right_side, (((1,), (1,)), ((), ())), preferred_element_type=jnp.float32
    )


def column_sums(values):
    return jnp.sum(values.astype(jnp.float32), axis=0)


def block_scores(query_block, key_heads, group_block, groups, score_scale):
    raw_scores = (
        jnp.einsum("qhd,khd->hqk", query_block, key_heads, preferred_element_type=jnp.float32)
        * score_scale
    )
    allowed = group_block[:, None] == groups[None, :]
    return jnp.where(allowed[None], raw_scores, -1e30)


def general_device(
    frames,
    lengths,
    query_weight,
    query_bias,
    key_weight,
    value_weight,
    value_bias,
    output_weight,
    output_bias,
    first_gain,
    first_shift,
    inner_weight,
    inner_bias,
    outer_weight,
    outer_bias,
    second_gain,
    second_shift,
    grad_out,
):
    frame_count = frames.shape[0]
    model_width = frames.shape[1]
    head_size = model_width // HEADS
    score_scale = head_size ** (-0.5)
    places = jnp.arange(frame_count, dtype=jnp.int32)
    bounds = jnp.stack([lengths[0, 0], lengths[0, 0] + lengths[0, 1]])
    groups = jnp.sum((places[:, None] >= bounds[None, :]).astype(jnp.int32), axis=1)
    live_mask = (places < bounds[-1]).astype(jnp.float32)
    gathered = (
        lax.all_gather(query_weight, ("dp", "fsdp"), axis=0, tiled=True),
        lax.all_gather(query_bias, ("dp", "fsdp"), axis=0, tiled=True),
        lax.all_gather(key_weight, ("dp", "fsdp"), axis=0, tiled=True),
        lax.all_gather(value_weight, ("dp", "fsdp"), axis=0, tiled=True),
        lax.all_gather(value_bias, ("dp", "fsdp"), axis=0, tiled=True),
        lax.all_gather(output_weight, ("dp", "fsdp"), axis=0, tiled=True),
        lax.all_gather(output_bias, ("dp", "fsdp"), axis=0, tiled=True),
        lax.all_gather(first_gain, ("dp", "fsdp"), axis=0, tiled=True),
        lax.all_gather(first_shift, ("dp", "fsdp"), axis=0, tiled=True),
        lax.all_gather(inner_weight, ("dp", "fsdp"), axis=0, tiled=True),
        lax.all_gather(inner_bias, ("dp", "fsdp"), axis=0, tiled=True),
        lax.all_gather(outer_weight, ("dp", "fsdp"), axis=0, tiled=True),
        lax.all_gather(outer_bias, ("dp", "fsdp"), axis=0, tiled=True),
        lax.all_gather(second_gain, ("dp", "fsdp"), axis=0, tiled=True),
        lax.all_gather(second_shift, ("dp", "fsdp"), axis=0, tiled=True),
    )
    (
        query_mat,
        query_vec,
        key_mat,
        value_mat,
        value_vec,
        output_mat,
        output_vec,
        first_scale,
        first_offset,
        inner_mat,
        inner_vec,
        outer_mat,
        outer_vec,
        second_scale,
        second_offset,
    ) = gathered
    query_rows = (matmul(frames, query_mat) + query_vec.astype(jnp.float32)).astype(jnp.bfloat16)
    key_rows = matmul(frames, key_mat).astype(jnp.bfloat16)
    value_rows = (matmul(frames, value_mat) + value_vec.astype(jnp.float32)).astype(jnp.bfloat16)
    query_heads = query_rows.reshape(frame_count, HEADS, head_size)
    key_heads = key_rows.reshape(frame_count, HEADS, head_size)
    value_heads = value_rows.reshape(frame_count, HEADS, head_size)
    scores = block_scores(query_heads, key_heads, groups, groups, score_scale)
    row_max = jnp.max(scores, axis=-1, keepdims=True)
    raw_weights = jnp.exp(scores - row_max)
    row_total = jnp.sum(raw_weights, axis=-1, keepdims=True)
    attn_prob = raw_weights / row_total
    log_totals = row_max + jnp.log(row_total)
    context_parts = jnp.einsum(
        "hqk,khd->qhd",
        attn_prob.astype(jnp.bfloat16),
        value_heads,
        preferred_element_type=jnp.float32,
    )
    context_rows = context_parts.reshape(frame_count, model_width).astype(jnp.bfloat16)
    frames_float = frames.astype(jnp.float32)
    resid_one = frames_float + matmul(context_rows, output_mat) + output_vec.astype(jnp.float32)
    hidden, first_pull = jax.vjp(
        layer_norm, resid_one, first_scale.astype(jnp.float32), first_offset.astype(jnp.float32)
    )
    hidden_low = hidden.astype(jnp.bfloat16)
    inner_pre = matmul(hidden_low, inner_mat) + inner_vec.astype(jnp.float32)
    active, gelu_pull = jax.vjp(exact_gelu, inner_pre)
    active_low = active.astype(jnp.bfloat16)
    outer_out = matmul(active_low, outer_mat) + outer_vec.astype(jnp.float32)
    normed_out, second_pull = jax.vjp(
        layer_norm,
        hidden + outer_out,
        second_scale.astype(jnp.float32),
        second_offset.astype(jnp.float32),
    )
    layer_out = (normed_out * live_mask[:, None]).astype(jnp.bfloat16)
    grad_top = grad_out.astype(jnp.float32) * live_mask[:, None]
    grad_two, second_gain_grad, second_shift_grad = second_pull(grad_top)
    grad_outer = grad_two.astype(jnp.bfloat16)
    outer_mat_grad = matmul_tn(active_low, grad_outer)
    outer_vec_grad = column_sums(grad_outer)
    (grad_inner,) = gelu_pull(matmul_nt(grad_outer, outer_mat))
    grad_inner_low = grad_inner.astype(jnp.bfloat16)
    inner_mat_grad = matmul_tn(hidden_low, grad_inner_low)
    inner_vec_grad = column_sums(grad_inner_low)
    grad_hidden = grad_two + matmul_nt(grad_inner_low, inner_mat)
    grad_one, first_gain_grad, first_shift_grad = first_pull(grad_hidden)
    grad_attn = grad_one.astype(jnp.bfloat16)
    output_mat_grad = matmul_tn(context_rows, grad_attn)
    output_vec_grad = column_sums(grad_attn)
    grad_context = (
        matmul_nt(grad_attn, output_mat).astype(jnp.bfloat16).reshape(frame_count, HEADS, head_size)
    )
    scores = block_scores(query_heads, key_heads, groups, groups, score_scale)
    attn_prob = jnp.exp(scores - log_totals)
    grad_prob = jnp.einsum(
        "qhd,khd->hqk", grad_context, value_heads, preferred_element_type=jnp.float32
    )
    inner_sum = jnp.sum(attn_prob * grad_prob, axis=-1, keepdims=True)
    grad_scores = (attn_prob * (grad_prob - inner_sum)).astype(jnp.bfloat16)
    query_grad_parts = (
        jnp.einsum("hqk,khd->qhd", grad_scores, key_heads, preferred_element_type=jnp.float32)
        * score_scale
    )
    key_grad_sum = (
        jnp.einsum("hqk,qhd->khd", grad_scores, query_heads, preferred_element_type=jnp.float32)
        * score_scale
    )
    value_grad_sum = jnp.einsum(
        "hqk,qhd->khd",
        attn_prob.astype(jnp.bfloat16),
        grad_context,
        preferred_element_type=jnp.float32,
    )
    grad_query = query_grad_parts.reshape(frame_count, model_width).astype(jnp.bfloat16)
    grad_key = key_grad_sum.reshape(frame_count, model_width).astype(jnp.bfloat16)
    grad_value = value_grad_sum.reshape(frame_count, model_width).astype(jnp.bfloat16)
    query_mat_grad = matmul_tn(frames, grad_query)
    query_vec_grad = column_sums(grad_query)
    key_mat_grad = matmul_tn(frames, grad_key)
    value_mat_grad = matmul_tn(frames, grad_value)
    value_vec_grad = column_sums(grad_value)
    frames_grad = (
        grad_one
        + matmul_nt(grad_query, query_mat)
        + matmul_nt(grad_key, key_mat)
        + matmul_nt(grad_value, value_mat)
    ).astype(jnp.bfloat16)
    shares = (
        lax.psum_scatter(query_mat_grad, ("dp", "fsdp"), scatter_dimension=0, tiled=True),
        lax.psum_scatter(query_vec_grad, ("dp", "fsdp"), scatter_dimension=0, tiled=True),
        lax.psum_scatter(key_mat_grad, ("dp", "fsdp"), scatter_dimension=0, tiled=True),
        lax.psum_scatter(value_mat_grad, ("dp", "fsdp"), scatter_dimension=0, tiled=True),
        lax.psum_scatter(value_vec_grad, ("dp", "fsdp"), scatter_dimension=0, tiled=True),
        lax.psum_scatter(output_mat_grad, ("dp", "fsdp"), scatter_dimension=0, tiled=True),
        lax.psum_scatter(output_vec_grad, ("dp", "fsdp"), scatter_dimension=0, tiled=True),
        lax.psum_scatter(first_gain_grad, ("dp", "fsdp"), scatter_dimension=0, tiled=True),
        lax.psum_scatter(first_shift_grad, ("dp", "fsdp"), scatter_dimension=0, tiled=True),
        lax.psum_scatter(inner_mat_grad, ("dp", "fsdp"), scatter_dimension=0, tiled=True),
        lax.psum_scatter(inner_vec_grad, ("dp", "fsdp"), scatter_dimension=0, tiled=True),
        lax.psum_scatter(outer_mat_grad, ("dp", "fsdp"), scatter_dimension=0, tiled=True),
        lax.psum_scatter(outer_vec_grad, ("dp", "fsdp"), scatter_dimension=0, tiled=True),
        lax.psum_scatter(second_gain_grad, ("dp", "fsdp"), scatter_dimension=0, tiled=True),
        lax.psum_scatter(second_shift_grad, ("dp", "fsdp"), scatter_dimension=0, tiled=True),
    )
    return (
        layer_out,
        frames_grad,
        shares[0],
        shares[1],
        shares[2],
        shares[3],
        shares[4],
        shares[5],
        shares[6],
        shares[7],
        shares[8],
        shares[9],
        shares[10],
        shares[11],
        shares[12],
        shares[13],
        shares[14],
    )


MESH = pl.DeviceIdType.MESH
NZ = 4
LANES = 128


class Net:
    def __init__(self):
        dp, fs = lax.axis_index("dp"), lax.axis_index("fsdp")
        self.y, self.c = lax.div(dp, 2), lax.rem(dp, 2)
        self.z, self.x = lax.div(fs, 2), lax.rem(fs, 2)

    def dev(self, y=None, c=None, z=None, x=None):
        y = self.y if y is None else y
        c = self.c if c is None else c
        z = self.z if z is None else z
        x = self.x if x is None else x
        return (y * 2 + c, z * 2 + x)

    def across(self, dim):
        if dim == "x":
            return self.dev(x=1 - self.x)
        if dim == "y":
            return self.dev(y=1 - self.y)
        return self.dev(c=1 - self.c)

    def greet(self):
        bar = pltpu.get_barrier_semaphore()

        def tell(device):
            pl.semaphore_signal(bar, inc=1, device_id=device, device_id_type=MESH)

        for dim in "xyc":
            tell(self.across(dim))
        for k in range(1, NZ):
            tell(self.dev(z=lax.rem(self.z + k, NZ)))

    def meet(self):
        pl.semaphore_wait(pltpu.get_barrier_semaphore(), 3 + NZ - 1)


class Way:
    def __init__(self, net, region, order, sems):
        self.net, self.region, self.order = net, region, order
        self.out, self.mate, self.recv = sems

    def copy(self, src, dst, slot, device, send=None):
        return pltpu.make_async_remote_copy(
            src_ref=src, dst_ref=dst, send_sem=self.out if send is None else send, recv_sem=self.recv.at[slot],
            device_id=device, device_id_type=MESH)

    def wait_for(self, ref, slot):
        self.copy(ref, ref, slot, self.net.across("c")).wait_recv()

    def part(self, have="", **at):
        n = self.net
        for d in "yzx":
            at.setdefault(d, None if d in have else getattr(n, d))
        return self.region(at["y"], n.c, at["z"], at["x"])

    def flip(self, *dims):
        return {d: 1 - getattr(self.net, d) for d in dims}

    def ahead(self, k):
        return lax.rem(self.net.z + k, NZ)


class Gather(Way):
    def __init__(self, net, region, order, sems, bulk):
        super().__init__(net, region, order, sems)
        self.bulk = bulk

    def lines_start(self, have):
        part = self.part(have)
        for k in range(1, NZ):
            self.copy(part, part, 0, self.net.dev(z=self.ahead(k))).start()

    def lines_wait(self, have):
        self.wait_for(self.bulk(len(have) * (NZ - 1) + NZ - 1), 0)

    def over(self, slot, d, have, **at):
        part = self.part(have, **at)
        return self.copy(part, part, slot, self.net.across(d))

    def sibling(self):
        part = self.region(None, self.net.c, None, None)
        return self.copy(part, part, 3, self.net.across("c"), self.mate)

    def stages(self):
        first, d2, d3 = self.order

        def start_a():
            self.lines_start("")

        def start_b():
            self.lines_wait("")
            self.over(1, d2, "z").start()
            self.over(2, d3, "z").start()

        def start_c():
            self.over(1, d2, "z").wait_recv()
            self.over(2, d3, "z", **self.flip(d2)).start()

        def start_d():
            self.wait_for(self.part(d2 + "z", **self.flip(d3)), 2)
            self.sibling().start()

        def start_e():
            self.sibling().wait_recv()

        if first == "z":
            return dict(a=start_a, b=start_b, c=start_c, d=start_d, e=start_e)

        def begin_a():
            self.over(1, first, "").start()

        def begin_b():
            self.over(1, first, "").wait_recv()
            self.lines_start(first)

        def begin_c():
            self.lines_wait(first)
            self.over(2, d3, first + "z").start()

        def begin_d():
            self.wait_for(self.part(first + "z", **self.flip(d3)), 2)
            self.sibling().start()

        return dict(a=begin_a, b=begin_b, c=begin_c, d=begin_d, e=start_e)


class Scatter(Way):
    def __init__(self, net, region, order, sems, first, third, line):
        super().__init__(net, region, order, sems)
        self.into_first, self.into_third, self.into_line = first, third, line
        self.inner = order[0] != "z"
        self.near = order[0] if self.inner else order[1]
        self.far = order[2]
        self.rest = self.near + "z" if self.inner else "z"

    def sibling(self, core):
        part = self.region(None, core, None, None)
        return self.copy(part, part, 4, self.net.across("c"), self.mate)

    def sibling_out(self):
        return self.sibling(1 - self.net.c)

    def sibling_in(self):
        return self.sibling(self.net.c)

    def first(self):
        if self.inner:
            return self.copy(self.part(self.rest, **self.flip(self.far)), self.into_first, 0, self.net.across(self.far))
        part = self.part("z", **self.flip(self.far, self.near))
        return self.copy(part, self.into_first.at[0], 0, self.net.across(self.far))

    def second(self):
        part = self.part("z", **self.flip(self.far))
        return self.copy(part, self.into_first.at[1], 1, self.net.across(self.far))

    def third(self):
        part = self.part("" if self.inner else "z", **self.flip(self.near))
        return self.copy(part, self.into_third, 2, self.net.across(self.near))

    def along(self, k):
        ahead = self.ahead(k)
        part = self.part(self.near if self.inner else "", z=ahead)
        return self.copy(part, self.into_line.at[k - 1], 3, self.net.dev(z=ahead))

    @staticmethod
    def add(part, *came):
        total = part[...].astype(jnp.float32)
        for one in came:
            total = total + one[...].astype(jnp.float32)
        part[...] = total.astype(part.dtype)

    def lines_start(self):
        for k in range(1, NZ):
            self.along(k).start()

    def lines_wait(self):
        self.wait_for(self.into_line, 3)
        return [self.into_line.at[k] for k in range(NZ - 1)]

    def spread(self):
        self.first().start()
        if not self.inner:
            self.second().start()

    def fold_first(self):
        self.first().wait_recv()
        if self.inner:
            self.add(self.part(self.rest), self.into_first)
            self.lines_start()
        else:
            self.add(self.part("z", **self.flip(self.near)), self.into_first.at[0])
            self.third().start()

    def fold_second(self):
        if self.inner:
            self.add(self.part(self.near), *self.lines_wait())
            self.third().start()
        else:
            self.second().wait_recv()
            self.add(self.part("z"), self.into_first.at[1])

    def fold_third(self):
        self.third().wait_recv()
        if not self.inner:
            self.add(self.part("z"), self.into_third)
            self.lines_start()

    def total(self):
        came = [self.into_third] if self.inner else self.lines_wait()
        out = self.part()[...].astype(jnp.float32)
        for one in came:
            out = out + one[...].astype(jnp.float32)
        return out


def region_square(ref):
    pair, half = ref.shape[2] // NZ, ref.shape[3] // 2

    def region(y, c, z, x):
        rows = pl.ds(0, pair * NZ) if z is None else pl.ds(pl.multiple_of(z * pair, 16), pair)
        cols = pl.ds(0, half * 2) if x is None else pl.ds(pl.multiple_of(x * half, LANES), half)
        return ref.at[pl.ds(0, 2) if y is None else y, c, rows, cols]

    return region


def region_lead(ref, start, size):
    run = ref.shape[4] // 2

    def region(y, c, z, x):
        rows = pl.ds(0, 2 * run) if x is None else pl.ds(pl.multiple_of(x * run, 16), run)
        high, low = (pl.ds(0, 2), pl.ds(0, 2)) if z is None else (lax.div(z, 2), lax.rem(z, 2))
        return ref.at[pl.ds(0, 2) if y is None else y, c, high, low, rows, pl.ds(start, size)]

    return region


def region_small(ref):
    def region(y, c, z, x):
        return ref.at[pl.ds(0, 2) if y is None else y, c, pl.ds(0, NZ) if z is None else z, pl.ds(0, 2) if x is None else x]

    return region


def bulk_square(ref):
    pair, half = ref.shape[2] // NZ, ref.shape[3] // 2
    return lambda k: ref.at[pl.ds(0, k // 3), 0, pl.ds(0, 3 * pair), pl.ds(0, half)]


def bulk_lead(ref, start, size):
    rows = 3 * ref.shape[4] // 4
    return lambda k: ref.at[0, 0, pl.ds(0, k // 3), pl.ds(0, 2), pl.ds(0, rows), pl.ds(start, size)]


def bulk_small(ref):
    return lambda k: ref.at[0, 0, pl.ds(0, k), 0]


UNITS = range(13)
GATHER = ("zyx", "zxy", "zxy", "zyx", "zxy", "yzx", "xzy", "yzx", "zxy", "zxy", "yzx", "zyx", "zxy")
SCATTER = ("zxy", "zyx", "zxy", "yzx", "zxy", "yzx", "zxy", "zxy", "zxy", "yzx", "zxy", "xzy", "zxy")
OUTER = ((0, 256), (256, 256), (512, 128), (640, 128))


LANDING = ("first", "third", "line")


def landing_shapes(i, pair, half, run):
    order = SCATTER[i]
    if i < 8:
        piece, strip, wide = (pair, half), (pair * NZ, half), (pair * NZ, 2 * half)
        double = (pair, 2 * half)
    else:
        size = OUTER[i - 8][1]
        piece, strip, wide = (run, size), (2, 2, run, size), (2, 2, 2 * run, size)
        double = (2 * run, size)
    if order[0] == "z":
        return (2,) + strip, strip, (NZ - 1,) + piece
    if order[0] == "x":
        return wide, piece, (NZ - 1,) + double
    return (2,) + strip, piece, (NZ - 1, 2) + piece


def mm(left, right):
    return jnp.dot(left, right, preferred_element_type=jnp.float32)


def mm_nt(left, right):
    return lax.dot_general(left, right, (((1,), (1,)), ((), ())), preferred_element_type=jnp.float32)


def mm_tn(left, right):
    return lax.dot_general(left, right, (((0,), (0,)), ((), ())), preferred_element_type=jnp.float32)


def eights(block):
    return jnp.sum(block.reshape(block.shape[0] // 8, 8, block.shape[1]), axis=0)


STEP = 64
F32, BF16 = jnp.float32, jnp.bfloat16


def layer_kernel(names, *refs):
    r = SimpleNamespace(**dict(zip(names, refs, strict=True)))
    net = Net()
    frame_count, width = r.frames.shape
    half = width // 2
    lead = r.wq.shape[0]
    pair = 2 * lead
    own_rows = pl.ds(pl.multiple_of(net.z * pair, 16), pair)
    own_cols = pl.ds(pl.multiple_of(net.x * half, LANES), half)
    w8, w2 = r.w8, r.w2
    g2, e12 = r.g2, r.e12

    x_in = pltpu.make_async_copy(r.frames, r.xbuf, r.isem.at[0])
    g_in = pltpu.make_async_copy(r.grad_out, r.gbuf, r.isem.at[1])
    net.greet()
    x_in.start()
    g_in.start()

    gather, scatter = [], []
    for i in UNITS:
        cols = OUTER[i - 8] if 8 <= i < 12 else None
        if i < 8:
            region, bulk = region_square(w8.at[i]), bulk_square(w8.at[i])
            to = region_square(w2.at[i // 2, i % 2]) if i < 3 else region
        elif cols:
            region, bulk, to = region_lead(w2, *cols), bulk_lead(w2, *cols), region_lead(g2, *cols)
        else:
            region, bulk = region_small(r.small), bulk_small(r.small)
        kind = 0 if i < 8 else 1 if cols else 2
        sems = r.gout.at[kind], r.gmate.at[kind], r.grecv.at[i]
        gather.append(Gather(net, region, GATHER[i], sems, bulk).stages())
        if i < 12:
            landing = (getattr(r, f"{name}{i}") for name in LANDING)
            sems = r.sout.at[kind], r.smate.at[kind], r.srecv.at[i]
            scatter.append(Scatter(net, to, SCATTER[i], sems, *landing))

    def sent(ref, sem):
        pltpu.make_async_remote_copy(
            src_ref=ref, dst_ref=ref, send_sem=sem, recv_sem=r.grecv.at[0, 0], device_id=net.across("c"),
            device_id_type=MESH).wait_send()

    def all_sent(out, mate):
        runs = frame_count - 2 * 16
        sent(e12.at[pl.ds(0, 12), pl.ds(0, runs), pl.ds(0, half)], out.at[0])
        sent(r.act.at[pl.ds(0, 3), pl.ds(0, runs), :], out.at[1])
        sent(w8.at[:, :, 0], mate.at[0])
        sent(w2.at[:, 0], mate.at[1])

    def shard(u):
        if u < 4:
            return (r.wq, r.wk, r.wv, r.wo)[u][...]
        return r.wi[:, (u - 4) * width:(u - 3) * width]

    def swap(u):
        return pltpu.make_async_remote_copy(
            src_ref=r.xs.at[u], dst_ref=r.xr.at[u], send_sem=r.xss.at[0], recv_sem=r.xrs.at[u],
            device_id=net.across("x"), device_id_type=MESH)

    def offer(u):
        v = shard(u).astype(F32)
        theirs = jnp.where(net.x == 0, v[:, half:], v[:, :half])
        r.xs[u] = jnp.concatenate([theirs, jnp.zeros((8, half), F32)], axis=0).astype(BF16)

    def merge(u):
        swap(u).wait_recv()
        v = shard(u).astype(F32)
        mine = jnp.where(net.x == 0, v[:, :half], v[:, half:])
        came = r.xr[u].astype(F32)[:lead]
        first, second = jnp.where(net.x == 0, mine, came), jnp.where(net.x == 0, came, mine)
        w8[u, net.y, net.c, own_rows, own_cols] = jnp.concatenate([first, second], axis=0).astype(BF16)

    def place():
        for k in range(8):
            offer(k)
        pack = r.pack
        pack[...] = jnp.zeros_like(pack)
        for row, one in enumerate((r.bq, None, r.bv, r.bo, r.g1, r.s1, r.b2, r.gg2, r.s2, r.bi1)):
            if one is not None:
                size = one.shape[0]
                pack[row:row + 1, :size] = one[...].astype(F32).reshape(1, size)
        r.small[net.y, net.c, net.z, net.x] = pack[...].astype(BF16)
        w2[net.y, net.c, lax.div(net.z, 2), lax.rem(net.z, 2), pl.ds(pl.multiple_of(net.x * 4 * lead, 16), 4 * lead), :] = (
            r.wouter[...])
        masks()
        turn()
        net.meet()
        for k in range(8):
            swap(k).start()

    l0 = r.lengths[0, 0]
    l1 = l0 + r.lengths[0, 1]
    vec, bi, gsm, cs = r.vec, r.bi, r.gsm, r.cs
    fa, q3 = r.fa, r.q3
    act, gp, act_t = r.act, r.gp, r.act_t

    def loop(body, step=STEP, total=frame_count):
        def one(i, carry):
            body(pl.ds(pl.multiple_of(i * step, step), step))
            return carry

        lax.fori_loop(0, total // step, one, 0)

    def groups(shape, dim, start=0):
        place = lax.broadcasted_iota(jnp.int32, shape, dim) + start
        return (place >= l0).astype(jnp.int32) + (place >= l1).astype(jnp.int32)

    def masks():
        shape = (frame_count, LANES)
        lane = lax.broadcasted_iota(jnp.int32, shape, 1)
        group = groups(shape, 0)
        for e in range(2):
            spare = lane - (1 - e) * (LANES // 2)
            inside = (spare >= 0) & (spare < 3)
            r.mq[e] = jnp.where(inside & (spare != group), -1e30, 0.0).astype(BF16)
            r.mk[e] = jnp.where(inside & (spare == group), 1.0, 0.0).astype(BF16)

    def vectors():
        got = r.small[...].reshape(32 * 16, LANES)
        lane = lax.broadcasted_iota(jnp.int32, (LANES, width), 0)
        col = lax.broadcasted_iota(jnp.int32, (LANES, width), 1)
        tile = jnp.where((lane < lead) & (lane == lax.rem(col, lead)), 1.0, 0.0).astype(BF16)
        wide = mm(got, tile).reshape(32, 16, width)
        owner = lax.broadcasted_iota(jnp.int32, wide.shape, 0)
        place = lax.div(lax.broadcasted_iota(jnp.int32, wide.shape, 2), lead)
        vec[...] = jnp.sum(jnp.where(owner == place, wide, 0.0), axis=0)
        inner = got.astype(F32).reshape(32, 16, LANES)[:, 9, :].astype(BF16)
        for c in range(4):
            lane = lax.broadcasted_iota(jnp.int32, (LANES, width), 0)
            col = lax.broadcasted_iota(jnp.int32, (LANES, width), 1) + c * width
            tile = jnp.where((lane < 4 * lead) & (lane == lax.rem(col, 4 * lead)), 1.0, 0.0).astype(BF16)
            wide = mm(inner, tile)
            owner = lax.broadcasted_iota(jnp.int32, wide.shape, 0)
            place = lax.div(lax.broadcasted_iota(jnp.int32, wide.shape, 1) + c * width, 4 * lead)
            bi[c] = jnp.sum(jnp.where(owner == place, wide, 0.0), axis=0, keepdims=True)

    def square(u):
        return w8[u].reshape(width, width)

    def project(u):
        rows = mm(r.xbuf[...], square(u)) + vec[pl.ds(u, 1), :]
        q3[u] = (rows * 0.125 if u == 0 else rows).astype(BF16)

    def head_lanes(shape, e):
        return lax.div(lax.broadcasted_iota(jnp.int32, shape, 1), LANES // 2) == e

    ROWS = 256

    def attend(p):
        cols = pl.ds(pl.multiple_of(p * LANES, LANES), LANES)
        sides = []
        for e in range(2):
            mine = head_lanes((frame_count, LANES), e)
            keys = jnp.where(mine, q3[1, :, cols], r.mk[e])
            vals = jnp.where(mine, q3[2, :, cols], jnp.ones((), BF16))
            sides.append((keys, vals))
        for i in range(frame_count // ROWS):
            rows = pl.ds(i * ROWS, ROWS)
            outs = []
            for e in range(2):
                keys, vals = sides[e]
                mine = head_lanes((ROWS, LANES), e)
                query = jnp.where(mine, q3[0, rows, cols], r.mq[e, rows, :])
                scores = mm_nt(query, keys)
                top = jnp.max(scores, axis=1, keepdims=True)
                weights = jnp.exp(scores - top).astype(BF16)
                e12[2 * p + e, rows, :] = weights
                outs.append(mm(weights, vals))
            low = head_lanes((ROWS, LANES), 0)
            over = jnp.where(low, outs[0], outs[1])
            under = pltpu.roll(jnp.where(low, outs[1], outs[0]), LANES // 2, 1)
            inverse = 1.0 / under
            r.linv[rows, cols] = inverse
            r.ctx[rows, cols] = (over * inverse).astype(BF16)

    def norm_one():
        fa[...] = mm(r.ctx[...], square(3))
        r.ctx_t[...] = jnp.transpose(r.ctx[...]).reshape(r.ctx_t.shape)

        def body(rows):
            v = r.xbuf[rows, :].astype(F32) + fa[rows, :] + vec[3:4, :]
            center = v - jnp.mean(v, axis=1, keepdims=True)
            scale = lax.rsqrt(jnp.mean(center * center, axis=1, keepdims=True) + 1e-05)
            normed = center * scale
            r.n1[rows, :] = normed
            r.r1[rows, :] = jnp.broadcast_to(scale, (STEP, LANES))
            r.low[rows, :] = (normed * vec[4:5, :] + vec[5:6, :]).astype(BF16)

        loop(body)
        r.hid_t[...] = jnp.transpose(r.low[...]).reshape(r.hid_t.shape)

    def feed(c):
        fa[...] = mm(r.low[...], square(4 + c))

        def body(rows):
            v = fa[rows, :] + bi[c]
            phi = 0.5 + 0.5 * lax.erf(v * 0.7071067811865476)
            bell = jnp.exp(v * v * -0.5) * 0.3989422804014327
            act[c, rows, :] = (v * phi).astype(BF16)
            gp[c, rows, :] = (phi + v * bell).astype(BF16)

        loop(body, 32)
        act_t[c // 2, c % 2] = jnp.transpose(act[c])

    def block(ref, c):
        return ref[c // 2, c % 2].reshape(width, width)

    def feed_out(k):
        start, size = OUTER[k]
        cols = slice(start, start + size)
        total = None
        for c in range(4):
            one = mm(act[c], w2[c // 2, c % 2, :, :, :, cols].reshape(width, size))
            total = one if total is None else total + one
        fa[:, cols] = total

    def fold(slot, row):
        gsm[row:row + 1, :] = jnp.sum(cs[slot], axis=0, keepdims=True)

    def norm_two():
        g_in.wait()
        cs[...] = jnp.zeros_like(cs)

        def body(rows):
            hidden = r.n1[rows, :] * vec[4:5, :] + vec[5:6, :]
            v = hidden + fa[rows, :] + vec[6:7, :]
            center = v - jnp.mean(v, axis=1, keepdims=True)
            scale = lax.rsqrt(jnp.mean(center * center, axis=1, keepdims=True) + 1e-05)
            normed = center * scale
            place = lax.broadcasted_iota(jnp.int32, normed.shape, 0) + rows.start
            live = jnp.where(place < l1, 1.0, 0.0)
            r.xbuf[rows, :] = ((normed * vec[7:8, :] + vec[8:9, :]) * live).astype(BF16)
            top = r.gbuf[rows, :].astype(F32) * live
            e = top * vec[7:8, :]
            d = e - jnp.mean(e, axis=1, keepdims=True) - normed * jnp.mean(e * normed, axis=1, keepdims=True)
            d = d * scale
            r.d2[rows, :] = d
            low = d.astype(BF16)
            r.low[rows, :] = low
            cs[0] += eights(top * normed)
            cs[1] += eights(top)
            cs[2] += eights(low.astype(F32))

        loop(body)
        fold(0, 7)
        fold(1, 8)
        fold(2, 6)

    layer_out = pltpu.make_async_copy(r.xbuf, r.layer_out, r.isem.at[0])
    frames_out = pltpu.make_async_copy(r.gbuf, r.frames_grad, r.isem.at[1])

    def back_feed(c):
        fa[...] = mm_nt(r.low[...], block(w2, c))
        cs[0] = jnp.zeros_like(cs[0])

        def body(rows):
            low = (fa[rows, :] * gp[c, rows, :].astype(F32)).astype(BF16)
            gp[c, rows, :] = low
            cs[0] += eights(low.astype(F32))

        loop(body)
        fold(0, 9 + c)

    def grad_square(u, left, right, own):
        core = net.c if own else 1 - net.c
        to = w2.at[u // 2, u % 2] if u < 3 else w8.at[u]
        rows = mm(left[:, core].reshape(2 * pair * NZ, frame_count), right()).reshape(2, pair * NZ, width)
        if own:
            scatter[u].sibling_in().wait_recv()
            rows = rows + to[:, core].astype(F32)
        to[:, core] = rows.astype(BF16)

    def grad_outer(i, own):
        core = net.c if own else 1 - net.c
        start, size = OUTER[i - 8]
        cols = pl.ds(start, size)
        left = act_t[:, core].reshape(2 * width, frame_count)
        rows = mm(left, r.low[:, cols]).reshape((2,) + g2.shape[2:5] + (size,))
        if own:
            scatter[i].sibling_in().wait_recv()
            rows = rows + g2[:, core, :, :, :, cols].astype(F32)
        g2[:, core, :, :, :, cols] = rows.astype(BF16)

    def back_hidden(c):
        got = mm_nt(gp[c], square(4 + c))
        fa[...] = got if c == 0 else fa[...] + got

    def back_norm_one():
        cs[...] = jnp.zeros_like(cs)

        def body(rows):
            d = r.d2[rows, :] + fa[rows, :]
            normed = r.n1[rows, :]
            e = d * vec[4:5, :]
            cs[0] += eights(d * normed)
            cs[1] += eights(d)
            d = e - jnp.mean(e, axis=1, keepdims=True) - normed * jnp.mean(e * normed, axis=1, keepdims=True)
            d = d * r.r1[rows, 0:1]
            r.d2[rows, :] = d
            low = d.astype(BF16)
            r.low[rows, :] = low
            cs[2] += eights(low.astype(F32))

        loop(body)
        fold(0, 4)
        fold(1, 5)
        fold(2, 3)

    def back_context():
        act[3] = mm_nt(r.low[...], square(3)).astype(BF16)

    def back_attend(p):
        cols = pl.ds(pl.multiple_of(p * LANES, LANES), LANES)
        shape = (frame_count, LANES)
        low = head_lanes(shape, 0)
        scaled = (act[3, :, cols].astype(F32) * r.linv[:, cols]).astype(BF16)
        product = scaled.astype(F32) * r.ctx[:, cols].astype(F32)
        lane = lax.broadcasted_iota(jnp.int32, shape, 1)
        k2, v2, q2 = q3[1, :, cols], q3[2, :, cols], q3[0, :, cols]
        dq, dk, dv = [], [], []
        for e in range(2):
            mine = head_lanes(shape, e)
            spare = lane - (1 - e) * (LANES // 2)
            dot = jnp.sum(jnp.where(mine, product, 0.0), axis=1, keepdims=True)
            high = dot.astype(BF16).astype(F32)
            extra = jnp.where(spare == 0, high, jnp.where(spare == 1, dot - high, 0.0)).astype(BF16)
            left = jnp.where(mine, scaled, extra)
            minus = jnp.where((spare == 0) | (spare == 1), -1.0, 0.0).astype(BF16)
            right = jnp.where(mine, v2, minus)
            for i in range(frame_count // ROWS):
                part = slice(i * ROWS, (i + 1) * ROWS)
                r.ds[e, part, :] = (e12[2 * p + e, part, :].astype(F32) * mm_nt(left[part], right)).astype(BF16)
            dq.append(mm(r.ds[e], k2))
            dk.append(mm_tn(r.ds[e], q2))
            dv.append(mm_tn(e12[2 * p + e], scaled))
        act[0, :, cols] = (jnp.where(low, dq[0], dq[1]) * 0.125).astype(BF16)
        act[1, :, cols] = jnp.where(low, dk[0], dk[1]).astype(BF16)
        act[2, :, cols] = jnp.where(low, dv[0], dv[1]).astype(BF16)

    def bias_sums():
        cs[...] = jnp.zeros_like(cs)

        def body(rows):
            cs[0] += eights(act[0, rows, :].astype(F32))
            cs[1] += eights(act[2, rows, :].astype(F32))

        loop(body)
        fold(0, 0)
        fold(1, 2)
        gsm[1:2, :] = jnp.zeros((1, width), F32)
        gsm[13:16, :] = jnp.zeros((3, width), F32)

    def back_frames(k):
        got = mm_nt(act[k], square(k))
        if k < 2:
            fa[...] = (r.d2 if k == 0 else fa)[...] + got
            return
        layer_out.wait()
        r.gbuf[...] = (fa[...] + got).astype(BF16)
        frames_out.start()

    def small_copy(k, device):
        return pltpu.make_async_remote_copy(
            src_ref=r.sm.at[k], dst_ref=r.sl.at[k], send_sem=r.sms.at[0], recv_sem=r.smr.at[k],
            device_id=device, device_id_type=MESH)

    def small_step(k):
        if k == 0:
            r.sm[0] = gsm[...]
        else:
            r.sm[k] = r.sm[k - 1] + r.sl[k - 1]
        if k < 3:
            small_copy(k, net.across("cyx"[k])).start()

    def small_wait(k):
        small_copy(k, net.across("cyx"[k])).wait_recv()

    def small_line(k):
        return pltpu.make_async_remote_copy(
            src_ref=r.sm.at[3], dst_ref=r.sl.at[2 + k], send_sem=r.sms.at[0], recv_sem=r.smr.at[3],
            device_id=net.dev(z=lax.rem(net.z + k, NZ)), device_id_type=MESH)

    def small_total():
        landed = r.sl.at[pl.ds(3, NZ - 1)]
        pltpu.make_async_remote_copy(
            src_ref=landed, dst_ref=landed, send_sem=r.sms.at[0], recv_sem=r.smr.at[3], device_id=net.across("c"),
            device_id_type=MESH).wait_recv()
        whole = r.sm[3] + r.sl[3] + r.sl[4] + r.sl[5]
        index = (net.y * 2 + net.c) * 2 * NZ + net.z * 2 + net.x
        turned = pltpu.roll(whole, lax.rem(width - index * lead, width), 1)
        row = lax.broadcasted_iota(jnp.int32, (16, width), 0)
        block = lax.div(index, 8)
        inner = jnp.sum(jnp.where(row == 9 + block, whole, 0.0), axis=0, keepdims=True)
        inner = pltpu.roll(jnp.broadcast_to(inner, (8, width)), lax.rem(width - lax.rem(index, 8) * 4 * lead, width), 1)
        r.gsmall[0:8, :] = turned[0:8, :LANES]
        r.gsmall[8:16, :] = jnp.where(row[:8, :LANES] == 0, turned[8:9, :LANES], inner[:, :LANES])

    def swap_back(u):
        return pltpu.make_async_remote_copy(
            src_ref=r.ys.at[u], dst_ref=r.yr.at[u], send_sem=r.yss.at[0], recv_sem=r.yrs.at[0],
            device_id=net.across("x"), device_id_type=MESH)

    def out_of(u):
        if u < 4:
            return (r.gwq, r.gwk, r.gwv, r.gwo)[u], 0
        return r.gwi, (u - 4) * width

    def total_square(u):
        r.f8[...] = scatter[u].total()
        out, start = out_of(u)
        mine, theirs = pl.multiple_of(net.x * lead, 8), pl.multiple_of((1 - net.x) * lead, 8)
        r.ys[u] = jnp.concatenate([r.f8[pl.ds(theirs, lead), :], jnp.zeros((8, half), F32)], axis=0).astype(BF16)
        swap_back(u).start()
        out[:, pl.ds(pl.multiple_of(start + net.x * half, LANES), half)] = r.f8[pl.ds(mine, lead), :]

    def last():
        pltpu.make_async_remote_copy(
            src_ref=r.ys, dst_ref=r.yr, send_sem=r.yss.at[0], recv_sem=r.yrs.at[0], device_id=net.across("x"),
            device_id_type=MESH).wait_recv()
        for u in range(8):
            out, start = out_of(u)
            out[:, pl.ds(pl.multiple_of(start + (1 - net.x) * half, LANES), half)] = r.yr[u].astype(F32)[:lead]

    def total_outer(i):
        r.gwouter[:, pl.ds(*OUTER[i - 8])] = scatter[i].total()

    def unit(i, left=None, right=None):
        steps = SimpleNamespace(**gather[i])
        if i == len(UNITS) - 1:
            return steps
        way, square = scatter[i], i < 8

        def half_of(own):
            if square:
                grad_square(i, left, right, own)
            else:
                grad_outer(i, own)

        def away():
            half_of(False)
            way.sibling_out().start()

        def home():
            half_of(True)
            way.spread()

        steps.away, steps.home = away, home
        steps.t, steps.u, steps.v = way.fold_first, way.fold_second, way.fold_third
        if square:
            steps.p = functools.partial(merge, i)
            steps.x = functools.partial(total_square, i)
        else:
            steps.x = functools.partial(total_outer, i)
        return steps

    def give(k):
        pl.semaphore_signal(r.free.at[k], inc=1, device_id=net.across("c"), device_id_type=MESH)

    def take(k):
        pl.semaphore_wait(r.free.at[k], 1)

    def turn():
        x_in.wait()
        r.xt[...] = jnp.transpose(r.xbuf[...]).reshape(r.xt.shape)

    def gather_end():
        all_sent(r.gout, r.gmate)
        sent(e12.at[0, pl.ds(0, 15 * 16), pl.ds(0, LANES)], r.gout.at[2])
        sent(r.small.at[:, 0], r.gmate.at[2])

    def small(k):
        if k > 0:
            small_wait(k - 1)
        small_step(k)
        if k == 3:
            for one in range(1, NZ):
                small_line(one).start()

    def end():
        all_sent(r.sout, r.smate)
        sent(r.xs, r.xss.at[0])
        sent(r.ys, r.yss.at[0])
        sent(r.sl, r.sms.at[0])
        frames_out.wait()

    def go(*steps):
        for step in steps:
            step()

    q, k, v = (unit(u, r.xt, lambda u=u: act[u]) for u in range(3))
    o = unit(3, r.ctx_t, lambda: r.low[...])
    i0, i1, i2, i3 = (unit(4 + u, r.hid_t, lambda u=u: gp[u]) for u in range(4))
    w0, w1, w2_, w3 = (unit(8 + u) for u in range(4))
    s = unit(12)
    place()
    go(s.a, w3.a, k.p, k.a, w2_.a, s.b, i0.p, q.p, q.a, i1.p, i1.a, v.p)
    go(w3.b, i2.p, i2.a, s.c, i3.p, i3.a, v.a, o.p, o.a, i0.a, k.b, w0.a)
    go(w3.c, s.d, q.b, s.e, k.c, v.b)
    vectors()
    go(w1.a, q.c, v.c, k.d, o.b, q.d, i0.b, v.d, k.e, i1.b)
    project(1)
    go(v.e, w0.b, o.c, i2.b, q.e)
    project(0)
    go(i3.b, w0.c, i0.c, i1.c)
    project(2)
    attend(5)
    go(o.d)
    attend(3)
    go(w3.d, w0.d, w2_.b)
    attend(2)
    go(i2.c, w1.b, i0.d, i1.d)
    attend(1)
    attend(4)
    attend(0)
    go(o.e, i0.e, w1.c, i3.c)
    norm_one()
    go(w0.e, i1.e)
    feed(1)
    go(i2.d, w2_.c)
    feed(0)
    go(w3.e, i3.d, i2.e)
    feed(2)
    go(w1.d, i3.e)
    feed(3)
    go(w2_.d)
    feed_out(3)
    feed_out(0)
    go(w1.e)
    feed_out(1)
    go(w2_.e)
    feed_out(2)
    norm_two()
    go(w3.away, w1.away, w0.away)
    gather_end()
    go(w2_.away, w3.home)
    back_feed(2)
    go(w1.home)
    back_feed(0)
    go(w0.home)
    back_feed(1)
    back_feed(3)
    go(w3.t)
    give(0)
    back_hidden(0)
    take(0)
    back_hidden(1)
    back_hidden(2)
    back_hidden(3)
    give(1)
    take(1)
    go(i1.away, w1.t, w0.t, w2_.home, i2.away, i1.home)
    back_norm_one()
    back_context()
    give(2)
    go(i2.home, w0.u, i3.away, w0.v, i0.away)
    take(2)
    go(o.away, w2_.t)
    back_attend(5)
    go(i3.home, i2.t)
    back_attend(2)
    go(i1.t, w2_.u, o.home)
    back_attend(1)
    back_attend(3)
    go(i0.home)
    back_attend(4)
    go(w2_.v)
    back_attend(0)
    go(q.away)
    layer_out.start()
    go(v.away, i2.u, i3.t, i2.v)
    back_frames(0)
    go(q.home, o.t, i0.t, k.away, i3.u, i3.v, w0.x, q.t, v.home, i0.u, i0.v, k.home)
    bias_sums()
    go(v.t, k.t, q.u, q.v, w1.u, k.u, i3.x, o.u)
    small(0)
    go(i0.x, k.v)
    small(1)
    go(i2.x, w3.u, i1.u)
    back_frames(1)
    go(w1.v, o.v, v.u, v.v)
    small(2)
    go(q.x)
    back_frames(2)
    small(3)
    go(k.x, w1.x, w3.v, o.x, i1.v, w3.x, v.x, w2_.x, i1.x)
    small_total()
    last()
    end()


def kernel_device(
    frames, lengths, query_weight, query_bias, key_weight, value_weight, value_bias, output_weight, output_bias,
    first_gain, first_shift, inner_weight, inner_bias, outer_weight, outer_bias, second_gain, second_shift, grad_out,
):
    count, width = frames.shape
    lead = query_weight.shape[0]
    pair, half = 2 * lead, width // 2
    vmem, hbm = pl.BlockSpec(memory_space=pltpu.VMEM), pl.BlockSpec(memory_space=pl.ANY)
    smem = pl.BlockSpec(memory_space=pltpu.SMEM)
    args = dict(
        frames=(hbm, frames), grad_out=(hbm, grad_out), lengths=(smem, lengths), wq=(vmem, query_weight),
        wk=(vmem, key_weight), wv=(vmem, value_weight), wo=(vmem, output_weight), wi=(vmem, inner_weight),
        wouter=(vmem, outer_weight), bq=(vmem, query_bias), bv=(vmem, value_bias), bo=(vmem, output_bias),
        g1=(vmem, first_gain), s1=(vmem, first_shift), b2=(vmem, outer_bias), gg2=(vmem, second_gain),
        s2=(vmem, second_shift), bi1=(vmem, inner_bias))
    shape = jax.ShapeDtypeStruct
    outs = dict(
        layer_out=(hbm, shape((count, width), BF16)), frames_grad=(hbm, shape((count, width), BF16)),
        gwq=(vmem, shape((lead, width), F32)), gwk=(vmem, shape((lead, width), F32)),
        gwv=(vmem, shape((lead, width), F32)), gwo=(vmem, shape((lead, width), F32)),
        gwi=(vmem, shape(inner_weight.shape, F32)), gwouter=(vmem, shape(outer_weight.shape, F32)),
        gsmall=(vmem, shape((16, LANES), F32)))
    dma = pltpu.SemaphoreType.DMA
    big = (count, width)
    square = (2, 2, pair * NZ, width)
    turned = (2, 2, pair * NZ, count)
    lead_shape = (2, 2, 2, 2, 8 * lead, width)
    scratch = dict(
        w8=((8,) + square, BF16), w2=(lead_shape, BF16), g2=(lead_shape, BF16), small=((2, 2, NZ, 2, 16, LANES), BF16),
        pack=((16, LANES), F32), xs=((8, lead + 8, half), BF16), xr=((8, lead + 8, half), BF16),
        ys=((8, lead + 8, half), BF16), yr=((8, lead + 8, half), BF16), xbuf=(big, BF16), gbuf=(big, BF16), q3=((3,) + big, BF16),
        e12=((HEADS, count, count), BF16), linv=(big, F32), ctx=(big, BF16), xt=(turned, BF16), ctx_t=(turned, BF16),
        hid_t=(turned, BF16), low=(big, BF16), n1=(big, F32), r1=((count, LANES), F32), act=((4,) + big, BF16),
        gp=((4,) + big, BF16), act_t=((2, 2, width, count), BF16), fa=(big, F32), d2=(big, F32),
        ds=((2, count, count), BF16), mq=((2, count, LANES), BF16), mk=((2, count, LANES), BF16), vec=((16, width), F32),
        bi=((4, 1, width), F32), gsm=((16, width), F32), cs=((3, 8, width), F32), sm=((4, 16, width), F32),
        sl=((6, 16, width), F32), f8=((pair, half), F32))
    for i in range(12):
        for kind, size in zip(LANDING, landing_shapes(i, pair, half, 4 * lead), strict=True):
            scratch[f"{kind}{i}"] = (size, BF16)
    scratch = {k: pltpu.VMEM(*v) for k, v in scratch.items()}
    scratch.update(
        gout=dma((3,)), gmate=dma((3,)), grecv=dma((13, 4)), sout=dma((2,)), smate=dma((2,)), srecv=dma((12, 5)),
        xss=dma((1,)), xrs=dma((8,)), yss=dma((1,)), yrs=dma((1,)), sms=dma((1,)), smr=dma((4,)), isem=dma((2,)), free=pltpu.SemaphoreType.REGULAR((3,)))
    got = pl.pallas_call(
        functools.partial(layer_kernel, (*args, *outs, *scratch)),
        out_shape=[o[1] for o in outs.values()],
        in_specs=[a[0] for a in args.values()],
        out_specs=[o[0] for o in outs.values()],
        scratch_shapes=list(scratch.values()),
        compiler_params=pltpu.CompilerParams(collective_id=0, has_side_effects=True, vmem_limit_bytes=VMEM_BYTES),
    )(*(a[1] for a in args.values()))

    bias, wide = shape((lead,), F32), shape((4 * lead,), F32)
    vectors = {3: bias, 6: bias, 8: bias, 9: bias, 10: bias, 12: wide, 14: bias, 15: bias, 16: bias}
    row_of = {3: 0, 6: 2, 8: 3, 9: 4, 10: 5, 12: 9, 14: 6, 15: 7, 16: 8}
    places = [i for i in range(17) if i not in vectors]

    def publish(*refs):
        came, small, out = refs[:8], refs[8], refs[9:]
        for a, i in zip(came, places, strict=True):
            out[i][...] = a[...]
        for i, row in row_of.items():
            size = vectors[i].shape[0]
            out[i][...] = small[row:row + 1, :size].reshape(size)

    whole = dict(zip(places, (o[1] for o in list(outs.values())[:8]), strict=True))
    return tuple(pl.pallas_call(
        publish,
        out_shape=[vectors[i] if i in vectors else whole[i] for i in range(17)],
        in_specs=[vmem] * 9,
        out_specs=[vmem] * 17,
    )(*got))


VMEM_BYTES = 63 << 20


def solution(mesh):
    split = P(("dp", "fsdp"))
    rows = P(("dp", "fsdp"), None)
    in_specs = (
        rows, rows, rows, split, rows, rows, split, rows, split, split, split, rows, split, rows, split, split, split, rows,
    )
    out_specs = (
        rows, rows, rows, split, rows, rows, split, rows, split, split, split, rows, split, rows, split, split, split,
    )
    fits = mesh.shape["dp"] == 4 and mesh.shape["fsdp"] == 2 * NZ

    def per_device(frames, lengths, query_weight, *rest):
        lead, width = query_weight.shape
        good = fits and lead % 8 == 0 and 4 * lead <= LANES and width == 768
        run = kernel_device if good else general_device
        return run(frames, lengths, query_weight, *rest)

    return jax.shard_map(per_device, mesh=mesh, in_specs=in_specs, out_specs=out_specs, check_vma=False)
```

```python
import functools
from types import SimpleNamespace

import jax
import jax.numpy as jnp
from jax import lax
from jax.experimental import pallas as pl
from jax.experimental.pallas import tpu as pltpu
from jax.sharding import PartitionSpec as P

HEADS = 12


def layer_norm(values, gain_vec, shift_vec):
    center = values - jnp.mean(values, axis=-1, keepdims=True)
    spread = jnp.mean(center * center, axis=-1, keepdims=True)
    return center * lax.rsqrt(spread + 1e-05) * gain_vec + shift_vec


def exact_gelu(values):
    return jax.nn.gelu(values, approximate=False)


def matmul(left_side, right_side):
    return jnp.dot(left_side, right_side, preferred_element_type=jnp.float32)


def matmul_tn(left_side, right_side):
    return lax.dot_general(
        left_side, right_side, (((0,), (0,)), ((), ())), preferred_element_type=jnp.float32
    )


def matmul_nt(left_side, right_side):
    return lax.dot_general(
        left_side, right_side, (((1,), (1,)), ((), ())), preferred_element_type=jnp.float32
    )


def column_sums(values):
    return jnp.sum(values.astype(jnp.float32), axis=0)


def block_scores(query_block, key_heads, group_block, groups, score_scale):
    raw_scores = (
        jnp.einsum("qhd,khd->hqk", query_block, key_heads, preferred_element_type=jnp.float32)
        * score_scale
    )
    allowed = group_block[:, None] == groups[None, :]
    return jnp.where(allowed[None], raw_scores, -1e30)


def general_device(
    frames,
    lengths,
    query_weight,
    query_bias,
    key_weight,
    value_weight,
    value_bias,
    output_weight,
    output_bias,
    first_gain,
    first_shift,
    inner_weight,
    inner_bias,
    outer_weight,
    outer_bias,
    second_gain,
    second_shift,
    grad_out,
):
    frame_count = frames.shape[0]
    model_width = frames.shape[1]
    head_size = model_width // HEADS
    score_scale = head_size ** (-0.5)
    places = jnp.arange(frame_count, dtype=jnp.int32)
    bounds = jnp.stack([lengths[0, 0], lengths[0, 0] + lengths[0, 1]])
    groups = jnp.sum((places[:, None] >= bounds[None, :]).astype(jnp.int32), axis=1)
    live_mask = (places < bounds[-1]).astype(jnp.float32)
    gathered = (
        lax.all_gather(query_weight, ("dp", "fsdp"), axis=0, tiled=True),
        lax.all_gather(query_bias, ("dp", "fsdp"), axis=0, tiled=True),
        lax.all_gather(key_weight, ("dp", "fsdp"), axis=0, tiled=True),
        lax.all_gather(value_weight, ("dp", "fsdp"), axis=0, tiled=True),
        lax.all_gather(value_bias, ("dp", "fsdp"), axis=0, tiled=True),
        lax.all_gather(output_weight, ("dp", "fsdp"), axis=0, tiled=True),
        lax.all_gather(output_bias, ("dp", "fsdp"), axis=0, tiled=True),
        lax.all_gather(first_gain, ("dp", "fsdp"), axis=0, tiled=True),
        lax.all_gather(first_shift, ("dp", "fsdp"), axis=0, tiled=True),
        lax.all_gather(inner_weight, ("dp", "fsdp"), axis=0, tiled=True),
        lax.all_gather(inner_bias, ("dp", "fsdp"), axis=0, tiled=True),
        lax.all_gather(outer_weight, ("dp", "fsdp"), axis=0, tiled=True),
        lax.all_gather(outer_bias, ("dp", "fsdp"), axis=0, tiled=True),
        lax.all_gather(second_gain, ("dp", "fsdp"), axis=0, tiled=True),
        lax.all_gather(second_shift, ("dp", "fsdp"), axis=0, tiled=True),
    )
    (
        query_mat,
        query_vec,
        key_mat,
        value_mat,
        value_vec,
        output_mat,
        output_vec,
        first_scale,
        first_offset,
        inner_mat,
        inner_vec,
        outer_mat,
        outer_vec,
        second_scale,
        second_offset,
    ) = gathered
    query_rows = (matmul(frames, query_mat) + query_vec.astype(jnp.float32)).astype(jnp.bfloat16)
    key_rows = matmul(frames, key_mat).astype(jnp.bfloat16)
    value_rows = (matmul(frames, value_mat) + value_vec.astype(jnp.float32)).astype(jnp.bfloat16)
    query_heads = query_rows.reshape(frame_count, HEADS, head_size)
    key_heads = key_rows.reshape(frame_count, HEADS, head_size)
    value_heads = value_rows.reshape(frame_count, HEADS, head_size)
    scores = block_scores(query_heads, key_heads, groups, groups, score_scale)
    row_max = jnp.max(scores, axis=-1, keepdims=True)
    raw_weights = jnp.exp(scores - row_max)
    row_total = jnp.sum(raw_weights, axis=-1, keepdims=True)
    attn_prob = raw_weights / row_total
    log_totals = row_max + jnp.log(row_total)
    context_parts = jnp.einsum(
        "hqk,khd->qhd",
        attn_prob.astype(jnp.bfloat16),
        value_heads,
        preferred_element_type=jnp.float32,
    )
    context_rows = context_parts.reshape(frame_count, model_width).astype(jnp.bfloat16)
    frames_float = frames.astype(jnp.float32)
    resid_one = frames_float + matmul(context_rows, output_mat) + output_vec.astype(jnp.float32)
    hidden, first_pull = jax.vjp(
        layer_norm, resid_one, first_scale.astype(jnp.float32), first_offset.astype(jnp.float32)
    )
    hidden_low = hidden.astype(jnp.bfloat16)
    inner_pre = matmul(hidden_low, inner_mat) + inner_vec.astype(jnp.float32)
    active, gelu_pull = jax.vjp(exact_gelu, inner_pre)
    active_low = active.astype(jnp.bfloat16)
    outer_out = matmul(active_low, outer_mat) + outer_vec.astype(jnp.float32)
    normed_out, second_pull = jax.vjp(
        layer_norm,
        hidden + outer_out,
        second_scale.astype(jnp.float32),
        second_offset.astype(jnp.float32),
    )
    layer_out = (normed_out * live_mask[:, None]).astype(jnp.bfloat16)
    grad_top = grad_out.astype(jnp.float32) * live_mask[:, None]
    grad_two, second_gain_grad, second_shift_grad = second_pull(grad_top)
    grad_outer = grad_two.astype(jnp.bfloat16)
    outer_mat_grad = matmul_tn(active_low, grad_outer)
    outer_vec_grad = column_sums(grad_outer)
    (grad_inner,) = gelu_pull(matmul_nt(grad_outer, outer_mat))
    grad_inner_low = grad_inner.astype(jnp.bfloat16)
    inner_mat_grad = matmul_tn(hidden_low, grad_inner_low)
    inner_vec_grad = column_sums(grad_inner_low)
    grad_hidden = grad_two + matmul_nt(grad_inner_low, inner_mat)
    grad_one, first_gain_grad, first_shift_grad = first_pull(grad_hidden)
    grad_attn = grad_one.astype(jnp.bfloat16)
    output_mat_grad = matmul_tn(context_rows, grad_attn)
    output_vec_grad = column_sums(grad_attn)
    grad_context = (
        matmul_nt(grad_attn, output_mat).astype(jnp.bfloat16).reshape(frame_count, HEADS, head_size)
    )
    scores = block_scores(query_heads, key_heads, groups, groups, score_scale)
    attn_prob = jnp.exp(scores - log_totals)
    grad_prob = jnp.einsum(
        "qhd,khd->hqk", grad_context, value_heads, preferred_element_type=jnp.float32
    )
    inner_sum = jnp.sum(attn_prob * grad_prob, axis=-1, keepdims=True)
    grad_scores = (attn_prob * (grad_prob - inner_sum)).astype(jnp.bfloat16)
    query_grad_parts = (
        jnp.einsum("hqk,khd->qhd", grad_scores, key_heads, preferred_element_type=jnp.float32)
        * score_scale
    )
    key_grad_sum = (
        jnp.einsum("hqk,qhd->khd", grad_scores, query_heads, preferred_element_type=jnp.float32)
        * score_scale
    )
    value_grad_sum = jnp.einsum(
        "hqk,qhd->khd",
        attn_prob.astype(jnp.bfloat16),
        grad_context,
        preferred_element_type=jnp.float32,
    )
    grad_query = query_grad_parts.reshape(frame_count, model_width).astype(jnp.bfloat16)
    grad_key = key_grad_sum.reshape(frame_count, model_width).astype(jnp.bfloat16)
    grad_value = value_grad_sum.reshape(frame_count, model_width).astype(jnp.bfloat16)
    query_mat_grad = matmul_tn(frames, grad_query)
    query_vec_grad = column_sums(grad_query)
    key_mat_grad = matmul_tn(frames, grad_key)
    value_mat_grad = matmul_tn(frames, grad_value)
    value_vec_grad = column_sums(grad_value)
    frames_grad = (
        grad_one
        + matmul_nt(grad_query, query_mat)
        + matmul_nt(grad_key, key_mat)
        + matmul_nt(grad_value, value_mat)
    ).astype(jnp.bfloat16)
    shares = (
        lax.psum_scatter(query_mat_grad, ("dp", "fsdp"), scatter_dimension=0, tiled=True),
        lax.psum_scatter(query_vec_grad, ("dp", "fsdp"), scatter_dimension=0, tiled=True),
        lax.psum_scatter(key_mat_grad, ("dp", "fsdp"), scatter_dimension=0, tiled=True),
        lax.psum_scatter(value_mat_grad, ("dp", "fsdp"), scatter_dimension=0, tiled=True),
        lax.psum_scatter(value_vec_grad, ("dp", "fsdp"), scatter_dimension=0, tiled=True),
        lax.psum_scatter(output_mat_grad, ("dp", "fsdp"), scatter_dimension=0, tiled=True),
        lax.psum_scatter(output_vec_grad, ("dp", "fsdp"), scatter_dimension=0, tiled=True),
        lax.psum_scatter(first_gain_grad, ("dp", "fsdp"), scatter_dimension=0, tiled=True),
        lax.psum_scatter(first_shift_grad, ("dp", "fsdp"), scatter_dimension=0, tiled=True),
        lax.psum_scatter(inner_mat_grad, ("dp", "fsdp"), scatter_dimension=0, tiled=True),
        lax.psum_scatter(inner_vec_grad, ("dp", "fsdp"), scatter_dimension=0, tiled=True),
        lax.psum_scatter(outer_mat_grad, ("dp", "fsdp"), scatter_dimension=0, tiled=True),
        lax.psum_scatter(outer_vec_grad, ("dp", "fsdp"), scatter_dimension=0, tiled=True),
        lax.psum_scatter(second_gain_grad, ("dp", "fsdp"), scatter_dimension=0, tiled=True),
        lax.psum_scatter(second_shift_grad, ("dp", "fsdp"), scatter_dimension=0, tiled=True),
    )
    return (
        layer_out,
        frames_grad,
        shares[0],
        shares[1],
        shares[2],
        shares[3],
        shares[4],
        shares[5],
        shares[6],
        shares[7],
        shares[8],
        shares[9],
        shares[10],
        shares[11],
        shares[12],
        shares[13],
        shares[14],
    )


MESH = pl.DeviceIdType.MESH
NZ = 4
LANES = 128


class Net:
    def __init__(self):
        dp, fs = lax.axis_index("dp"), lax.axis_index("fsdp")
        self.y, self.c = lax.div(dp, 2), lax.rem(dp, 2)
        self.z, self.x = lax.div(fs, 2), lax.rem(fs, 2)

    def dev(self, y=None, c=None, z=None, x=None):
        y = self.y if y is None else y
        c = self.c if c is None else c
        z = self.z if z is None else z
        x = self.x if x is None else x
        return (y * 2 + c, z * 2 + x)

    def across(self, dim):
        if dim == "x":
            return self.dev(x=1 - self.x)
        if dim == "y":
            return self.dev(y=1 - self.y)
        return self.dev(c=1 - self.c)

    def greet(self):
        bar = pltpu.get_barrier_semaphore()

        def tell(device):
            pl.semaphore_signal(bar, inc=1, device_id=device, device_id_type=MESH)

        for dim in "xyc":
            tell(self.across(dim))
        for k in range(1, NZ):
            tell(self.dev(z=lax.rem(self.z + k, NZ)))

    def meet(self):
        pl.semaphore_wait(pltpu.get_barrier_semaphore(), 3 + NZ - 1)


class Way:
    def __init__(self, net, region, order, sems):
        self.net, self.region, self.order = net, region, order
        self.out, self.mate, self.recv = sems

    def copy(self, src, dst, slot, device, send=None):
        return pltpu.make_async_remote_copy(
            src_ref=src, dst_ref=dst, send_sem=self.out if send is None else send, recv_sem=self.recv.at[slot],
            device_id=device, device_id_type=MESH)

    def wait_for(self, ref, slot):
        self.copy(ref, ref, slot, self.net.across("c")).wait_recv()

    def part(self, have="", **at):
        n = self.net
        for d in "yzx":
            at.setdefault(d, None if d in have else getattr(n, d))
        return self.region(at["y"], n.c, at["z"], at["x"])

    def flip(self, *dims):
        return {d: 1 - getattr(self.net, d) for d in dims}

    def ahead(self, k):
        return lax.rem(self.net.z + k, NZ)


class Gather(Way):
    def __init__(self, net, region, order, sems, bulk):
        super().__init__(net, region, order, sems)
        self.bulk = bulk

    def lines_start(self, have):
        part = self.part(have)
        for k in range(1, NZ):
            self.copy(part, part, 0, self.net.dev(z=self.ahead(k))).start()

    def lines_wait(self, have):
        self.wait_for(self.bulk(len(have) * (NZ - 1) + NZ - 1), 0)

    def over(self, slot, d, have, **at):
        part = self.part(have, **at)
        return self.copy(part, part, slot, self.net.across(d))

    def sibling(self):
        part = self.region(None, self.net.c, None, None)
        return self.copy(part, part, 3, self.net.across("c"), self.mate)

    def stages(self):
        first, d2, d3 = self.order

        def start_a():
            self.lines_start("")

        def start_b():
            self.lines_wait("")
            self.over(1, d2, "z").start()
            self.over(2, d3, "z").start()

        def start_c():
            self.over(1, d2, "z").wait_recv()
            self.over(2, d3, "z", **self.flip(d2)).start()

        def start_d():
            self.wait_for(self.part(d2 + "z", **self.flip(d3)), 2)
            self.sibling().start()

        def start_e():
            self.sibling().wait_recv()

        if first == "z":
            return dict(a=start_a, b=start_b, c=start_c, d=start_d, e=start_e)

        def begin_a():
            self.over(1, first, "").start()

        def begin_b():
            self.over(1, first, "").wait_recv()
            self.lines_start(first)

        def begin_c():
            self.lines_wait(first)
            self.over(2, d3, first + "z").start()

        def begin_d():
            self.wait_for(self.part(first + "z", **self.flip(d3)), 2)
            self.sibling().start()

        return dict(a=begin_a, b=begin_b, c=begin_c, d=begin_d, e=start_e)


class Scatter(Way):
    def __init__(self, net, region, order, sems, first, third, line):
        super().__init__(net, region, order, sems)
        self.into_first, self.into_third, self.into_line = first, third, line
        self.inner = order[0] != "z"
        self.near = order[0] if self.inner else order[1]
        self.far = order[2]
        self.rest = self.near + "z" if self.inner else "z"

    def sibling(self, core):
        part = self.region(None, core, None, None)
        return self.copy(part, part, 4, self.net.across("c"), self.mate)

    def sibling_out(self):
        return self.sibling(1 - self.net.c)

    def sibling_in(self):
        return self.sibling(self.net.c)

    def first(self):
        if self.inner:
            return self.copy(self.part(self.rest, **self.flip(self.far)), self.into_first, 0, self.net.across(self.far))
        part = self.part("z", **self.flip(self.far, self.near))
        return self.copy(part, self.into_first.at[0], 0, self.net.across(self.far))

    def second(self):
        part = self.part("z", **self.flip(self.far))
        return self.copy(part, self.into_first.at[1], 1, self.net.across(self.far))

    def third(self):
        part = self.part("" if self.inner else "z", **self.flip(self.near))
        return self.copy(part, self.into_third, 2, self.net.across(self.near))

    def along(self, k):
        ahead = self.ahead(k)
        part = self.part(self.near if self.inner else "", z=ahead)
        return self.copy(part, self.into_line.at[k - 1], 3, self.net.dev(z=ahead))

    @staticmethod
    def add(part, *came):
        total = part[...].astype(jnp.float32)
        for one in came:
            total = total + one[...].astype(jnp.float32)
        part[...] = total.astype(part.dtype)

    def lines_start(self):
        for k in range(1, NZ):
            self.along(k).start()

    def lines_wait(self):
        self.wait_for(self.into_line, 3)
        return [self.into_line.at[k] for k in range(NZ - 1)]

    def spread(self):
        self.first().start()
        if not self.inner:
            self.second().start()

    def fold_first(self):
        self.first().wait_recv()
        if self.inner:
            self.add(self.part(self.rest), self.into_first)
            self.lines_start()
        else:
            self.add(self.part("z", **self.flip(self.near)), self.into_first.at[0])
            self.third().start()

    def fold_second(self):
        if self.inner:
            self.add(self.part(self.near), *self.lines_wait())
            self.third().start()
        else:
            self.second().wait_recv()
            self.add(self.part("z"), self.into_first.at[1])

    def fold_third(self):
        self.third().wait_recv()
        if not self.inner:
            self.add(self.part("z"), self.into_third)
            self.lines_start()

    def total(self):
        came = [self.into_third] if self.inner else self.lines_wait()
        out = self.part()[...].astype(jnp.float32)
        for one in came:
            out = out + one[...].astype(jnp.float32)
        return out


def region_square(ref):
    pair, half = ref.shape[2] // NZ, ref.shape[3] // 2

    def region(y, c, z, x):
        rows = pl.ds(0, pair * NZ) if z is None else pl.ds(pl.multiple_of(z * pair, 16), pair)
        cols = pl.ds(0, half * 2) if x is None else pl.ds(pl.multiple_of(x * half, LANES), half)
        return ref.at[pl.ds(0, 2) if y is None else y, c, rows, cols]

    return region


def region_lead(ref, start, size):
    run = ref.shape[4] // 2

    def region(y, c, z, x):
        rows = pl.ds(0, 2 * run) if x is None else pl.ds(pl.multiple_of(x * run, 16), run)
        high, low = (pl.ds(0, 2), pl.ds(0, 2)) if z is None else (lax.div(z, 2), lax.rem(z, 2))
        return ref.at[pl.ds(0, 2) if y is None else y, c, high, low, rows, pl.ds(start, size)]

    return region


def region_small(ref):
    def region(y, c, z, x):
        return ref.at[pl.ds(0, 2) if y is None else y, c, pl.ds(0, NZ) if z is None else z, pl.ds(0, 2) if x is None else x]

    return region


def bulk_square(ref):
    pair, half = ref.shape[2] // NZ, ref.shape[3] // 2
    return lambda k: ref.at[pl.ds(0, k // 3), 0, pl.ds(0, 3 * pair), pl.ds(0, half)]


def bulk_lead(ref, start, size):
    rows = 3 * ref.shape[4] // 4
    return lambda k: ref.at[0, 0, pl.ds(0, k // 3), pl.ds(0, 2), pl.ds(0, rows), pl.ds(start, size)]


def bulk_small(ref):
    return lambda k: ref.at[0, 0, pl.ds(0, k), 0]


UNITS = range(13)
GATHER = ("zxy", "zyx", "zxy", "zyx", "yzx", "zxy", "xzy", "yzx", "zxy", "zxy", "yzx", "zyx", "zxy")
SCATTER = ("zyx", "zxy", "zxy", "yzx", "yzx", "zxy", "zxy", "zxy", "zxy", "yzx", "zxy", "xzy", "zxy")
OUTER = ((0, 256), (256, 256), (512, 128), (640, 128))


LANDING = ("first", "third", "line")


def landing_shapes(i, pair, half, run):
    order = SCATTER[i]
    if i < 8:
        piece, strip, wide = (pair, half), (pair * NZ, half), (pair * NZ, 2 * half)
        double = (pair, 2 * half)
    else:
        size = OUTER[i - 8][1]
        piece, strip, wide = (run, size), (2, 2, run, size), (2, 2, 2 * run, size)
        double = (2 * run, size)
    if order[0] == "z":
        return (2,) + strip, strip, (NZ - 1,) + piece
    if order[0] == "x":
        return wide, piece, (NZ - 1,) + double
    return (2,) + strip, piece, (NZ - 1, 2) + piece


def mm(left, right):
    return jnp.dot(left, right, preferred_element_type=jnp.float32)


def mm_nt(left, right):
    return lax.dot_general(left, right, (((1,), (1,)), ((), ())), preferred_element_type=jnp.float32)


def mm_tn(left, right):
    return lax.dot_general(left, right, (((0,), (0,)), ((), ())), preferred_element_type=jnp.float32)


def eights(block):
    return jnp.sum(block.reshape(block.shape[0] // 8, 8, block.shape[1]), axis=0)


STEP = 64
F32, BF16 = jnp.float32, jnp.bfloat16


def layer_kernel(names, *refs):
    r = SimpleNamespace(**dict(zip(names, refs, strict=True)))
    net = Net()
    frame_count, width = r.frames.shape
    half = width // 2
    lead = r.wq.shape[0]
    pair = 2 * lead
    own_rows = pl.ds(pl.multiple_of(net.z * pair, 16), pair)
    own_cols = pl.ds(pl.multiple_of(net.x * half, LANES), half)
    w8, w2 = r.w8, r.w2
    g2, e12 = r.g2, r.e12

    x_in = pltpu.make_async_copy(r.frames, r.xbuf, r.isem.at[0])
    g_in = pltpu.make_async_copy(r.grad_out, r.gbuf, r.isem.at[1])
    net.greet()
    x_in.start()
    g_in.start()

    gather, scatter = [], []
    for i in UNITS:
        cols = OUTER[i - 8] if 8 <= i < 12 else None
        if i < 8:
            region, bulk = region_square(w8.at[i]), bulk_square(w8.at[i])
            to = region_square(w2.at[i // 2, i % 2]) if i < 3 else region
        elif cols:
            region, bulk, to = region_lead(w2, *cols), bulk_lead(w2, *cols), region_lead(g2, *cols)
        else:
            region, bulk = region_small(r.small), bulk_small(r.small)
        kind = 0 if i < 8 else 1 if cols else 2
        sems = r.gout.at[kind], r.gmate.at[kind], r.grecv.at[i]
        gather.append(Gather(net, region, GATHER[i], sems, bulk).stages())
        if i < 12:
            landing = (getattr(r, f"{name}{i}") for name in LANDING)
            sems = r.sout.at[kind], r.smate.at[kind], r.srecv.at[i]
            scatter.append(Scatter(net, to, SCATTER[i], sems, *landing))

    def sent(ref, sem):
        pltpu.make_async_remote_copy(
            src_ref=ref, dst_ref=ref, send_sem=sem, recv_sem=r.grecv.at[0, 0], device_id=net.across("c"),
            device_id_type=MESH).wait_send()

    def all_sent(out, mate):
        runs = frame_count - 2 * 16
        sent(e12.at[pl.ds(0, 12), pl.ds(0, runs), pl.ds(0, half)], out.at[0])
        sent(r.act.at[pl.ds(0, 3), pl.ds(0, runs), :], out.at[1])
        sent(w8.at[:, :, 0], mate.at[0])
        sent(w2.at[:, 0], mate.at[1])

    def shard(u):
        if u < 4:
            return (r.wq, r.wk, r.wv, r.wo)[u][...]
        return r.wi[:, (u - 4) * width:(u - 3) * width]

    def swap(u):
        return pltpu.make_async_remote_copy(
            src_ref=r.xs.at[u], dst_ref=r.xr.at[u], send_sem=r.xss.at[0], recv_sem=r.xrs.at[u],
            device_id=net.across("x"), device_id_type=MESH)

    def offer(u):
        v = shard(u).astype(F32)
        theirs = jnp.where(net.x == 0, v[:, half:], v[:, :half])
        r.xs[u] = jnp.concatenate([theirs, jnp.zeros((8, half), F32)], axis=0).astype(BF16)

    def merge(u):
        swap(u).wait_recv()
        v = shard(u).astype(F32)
        mine = jnp.where(net.x == 0, v[:, :half], v[:, half:])
        came = r.xr[u].astype(F32)[:lead]
        first, second = jnp.where(net.x == 0, mine, came), jnp.where(net.x == 0, came, mine)
        w8[u, net.y, net.c, own_rows, own_cols] = jnp.concatenate([first, second], axis=0).astype(BF16)

    def place():
        for k in range(8):
            offer(k)
        pack = r.pack
        pack[...] = jnp.zeros_like(pack)
        for row, one in enumerate((r.bq, None, r.bv, r.bo, r.g1, r.s1, r.b2, r.gg2, r.s2, r.bi1)):
            if one is not None:
                size = one.shape[0]
                pack[row:row + 1, :size] = one[...].astype(F32).reshape(1, size)
        r.small[net.y, net.c, net.z, net.x] = pack[...].astype(BF16)
        w2[net.y, net.c, lax.div(net.z, 2), lax.rem(net.z, 2), pl.ds(pl.multiple_of(net.x * 4 * lead, 16), 4 * lead), :] = (
            r.wouter[...])
        masks()
        turn()
        net.meet()
        for k in range(8):
            swap(k).start()

    l0 = r.lengths[0, 0]
    l1 = l0 + r.lengths[0, 1]
    vec, bi, gsm, cs = r.vec, r.bi, r.gsm, r.cs
    fa, q3 = r.fa, r.q3
    act, gp, act_t = r.act, r.gp, r.act_t

    def loop(body, step=STEP, total=frame_count):
        def one(i, carry):
            body(pl.ds(pl.multiple_of(i * step, step), step))
            return carry

        lax.fori_loop(0, total // step, one, 0)

    def groups(shape, dim, start=0):
        place = lax.broadcasted_iota(jnp.int32, shape, dim) + start
        return (place >= l0).astype(jnp.int32) + (place >= l1).astype(jnp.int32)

    def masks():
        shape = (frame_count, LANES)
        lane = lax.broadcasted_iota(jnp.int32, shape, 1)
        group = groups(shape, 0)
        for e in range(2):
            spare = lane - (1 - e) * (LANES // 2)
            inside = (spare >= 0) & (spare < 3)
            r.mq[e] = jnp.where(inside & (spare != group), -1e30, 0.0).astype(BF16)
            r.mk[e] = jnp.where(inside & (spare == group), 1.0, 0.0).astype(BF16)

    def vectors():
        got = r.small[...].reshape(32 * 16, LANES)
        lane = lax.broadcasted_iota(jnp.int32, (LANES, width), 0)
        col = lax.broadcasted_iota(jnp.int32, (LANES, width), 1)
        tile = jnp.where((lane < lead) & (lane == lax.rem(col, lead)), 1.0, 0.0).astype(BF16)
        wide = mm(got, tile).reshape(32, 16, width)
        owner = lax.broadcasted_iota(jnp.int32, wide.shape, 0)
        place = lax.div(lax.broadcasted_iota(jnp.int32, wide.shape, 2), lead)
        vec[...] = jnp.sum(jnp.where(owner == place, wide, 0.0), axis=0)
        inner = got.astype(F32).reshape(32, 16, LANES)[:, 9, :].astype(BF16)
        for c in range(4):
            lane = lax.broadcasted_iota(jnp.int32, (LANES, width), 0)
            col = lax.broadcasted_iota(jnp.int32, (LANES, width), 1) + c * width
            tile = jnp.where((lane < 4 * lead) & (lane == lax.rem(col, 4 * lead)), 1.0, 0.0).astype(BF16)
            wide = mm(inner, tile)
            owner = lax.broadcasted_iota(jnp.int32, wide.shape, 0)
            place = lax.div(lax.broadcasted_iota(jnp.int32, wide.shape, 1) + c * width, 4 * lead)
            bi[c] = jnp.sum(jnp.where(owner == place, wide, 0.0), axis=0, keepdims=True)

    def square(u):
        return w8[u].reshape(width, width)

    def project(u):
        rows = mm(r.xbuf[...], square(u)) + vec[pl.ds(u, 1), :]
        q3[u] = (rows * jnp.where(u == 0, 0.125, 1.0)).astype(BF16)

    def head_lanes(shape, e):
        return lax.div(lax.broadcasted_iota(jnp.int32, shape, 1), LANES // 2) == e

    ROWS = 256

    def attend(p):
        cols = pl.ds(pl.multiple_of(p * LANES, LANES), LANES)
        sides = []
        for e in range(2):
            mine = head_lanes((frame_count, LANES), e)
            keys = jnp.where(mine, q3[1, :, cols], r.mk[e])
            vals = jnp.where(mine, q3[2, :, cols], jnp.ones((), BF16))
            sides.append((keys, vals))
        for i in range(frame_count // ROWS):
            rows = pl.ds(i * ROWS, ROWS)
            outs = []
            for e in range(2):
                keys, vals = sides[e]
                mine = head_lanes((ROWS, LANES), e)
                query = jnp.where(mine, q3[0, rows, cols], r.mq[e, rows, :])
                scores = mm_nt(query, keys)
                top = jnp.max(scores, axis=1, keepdims=True)
                weights = jnp.exp(scores - top).astype(BF16)
                e12[2 * p + e, rows, :] = weights
                outs.append(mm(weights, vals))
            low = head_lanes((ROWS, LANES), 0)
            over = jnp.where(low, outs[0], outs[1])
            under = pltpu.roll(jnp.where(low, outs[1], outs[0]), LANES // 2, 1)
            inverse = 1.0 / under
            r.linv[rows, cols] = inverse
            r.ctx[rows, cols] = (over * inverse).astype(BF16)

    def norm_one():
        fa[...] = mm(r.ctx[...], square(3))
        r.ctx_t[...] = jnp.transpose(r.ctx[...]).reshape(r.ctx_t.shape)

        def body(rows):
            v = r.xbuf[rows, :].astype(F32) + fa[rows, :] + vec[3:4, :]
            center = v - jnp.mean(v, axis=1, keepdims=True)
            scale = lax.rsqrt(jnp.mean(center * center, axis=1, keepdims=True) + 1e-05)
            normed = center * scale
            r.n1[rows, :] = normed
            r.r1[rows, :] = jnp.broadcast_to(scale, (STEP, LANES))
            r.low[rows, :] = (normed * vec[4:5, :] + vec[5:6, :]).astype(BF16)

        loop(body)
        r.hid_t[...] = jnp.transpose(r.low[...]).reshape(r.hid_t.shape)

    def feed(c):
        fa[...] = mm(r.low[...], square(4 + c))

        def body(rows):
            v = fa[rows, :] + bi[c]
            phi = 0.5 + 0.5 * lax.erf(v * 0.7071067811865476)
            bell = jnp.exp(v * v * -0.5) * 0.3989422804014327
            act[c, rows, :] = (v * phi).astype(BF16)
            gp[c, rows, :] = (phi + v * bell).astype(BF16)

        loop(body, 32)
        act_t[lax.div(c, 2), lax.rem(c, 2)] = jnp.transpose(act[c])

    def block(ref, c):
        return ref[lax.div(c, 2), lax.rem(c, 2)].reshape(width, width)

    def feed_out(k):
        start, size = OUTER[k]
        cols = slice(start, start + size)
        total = None
        for c in range(4):
            one = mm(act[c], w2[c // 2, c % 2, :, :, :, cols].reshape(width, size))
            total = one if total is None else total + one
        fa[:, cols] = total

    def fold(slot, row):
        gsm[pl.ds(row, 1), :] = jnp.sum(cs[slot], axis=0, keepdims=True)

    def norm_two():
        g_in.wait()
        cs[...] = jnp.zeros_like(cs)

        def body(rows):
            hidden = r.n1[rows, :] * vec[4:5, :] + vec[5:6, :]
            v = hidden + fa[rows, :] + vec[6:7, :]
            center = v - jnp.mean(v, axis=1, keepdims=True)
            scale = lax.rsqrt(jnp.mean(center * center, axis=1, keepdims=True) + 1e-05)
            normed = center * scale
            place = lax.broadcasted_iota(jnp.int32, normed.shape, 0) + rows.start
            live = jnp.where(place < l1, 1.0, 0.0)
            r.xbuf[rows, :] = ((normed * vec[7:8, :] + vec[8:9, :]) * live).astype(BF16)
            top = r.gbuf[rows, :].astype(F32) * live
            e = top * vec[7:8, :]
            d = e - jnp.mean(e, axis=1, keepdims=True) - normed * jnp.mean(e * normed, axis=1, keepdims=True)
            d = d * scale
            r.d2[rows, :] = d
            low = d.astype(BF16)
            r.low[rows, :] = low
            cs[0] += eights(top * normed)
            cs[1] += eights(top)
            cs[2] += eights(low.astype(F32))

        loop(body)
        fold(0, 7)
        fold(1, 8)
        fold(2, 6)

    layer_out = pltpu.make_async_copy(r.xbuf, r.layer_out, r.isem.at[0])
    frames_out = pltpu.make_async_copy(r.gbuf, r.frames_grad, r.isem.at[1])

    def back_feed(c):
        fa[...] = mm_nt(r.low[...], block(w2, c))
        cs[0] = jnp.zeros_like(cs[0])

        def body(rows):
            low = (fa[rows, :] * gp[c, rows, :].astype(F32)).astype(BF16)
            gp[c, rows, :] = low
            cs[0] += eights(low.astype(F32))

        loop(body)
        fold(0, 9 + c)

    def grad_square(u, left, right, own):
        core = net.c if own else 1 - net.c
        to = w2.at[u // 2, u % 2] if u < 3 else w8.at[u]
        rows = mm(left[:, core].reshape(2 * pair * NZ, frame_count), right()).reshape(2, pair * NZ, width)
        if own:
            scatter[u].sibling_in().wait_recv()
            rows = rows + to[:, core].astype(F32)
        to[:, core] = rows.astype(BF16)

    def grad_outer(i, own):
        core = net.c if own else 1 - net.c
        start, size = OUTER[i - 8]
        cols = pl.ds(start, size)
        left = act_t[:, core].reshape(2 * width, frame_count)
        rows = mm(left, r.low[:, cols]).reshape((2,) + g2.shape[2:5] + (size,))
        if own:
            scatter[i].sibling_in().wait_recv()
            rows = rows + g2[:, core, :, :, :, cols].astype(F32)
        g2[:, core, :, :, :, cols] = rows.astype(BF16)

    def back_hidden(c):
        got = mm_nt(gp[c], square(4 + c))

        @pl.when(c == 0)
        def _():
            fa[...] = got

        @pl.when(c > 0)
        def _():
            fa[...] += got

    def back_norm_one():
        cs[...] = jnp.zeros_like(cs)

        def body(rows):
            d = r.d2[rows, :] + fa[rows, :]
            normed = r.n1[rows, :]
            e = d * vec[4:5, :]
            cs[0] += eights(d * normed)
            cs[1] += eights(d)
            d = e - jnp.mean(e, axis=1, keepdims=True) - normed * jnp.mean(e * normed, axis=1, keepdims=True)
            d = d * r.r1[rows, 0:1]
            r.d2[rows, :] = d
            low = d.astype(BF16)
            r.low[rows, :] = low
            cs[2] += eights(low.astype(F32))

        loop(body)
        fold(0, 4)
        fold(1, 5)
        fold(2, 3)

    def back_context():
        act[3] = mm_nt(r.low[...], square(3)).astype(BF16)

    def back_attend(p):
        cols = pl.ds(pl.multiple_of(p * LANES, LANES), LANES)
        shape = (frame_count, LANES)
        low = head_lanes(shape, 0)
        scaled = (act[3, :, cols].astype(F32) * r.linv[:, cols]).astype(BF16)
        product = scaled.astype(F32) * r.ctx[:, cols].astype(F32)
        lane = lax.broadcasted_iota(jnp.int32, shape, 1)
        k2, v2, q2 = q3[1, :, cols], q3[2, :, cols], q3[0, :, cols]
        dq, dk, dv = [], [], []
        for e in range(2):
            mine = head_lanes(shape, e)
            spare = lane - (1 - e) * (LANES // 2)
            dot = jnp.sum(jnp.where(mine, product, 0.0), axis=1, keepdims=True)
            high = dot.astype(BF16).astype(F32)
            extra = jnp.where(spare == 0, high, jnp.where(spare == 1, dot - high, 0.0)).astype(BF16)
            left = jnp.where(mine, scaled, extra)
            minus = jnp.where((spare == 0) | (spare == 1), -1.0, 0.0).astype(BF16)
            right = jnp.where(mine, v2, minus)
            for i in range(frame_count // ROWS):
                part = slice(i * ROWS, (i + 1) * ROWS)
                r.ds[e, part, :] = (e12[2 * p + e, part, :].astype(F32) * mm_nt(left[part], right)).astype(BF16)
            dq.append(mm(r.ds[e], k2))
            dk.append(mm_tn(r.ds[e], q2))
            dv.append(mm_tn(e12[2 * p + e], scaled))
        act[0, :, cols] = (jnp.where(low, dq[0], dq[1]) * 0.125).astype(BF16)
        act[1, :, cols] = jnp.where(low, dk[0], dk[1]).astype(BF16)
        act[2, :, cols] = jnp.where(low, dv[0], dv[1]).astype(BF16)

    def bias_sums():
        cs[...] = jnp.zeros_like(cs)

        def body(rows):
            cs[0] += eights(act[0, rows, :].astype(F32))
            cs[1] += eights(act[2, rows, :].astype(F32))

        loop(body)
        fold(0, 0)
        fold(1, 2)
        gsm[1:2, :] = jnp.zeros((1, width), F32)
        gsm[13:16, :] = jnp.zeros((3, width), F32)

    def back_frames(k):
        r.d2[...] += mm_nt(act[k], square(k))

    def frames_ready():
        layer_out.wait()

        def body(rows):
            r.gbuf[rows, :] = r.d2[rows, :].astype(BF16)

        loop(body)
        frames_out.start()

    def small_copy(k, device):
        return pltpu.make_async_remote_copy(
            src_ref=r.sm.at[k], dst_ref=r.sl.at[k], send_sem=r.sms.at[0], recv_sem=r.smr.at[k],
            device_id=device, device_id_type=MESH)

    def small_step(k):
        if k == 0:
            r.sm[0] = gsm[...]
        else:
            r.sm[k] = r.sm[k - 1] + r.sl[k - 1]
        if k < 3:
            small_copy(k, net.across("cyx"[k])).start()

    def small_wait(k):
        small_copy(k, net.across("cyx"[k])).wait_recv()

    def small_line(k):
        return pltpu.make_async_remote_copy(
            src_ref=r.sm.at[3], dst_ref=r.sl.at[2 + k], send_sem=r.sms.at[0], recv_sem=r.smr.at[3],
            device_id=net.dev(z=lax.rem(net.z + k, NZ)), device_id_type=MESH)

    def small_total():
        landed = r.sl.at[pl.ds(3, NZ - 1)]
        pltpu.make_async_remote_copy(
            src_ref=landed, dst_ref=landed, send_sem=r.sms.at[0], recv_sem=r.smr.at[3], device_id=net.across("c"),
            device_id_type=MESH).wait_recv()
        whole = r.sm[3] + r.sl[3] + r.sl[4] + r.sl[5]
        index = (net.y * 2 + net.c) * 2 * NZ + net.z * 2 + net.x
        turned = pltpu.roll(whole, lax.rem(width - index * lead, width), 1)
        row = lax.broadcasted_iota(jnp.int32, (16, width), 0)
        block = lax.div(index, 8)
        inner = jnp.sum(jnp.where(row == 9 + block, whole, 0.0), axis=0, keepdims=True)
        inner = pltpu.roll(jnp.broadcast_to(inner, (8, width)), lax.rem(width - lax.rem(index, 8) * 4 * lead, width), 1)
        r.gsmall[0:8, :] = turned[0:8, :LANES]
        r.gsmall[8:16, :] = jnp.where(row[:8, :LANES] == 0, turned[8:9, :LANES], inner[:, :LANES])

    def swap_back(u):
        return pltpu.make_async_remote_copy(
            src_ref=r.ys.at[u], dst_ref=r.yr.at[u], send_sem=r.yss.at[0], recv_sem=r.yrs.at[0],
            device_id=net.across("x"), device_id_type=MESH)

    def out_of(u):
        if u < 4:
            return (r.gwq, r.gwk, r.gwv, r.gwo)[u], 0
        return r.gwi, (u - 4) * width

    def total_square(u):
        r.f8[...] = scatter[u].total()
        out, start = out_of(u)
        mine, theirs = pl.multiple_of(net.x * lead, 8), pl.multiple_of((1 - net.x) * lead, 8)
        r.ys[u] = jnp.concatenate([r.f8[pl.ds(theirs, lead), :], jnp.zeros((8, half), F32)], axis=0).astype(BF16)
        swap_back(u).start()
        out[:, pl.ds(pl.multiple_of(start + net.x * half, LANES), half)] = r.f8[pl.ds(mine, lead), :]

    def last():
        pltpu.make_async_remote_copy(
            src_ref=r.ys, dst_ref=r.yr, send_sem=r.yss.at[0], recv_sem=r.yrs.at[0], device_id=net.across("x"),
            device_id_type=MESH).wait_recv()
        for u in range(8):
            out, start = out_of(u)
            out[:, pl.ds(pl.multiple_of(start + (1 - net.x) * half, LANES), half)] = r.yr[u].astype(F32)[:lead]

    def total_outer(i):
        r.gwouter[:, pl.ds(*OUTER[i - 8])] = scatter[i].total()

    def unit(i, left=None, right=None):
        steps = SimpleNamespace(**gather[i])
        if i == len(UNITS) - 1:
            return steps
        way, square = scatter[i], i < 8

        def half_of(own):
            if square:
                grad_square(i, left, right, own)
            else:
                grad_outer(i, own)

        def away():
            half_of(False)
            way.sibling_out().start()

        def home():
            half_of(True)
            way.spread()

        steps.away, steps.home = away, home
        steps.t, steps.u, steps.v = way.fold_first, way.fold_second, way.fold_third
        if square:
            steps.p = functools.partial(merge, i)
            steps.x = functools.partial(total_square, i)
        else:
            steps.x = functools.partial(total_outer, i)
        return steps

    def give(k):
        pl.semaphore_signal(r.free.at[k], inc=1, device_id=net.across("c"), device_id_type=MESH)

    def take(k):
        pl.semaphore_wait(r.free.at[k], 1)

    def turn():
        x_in.wait()
        r.xt[...] = jnp.transpose(r.xbuf[...]).reshape(r.xt.shape)

    def gather_end():
        all_sent(r.gout, r.gmate)
        sent(e12.at[0, pl.ds(0, 15 * 16), pl.ds(0, LANES)], r.gout.at[2])
        sent(r.small.at[:, 0], r.gmate.at[2])

    def small(k):
        if k > 0:
            small_wait(k - 1)
        small_step(k)
        if k == 3:
            for one in range(1, NZ):
                small_line(one).start()

    def end():
        all_sent(r.sout, r.smate)
        sent(r.xs, r.xss.at[0])
        sent(r.ys, r.yss.at[0])
        sent(r.sl, r.sms.at[0])
        frames_out.wait()

    def rolled(count, body):
        def one(i, carry):
            body(i)
            return carry

        lax.fori_loop(0, count, one, 0)

    def go(*steps):
        for step in steps:
            step()

    q, k, v = (unit(u, r.xt, lambda u=u: act[u]) for u in range(3))
    o = unit(3, r.ctx_t, lambda: r.low[...])
    i0, i1, i2, i3 = (unit(4 + u, r.hid_t, lambda u=u: gp[u]) for u in range(4))
    w0, w1, w2_, w3 = (unit(8 + u) for u in range(4))
    s = unit(12)
    place()
    go(s.a, w3.a, q.p, q.a, w2_.a, s.b, i1.p, k.p, k.a, i0.p, i0.a, v.p)
    go(w3.b, i2.p, i2.a, s.c, i3.p, i3.a, v.a, o.p, o.a, i1.a, q.b, w0.a)
    go(w3.c, s.d, k.b, s.e, q.c, v.b)
    vectors()
    go(w1.a, k.c, v.c, q.d, o.b, k.d, i1.b, v.d, q.e, i0.b)

    def project_run(i):
        project(i)

        @pl.when(i == 0)
        def _():
            go(v.e, w0.b, o.c, i2.b, k.e)

        @pl.when(i == 1)
        def _():
            go(i3.b, w0.c, i1.c, i0.c)

    rolled(3, project_run)

    def attend_run(i):
        attend(i)

        @pl.when(i == 0)
        def _():
            go(o.d)

        @pl.when(i == 1)
        def _():
            go(w3.d, w0.d, w2_.b)

        @pl.when(i == 2)
        def _():
            go(i2.c, w1.b, i1.d, i0.d)

    rolled(6, attend_run)
    go(o.e, i1.e, w1.c, i3.c)
    norm_one()
    go(w0.e, i0.e)

    def feed_run(i):
        feed(i)

        @pl.when(i == 0)
        def _():
            go(i2.d, w2_.c)

        @pl.when(i == 1)
        def _():
            go(w3.e, i3.d, i2.e)

        @pl.when(i == 2)
        def _():
            go(w1.d, i3.e)

    rolled(4, feed_run)
    go(w2_.d)
    feed_out(3)
    feed_out(0)
    go(w1.e)
    feed_out(1)
    go(w2_.e)
    feed_out(2)
    norm_two()
    go(w3.away, w1.away, w0.away)
    gather_end()
    go(w2_.away, w3.home)

    def back_feed_run(i):
        back_feed(i)

        @pl.when(i == 0)
        def _():
            go(w1.home)

        @pl.when(i == 1)
        def _():
            go(w0.home)

    rolled(4, back_feed_run)
    go(w3.t)
    give(0)

    def back_hidden_run(i):
        back_hidden(i)

        @pl.when(i == 0)
        def _():
            take(0)

    rolled(4, back_hidden_run)
    give(1)
    take(1)
    go(i0.away, w1.t, w0.t, w2_.home, i2.away, i0.home)
    back_norm_one()
    back_context()
    give(2)
    go(i2.home, w0.u, i3.away, w0.v, i1.away)
    take(2)
    go(o.away, w2_.t)

    def back_attend_run(i):
        back_attend(i)

        @pl.when(i == 0)
        def _():
            go(i3.home, i2.t)

        @pl.when(i == 1)
        def _():
            go(i0.t, w2_.u, o.home)

        @pl.when(i == 3)
        def _():
            go(i1.home)

        @pl.when(i == 4)
        def _():
            go(w2_.v)

    rolled(6, back_attend_run)
    go(k.away)
    layer_out.start()
    go(v.away, i2.u, i3.t, i2.v)

    def back_frames_run(i):
        back_frames(i)

        @pl.when(i == 0)
        def _():
            go(k.home, o.t, i1.t, q.away, i3.u, i3.v, w0.x, k.t, v.home, i1.u, i1.v, q.home)
            bias_sums()
            go(v.t, q.t, k.u, k.v, w1.u, q.u, i3.x, o.u)
            small(0)
            go(i1.x, q.v)
            small(1)
            go(i2.x, w3.u, i0.u)

        @pl.when(i == 1)
        def _():
            go(w1.v, o.v, v.u, v.v)
            small(2)
            go(k.x)

    rolled(3, back_frames_run)
    frames_ready()
    small(3)
    go(q.x, w1.x, w3.v, o.x, i0.v, w3.x, v.x, w2_.x, i0.x)
    small_total()
    last()
    end()


def kernel_device(
    frames, lengths, query_weight, query_bias, key_weight, value_weight, value_bias, output_weight, output_bias,
    first_gain, first_shift, inner_weight, inner_bias, outer_weight, outer_bias, second_gain, second_shift, grad_out,
):
    count, width = frames.shape
    lead = query_weight.shape[0]
    pair, half = 2 * lead, width // 2
    vmem, hbm = pl.BlockSpec(memory_space=pltpu.VMEM), pl.BlockSpec(memory_space=pl.ANY)
    smem = pl.BlockSpec(memory_space=pltpu.SMEM)
    args = dict(
        frames=(hbm, frames), grad_out=(hbm, grad_out), lengths=(smem, lengths), wq=(vmem, query_weight),
        wk=(vmem, key_weight), wv=(vmem, value_weight), wo=(vmem, output_weight), wi=(vmem, inner_weight),
        wouter=(vmem, outer_weight), bq=(vmem, query_bias), bv=(vmem, value_bias), bo=(vmem, output_bias),
        g1=(vmem, first_gain), s1=(vmem, first_shift), b2=(vmem, outer_bias), gg2=(vmem, second_gain),
        s2=(vmem, second_shift), bi1=(vmem, inner_bias))
    shape = jax.ShapeDtypeStruct
    outs = dict(
        layer_out=(hbm, shape((count, width), BF16)), frames_grad=(hbm, shape((count, width), BF16)),
        gwq=(vmem, shape((lead, width), F32)), gwk=(vmem, shape((lead, width), F32)),
        gwv=(vmem, shape((lead, width), F32)), gwo=(vmem, shape((lead, width), F32)),
        gwi=(vmem, shape(inner_weight.shape, F32)), gwouter=(vmem, shape(outer_weight.shape, F32)),
        gsmall=(vmem, shape((16, LANES), F32)))
    dma = pltpu.SemaphoreType.DMA
    big = (count, width)
    square = (2, 2, pair * NZ, width)
    turned = (2, 2, pair * NZ, count)
    lead_shape = (2, 2, 2, 2, 8 * lead, width)
    scratch = dict(
        w8=((8,) + square, BF16), w2=(lead_shape, BF16), g2=(lead_shape, BF16), small=((2, 2, NZ, 2, 16, LANES), BF16),
        pack=((16, LANES), F32), xs=((8, lead + 8, half), BF16), xr=((8, lead + 8, half), BF16),
        ys=((8, lead + 8, half), BF16), yr=((8, lead + 8, half), BF16), xbuf=(big, BF16), gbuf=(big, BF16), q3=((3,) + big, BF16),
        e12=((HEADS, count, count), BF16), linv=(big, F32), ctx=(big, BF16), xt=(turned, BF16), ctx_t=(turned, BF16),
        hid_t=(turned, BF16), low=(big, BF16), n1=(big, F32), r1=((count, LANES), F32), act=((4,) + big, BF16),
        gp=((4,) + big, BF16), act_t=((2, 2, width, count), BF16), fa=(big, F32), d2=(big, F32),
        ds=((2, count, count), BF16), mq=((2, count, LANES), BF16), mk=((2, count, LANES), BF16), vec=((16, width), F32),
        bi=((4, 1, width), F32), gsm=((16, width), F32), cs=((3, 8, width), F32), sm=((4, 16, width), F32),
        sl=((6, 16, width), F32), f8=((pair, half), F32))
    for i in range(12):
        for kind, size in zip(LANDING, landing_shapes(i, pair, half, 4 * lead), strict=True):
            scratch[f"{kind}{i}"] = (size, BF16)
    scratch = {k: pltpu.VMEM(*v) for k, v in scratch.items()}
    scratch.update(
        gout=dma((3,)), gmate=dma((3,)), grecv=dma((13, 4)), sout=dma((2,)), smate=dma((2,)), srecv=dma((12, 5)),
        xss=dma((1,)), xrs=dma((8,)), yss=dma((1,)), yrs=dma((1,)), sms=dma((1,)), smr=dma((4,)), isem=dma((2,)), free=pltpu.SemaphoreType.REGULAR((3,)))
    got = pl.pallas_call(
        functools.partial(layer_kernel, (*args, *outs, *scratch)),
        out_shape=[o[1] for o in outs.values()],
        in_specs=[a[0] for a in args.values()],
        out_specs=[o[0] for o in outs.values()],
        scratch_shapes=list(scratch.values()),
        compiler_params=pltpu.CompilerParams(collective_id=0, has_side_effects=True, vmem_limit_bytes=VMEM_BYTES),
    )(*(a[1] for a in args.values()))

    bias, wide = shape((lead,), F32), shape((4 * lead,), F32)
    vectors = {3: bias, 6: bias, 8: bias, 9: bias, 10: bias, 12: wide, 14: bias, 15: bias, 16: bias}
    row_of = {3: 0, 6: 2, 8: 3, 9: 4, 10: 5, 12: 9, 14: 6, 15: 7, 16: 8}
    places = [i for i in range(17) if i not in vectors]

    def publish(*refs):
        came, small, out = refs[:8], refs[8], refs[9:]
        for a, i in zip(came, places, strict=True):
            out[i][...] = a[...]
        for i, row in row_of.items():
            size = vectors[i].shape[0]
            out[i][...] = small[row:row + 1, :size].reshape(size)

    whole = dict(zip(places, (o[1] for o in list(outs.values())[:8]), strict=True))
    return tuple(pl.pallas_call(
        publish,
        out_shape=[vectors[i] if i in vectors else whole[i] for i in range(17)],
        in_specs=[vmem] * 9,
        out_specs=[vmem] * 17,
    )(*got))


VMEM_BYTES = 63 << 20


def solution(mesh):
    split = P(("dp", "fsdp"))
    rows = P(("dp", "fsdp"), None)
    in_specs = (
        rows, rows, rows, split, rows, rows, split, rows, split, split, split, rows, split, rows, split, split, split, rows,
    )
    out_specs = (
        rows, rows, rows, split, rows, rows, split, rows, split, split, split, rows, split, rows, split, split, split,
    )
    fits = mesh.shape["dp"] == 4 and mesh.shape["fsdp"] == 2 * NZ

    def per_device(frames, lengths, query_weight, *rest):
        lead, width = query_weight.shape
        good = fits and lead % 8 == 0 and 4 * lead <= LANES and width == 768
        run = kernel_device if good else general_device
        return run(frames, lengths, query_weight, *rest)

    return jax.shard_map(per_device, mesh=mesh, in_specs=in_specs, out_specs=out_specs, check_vma=False)
```

```python
import functools
from types import SimpleNamespace

import jax
import jax.numpy as jnp
from jax import lax
from jax.experimental import pallas as pl
from jax.experimental.pallas import tpu as pltpu
from jax.sharding import PartitionSpec as P

HEADS = 12


def layer_norm(values, gain_vec, shift_vec):
    center = values - jnp.mean(values, axis=-1, keepdims=True)
    spread = jnp.mean(center * center, axis=-1, keepdims=True)
    return center * lax.rsqrt(spread + 1e-05) * gain_vec + shift_vec


def exact_gelu(values):
    return jax.nn.gelu(values, approximate=False)


def matmul(left_side, right_side):
    return jnp.dot(left_side, right_side, preferred_element_type=jnp.float32)


def matmul_tn(left_side, right_side):
    return lax.dot_general(
        left_side, right_side, (((0,), (0,)), ((), ())), preferred_element_type=jnp.float32
    )


def matmul_nt(left_side, right_side):
    return lax.dot_general(
        left_side, right_side, (((1,), (1,)), ((), ())), preferred_element_type=jnp.float32
    )


def column_sums(values):
    return jnp.sum(values.astype(jnp.float32), axis=0)


def block_scores(query_block, key_heads, group_block, groups, score_scale):
    raw_scores = (
        jnp.einsum("qhd,khd->hqk", query_block, key_heads, preferred_element_type=jnp.float32)
        * score_scale
    )
    allowed = group_block[:, None] == groups[None, :]
    return jnp.where(allowed[None], raw_scores, -1e30)


def general_device(
    frames,
    lengths,
    query_weight,
    query_bias,
    key_weight,
    value_weight,
    value_bias,
    output_weight,
    output_bias,
    first_gain,
    first_shift,
    inner_weight,
    inner_bias,
    outer_weight,
    outer_bias,
    second_gain,
    second_shift,
    grad_out,
):
    frame_count = frames.shape[0]
    model_width = frames.shape[1]
    head_size = model_width // HEADS
    score_scale = head_size ** (-0.5)
    places = jnp.arange(frame_count, dtype=jnp.int32)
    bounds = jnp.stack([lengths[0, 0], lengths[0, 0] + lengths[0, 1]])
    groups = jnp.sum((places[:, None] >= bounds[None, :]).astype(jnp.int32), axis=1)
    live_mask = (places < bounds[-1]).astype(jnp.float32)
    gathered = (
        lax.all_gather(query_weight, ("dp", "fsdp"), axis=0, tiled=True),
        lax.all_gather(query_bias, ("dp", "fsdp"), axis=0, tiled=True),
        lax.all_gather(key_weight, ("dp", "fsdp"), axis=0, tiled=True),
        lax.all_gather(value_weight, ("dp", "fsdp"), axis=0, tiled=True),
        lax.all_gather(value_bias, ("dp", "fsdp"), axis=0, tiled=True),
        lax.all_gather(output_weight, ("dp", "fsdp"), axis=0, tiled=True),
        lax.all_gather(output_bias, ("dp", "fsdp"), axis=0, tiled=True),
        lax.all_gather(first_gain, ("dp", "fsdp"), axis=0, tiled=True),
        lax.all_gather(first_shift, ("dp", "fsdp"), axis=0, tiled=True),
        lax.all_gather(inner_weight, ("dp", "fsdp"), axis=0, tiled=True),
        lax.all_gather(inner_bias, ("dp", "fsdp"), axis=0, tiled=True),
        lax.all_gather(outer_weight, ("dp", "fsdp"), axis=0, tiled=True),
        lax.all_gather(outer_bias, ("dp", "fsdp"), axis=0, tiled=True),
        lax.all_gather(second_gain, ("dp", "fsdp"), axis=0, tiled=True),
        lax.all_gather(second_shift, ("dp", "fsdp"), axis=0, tiled=True),
    )
    (
        query_mat,
        query_vec,
        key_mat,
        value_mat,
        value_vec,
        output_mat,
        output_vec,
        first_scale,
        first_offset,
        inner_mat,
        inner_vec,
        outer_mat,
        outer_vec,
        second_scale,
        second_offset,
    ) = gathered
    query_rows = (matmul(frames, query_mat) + query_vec.astype(jnp.float32)).astype(jnp.bfloat16)
    key_rows = matmul(frames, key_mat).astype(jnp.bfloat16)
    value_rows = (matmul(frames, value_mat) + value_vec.astype(jnp.float32)).astype(jnp.bfloat16)
    query_heads = query_rows.reshape(frame_count, HEADS, head_size)
    key_heads = key_rows.reshape(frame_count, HEADS, head_size)
    value_heads = value_rows.reshape(frame_count, HEADS, head_size)
    scores = block_scores(query_heads, key_heads, groups, groups, score_scale)
    row_max = jnp.max(scores, axis=-1, keepdims=True)
    raw_weights = jnp.exp(scores - row_max)
    row_total = jnp.sum(raw_weights, axis=-1, keepdims=True)
    attn_prob = raw_weights / row_total
    log_totals = row_max + jnp.log(row_total)
    context_parts = jnp.einsum(
        "hqk,khd->qhd",
        attn_prob.astype(jnp.bfloat16),
        value_heads,
        preferred_element_type=jnp.float32,
    )
    context_rows = context_parts.reshape(frame_count, model_width).astype(jnp.bfloat16)
    frames_float = frames.astype(jnp.float32)
    resid_one = frames_float + matmul(context_rows, output_mat) + output_vec.astype(jnp.float32)
    hidden, first_pull = jax.vjp(
        layer_norm, resid_one, first_scale.astype(jnp.float32), first_offset.astype(jnp.float32)
    )
    hidden_low = hidden.astype(jnp.bfloat16)
    inner_pre = matmul(hidden_low, inner_mat) + inner_vec.astype(jnp.float32)
    active, gelu_pull = jax.vjp(exact_gelu, inner_pre)
    active_low = active.astype(jnp.bfloat16)
    outer_out = matmul(active_low, outer_mat) + outer_vec.astype(jnp.float32)
    normed_out, second_pull = jax.vjp(
        layer_norm,
        hidden + outer_out,
        second_scale.astype(jnp.float32),
        second_offset.astype(jnp.float32),
    )
    layer_out = (normed_out * live_mask[:, None]).astype(jnp.bfloat16)
    grad_top = grad_out.astype(jnp.float32) * live_mask[:, None]
    grad_two, second_gain_grad, second_shift_grad = second_pull(grad_top)
    grad_outer = grad_two.astype(jnp.bfloat16)
    outer_mat_grad = matmul_tn(active_low, grad_outer)
    outer_vec_grad = column_sums(grad_outer)
    (grad_inner,) = gelu_pull(matmul_nt(grad_outer, outer_mat))
    grad_inner_low = grad_inner.astype(jnp.bfloat16)
    inner_mat_grad = matmul_tn(hidden_low, grad_inner_low)
    inner_vec_grad = column_sums(grad_inner_low)
    grad_hidden = grad_two + matmul_nt(grad_inner_low, inner_mat)
    grad_one, first_gain_grad, first_shift_grad = first_pull(grad_hidden)
    grad_attn = grad_one.astype(jnp.bfloat16)
    output_mat_grad = matmul_tn(context_rows, grad_attn)
    output_vec_grad = column_sums(grad_attn)
    grad_context = (
        matmul_nt(grad_attn, output_mat).astype(jnp.bfloat16).reshape(frame_count, HEADS, head_size)
    )
    scores = block_scores(query_heads, key_heads, groups, groups, score_scale)
    attn_prob = jnp.exp(scores - log_totals)
    grad_prob = jnp.einsum(
        "qhd,khd->hqk", grad_context, value_heads, preferred_element_type=jnp.float32
    )
    inner_sum = jnp.sum(attn_prob * grad_prob, axis=-1, keepdims=True)
    grad_scores = (attn_prob * (grad_prob - inner_sum)).astype(jnp.bfloat16)
    query_grad_parts = (
        jnp.einsum("hqk,khd->qhd", grad_scores, key_heads, preferred_element_type=jnp.float32)
        * score_scale
    )
    key_grad_sum = (
        jnp.einsum("hqk,qhd->khd", grad_scores, query_heads, preferred_element_type=jnp.float32)
        * score_scale
    )
    value_grad_sum = jnp.einsum(
        "hqk,qhd->khd",
        attn_prob.astype(jnp.bfloat16),
        grad_context,
        preferred_element_type=jnp.float32,
    )
    grad_query = query_grad_parts.reshape(frame_count, model_width).astype(jnp.bfloat16)
    grad_key = key_grad_sum.reshape(frame_count, model_width).astype(jnp.bfloat16)
    grad_value = value_grad_sum.reshape(frame_count, model_width).astype(jnp.bfloat16)
    query_mat_grad = matmul_tn(frames, grad_query)
    query_vec_grad = column_sums(grad_query)
    key_mat_grad = matmul_tn(frames, grad_key)
    value_mat_grad = matmul_tn(frames, grad_value)
    value_vec_grad = column_sums(grad_value)
    frames_grad = (
        grad_one
        + matmul_nt(grad_query, query_mat)
        + matmul_nt(grad_key, key_mat)
        + matmul_nt(grad_value, value_mat)
    ).astype(jnp.bfloat16)
    shares = (
        lax.psum_scatter(query_mat_grad, ("dp", "fsdp"), scatter_dimension=0, tiled=True),
        lax.psum_scatter(query_vec_grad, ("dp", "fsdp"), scatter_dimension=0, tiled=True),
        lax.psum_scatter(key_mat_grad, ("dp", "fsdp"), scatter_dimension=0, tiled=True),
        lax.psum_scatter(value_mat_grad, ("dp", "fsdp"), scatter_dimension=0, tiled=True),
        lax.psum_scatter(value_vec_grad, ("dp", "fsdp"), scatter_dimension=0, tiled=True),
        lax.psum_scatter(output_mat_grad, ("dp", "fsdp"), scatter_dimension=0, tiled=True),
        lax.psum_scatter(output_vec_grad, ("dp", "fsdp"), scatter_dimension=0, tiled=True),
        lax.psum_scatter(first_gain_grad, ("dp", "fsdp"), scatter_dimension=0, tiled=True),
        lax.psum_scatter(first_shift_grad, ("dp", "fsdp"), scatter_dimension=0, tiled=True),
        lax.psum_scatter(inner_mat_grad, ("dp", "fsdp"), scatter_dimension=0, tiled=True),
        lax.psum_scatter(inner_vec_grad, ("dp", "fsdp"), scatter_dimension=0, tiled=True),
        lax.psum_scatter(outer_mat_grad, ("dp", "fsdp"), scatter_dimension=0, tiled=True),
        lax.psum_scatter(outer_vec_grad, ("dp", "fsdp"), scatter_dimension=0, tiled=True),
        lax.psum_scatter(second_gain_grad, ("dp", "fsdp"), scatter_dimension=0, tiled=True),
        lax.psum_scatter(second_shift_grad, ("dp", "fsdp"), scatter_dimension=0, tiled=True),
    )
    return (
        layer_out,
        frames_grad,
        shares[0],
        shares[1],
        shares[2],
        shares[3],
        shares[4],
        shares[5],
        shares[6],
        shares[7],
        shares[8],
        shares[9],
        shares[10],
        shares[11],
        shares[12],
        shares[13],
        shares[14],
    )


MESH = pl.DeviceIdType.MESH
NZ = 4
LANES = 128


class Net:
    def __init__(self):
        dp, fs = lax.axis_index("dp"), lax.axis_index("fsdp")
        self.y, self.c = lax.div(dp, 2), lax.rem(dp, 2)
        self.z, self.x = lax.div(fs, 2), lax.rem(fs, 2)

    def dev(self, y=None, c=None, z=None, x=None):
        y = self.y if y is None else y
        c = self.c if c is None else c
        z = self.z if z is None else z
        x = self.x if x is None else x
        return (y * 2 + c, z * 2 + x)

    def across(self, dim):
        if dim == "x":
            return self.dev(x=1 - self.x)
        if dim == "y":
            return self.dev(y=1 - self.y)
        return self.dev(c=1 - self.c)

    def greet(self):
        bar = pltpu.get_barrier_semaphore()

        def tell(device):
            pl.semaphore_signal(bar, inc=1, device_id=device, device_id_type=MESH)

        for dim in "xyc":
            tell(self.across(dim))
        for k in range(1, NZ):
            tell(self.dev(z=lax.rem(self.z + k, NZ)))

    def meet(self):
        pl.semaphore_wait(pltpu.get_barrier_semaphore(), 3 + NZ - 1)


class Way:
    def __init__(self, net, region, order, sems):
        self.net, self.region, self.order = net, region, order
        self.out, self.mate, self.recv = sems

    def copy(self, src, dst, slot, device, send=None):
        return pltpu.make_async_remote_copy(
            src_ref=src, dst_ref=dst, send_sem=self.out if send is None else send, recv_sem=self.recv.at[slot],
            device_id=device, device_id_type=MESH)

    def wait_for(self, ref, slot):
        self.copy(ref, ref, slot, self.net.across("c")).wait_recv()

    def part(self, have="", **at):
        n = self.net
        for d in "yzx":
            at.setdefault(d, None if d in have else getattr(n, d))
        return self.region(at["y"], n.c, at["z"], at["x"])

    def flip(self, *dims):
        return {d: 1 - getattr(self.net, d) for d in dims}

    def ahead(self, k):
        return lax.rem(self.net.z + k, NZ)


class Gather(Way):
    def __init__(self, net, region, order, sems, bulk, line_out):
        super().__init__(net, region, order, sems)
        self.bulk, self.line_out = bulk, line_out

    def lines_start(self, have):
        n = self.net
        part = self.part(have)
        inside = lax.rem(lax.div(n.z + 1, 2), 2)
        self.copy(part, part, 4 * (1 - inside), n.dev(z=self.ahead(2)), self.line_out).start()

        @pl.when(n.z < NZ - 1)
        def _():
            self.copy(part, part, 0, n.dev(z=n.z + 1), self.line_out).start()

        @pl.when(n.z > 0)
        def _():
            self.copy(part, part, 0, n.dev(z=n.z - 1), self.line_out).start()

    def lines_pass(self, have):
        n = self.net

        @pl.when((n.z > 0) & (n.z < NZ - 1))
        def _():
            part = self.part(have, z=(NZ - 1) * (2 - n.z))
            self.wait_for(part, 4)
            self.copy(part, part, 0, n.dev(z=(NZ - 1) * (n.z - 1)), self.line_out).start()

    def lines_wait(self, have):
        n = self.net
        times = 2 if have else 1

        @pl.when((n.z > 0) & (n.z < NZ - 1))
        def _():
            self.wait_for(self.bulk(times, 2), 0)

        @pl.when((n.z == 0) | (n.z == NZ - 1))
        def _():
            self.wait_for(self.bulk(times, 3), 0)

    def over(self, slot, d, have, **at):
        part = self.part(have, **at)
        return self.copy(part, part, slot, self.net.across(d))

    def sibling(self):
        part = self.region(None, self.net.c, None, None)
        return self.copy(part, part, 3, self.net.across("c"), self.mate)

    def stages(self):
        first, d2, d3 = self.order

        def spread():
            self.lines_wait("")
            self.over(1, d2, "z").start()
            self.over(2, d3, "z").start()

        def turn():
            self.over(1, d2, "z").wait_recv()
            self.over(2, d3, "z", **self.flip(d2)).start()

        def mate():
            self.wait_for(self.part((first + d2 if first == "z" else first + "z"), **self.flip(d3)), 2)
            self.sibling().start()

        def ready():
            self.sibling().wait_recv()

        if first == "z":
            start, onward = functools.partial(self.lines_start, ""), functools.partial(self.lines_pass, "")
            return dict(a=start, b=onward, c=spread, d=turn, e=mate, g=ready)

        def begin():
            self.over(1, first, "").start()

        def lines():
            self.over(1, first, "").wait_recv()
            self.lines_start(first)

        def cross():
            self.lines_wait(first)
            self.over(2, d3, first + "z").start()

        return dict(a=begin, b=lines, c=functools.partial(self.lines_pass, first), d=cross, e=mate, g=ready)


class Scatter(Way):
    def __init__(self, net, region, order, sems, first, third, line):
        super().__init__(net, region, order, sems)
        self.into_first, self.into_third, self.into_line = first, third, line
        self.inner = order[0] != "z"
        self.near = order[0] if self.inner else order[1]
        self.far = order[2]
        self.rest = self.near + "z" if self.inner else "z"

    def sibling(self, core):
        part = self.region(None, core, None, None)
        return self.copy(part, part, 4, self.net.across("c"), self.mate)

    def sibling_out(self):
        return self.sibling(1 - self.net.c)

    def sibling_in(self):
        return self.sibling(self.net.c)

    def first(self):
        if self.inner:
            return self.copy(self.part(self.rest, **self.flip(self.far)), self.into_first, 0, self.net.across(self.far))
        part = self.part("z", **self.flip(self.far, self.near))
        return self.copy(part, self.into_first.at[0], 0, self.net.across(self.far))

    def second(self):
        part = self.part("z", **self.flip(self.far))
        return self.copy(part, self.into_first.at[1], 1, self.net.across(self.far))

    def third(self):
        part = self.part("" if self.inner else "z", **self.flip(self.near))
        return self.copy(part, self.into_third, 2, self.net.across(self.near))

    def along(self, k):
        ahead = self.ahead(k)
        part = self.part(self.near if self.inner else "", z=ahead)
        return self.copy(part, self.into_line.at[k - 1], 3, self.net.dev(z=ahead))

    @staticmethod
    def add(part, *came):
        total = part[...].astype(jnp.float32)
        for one in came:
            total = total + one[...].astype(jnp.float32)
        part[...] = total.astype(part.dtype)

    def lines_start(self):
        for k in range(1, NZ):
            self.along(k).start()

    def lines_wait(self):
        self.wait_for(self.into_line, 3)
        return [self.into_line.at[k] for k in range(NZ - 1)]

    def spread(self):
        self.first().start()
        if not self.inner:
            self.second().start()

    def fold_first(self):
        self.first().wait_recv()
        if self.inner:
            self.add(self.part(self.rest), self.into_first)
            self.lines_start()
        else:
            self.add(self.part("z", **self.flip(self.near)), self.into_first.at[0])
            self.third().start()

    def fold_second(self):
        if self.inner:
            self.add(self.part(self.near), *self.lines_wait())
            self.third().start()
        else:
            self.second().wait_recv()
            self.add(self.part("z"), self.into_first.at[1])

    def fold_third(self):
        self.third().wait_recv()
        if not self.inner:
            self.add(self.part("z"), self.into_third)
            self.lines_start()

    def total(self):
        came = [self.into_third] if self.inner else self.lines_wait()
        out = self.part()[...].astype(jnp.float32)
        for one in came:
            out = out + one[...].astype(jnp.float32)
        return out


def region_square(ref):
    pair, half = ref.shape[2] // NZ, ref.shape[3] // 2

    def region(y, c, z, x):
        rows = pl.ds(0, pair * NZ) if z is None else pl.ds(pl.multiple_of(z * pair, 16), pair)
        cols = pl.ds(0, half * 2) if x is None else pl.ds(pl.multiple_of(x * half, LANES), half)
        return ref.at[pl.ds(0, 2) if y is None else y, c, rows, cols]

    return region


def region_lead(ref, start, size):
    run = ref.shape[4] // 2

    def region(y, c, z, x):
        rows = pl.ds(0, 2 * run) if x is None else pl.ds(pl.multiple_of(x * run, 16), run)
        high, low = (pl.ds(0, 2), pl.ds(0, 2)) if z is None else (lax.div(z, 2), lax.rem(z, 2))
        return ref.at[pl.ds(0, 2) if y is None else y, c, high, low, rows, pl.ds(start, size)]

    return region


def region_small(ref):
    def region(y, c, z, x):
        return ref.at[pl.ds(0, 2) if y is None else y, c, pl.ds(0, NZ) if z is None else z, pl.ds(0, 2) if x is None else x]

    return region


def bulk_square(ref):
    pair, half = ref.shape[2] // NZ, ref.shape[3] // 2
    return lambda times, k: ref.at[pl.ds(0, times), 0, pl.ds(0, k * pair), pl.ds(0, half)]


def bulk_lead(ref, start, size):
    run = ref.shape[4] // 2
    return lambda times, k: ref.at[0, 0, pl.ds(0, times), pl.ds(0, 2), pl.ds(0, k * run // 2), pl.ds(start, size)]


def bulk_small(ref):
    return lambda times, k: ref.at[0, 0, pl.ds(0, k), 0]


def stretch(ref, count, width):
    deep, tall, _ = ref.shape
    rows = count // width
    for a in range(deep, 0, -1):
        if rows % (16 * a) == 0 and rows // a <= tall:
            return ref.at[pl.ds(0, a), pl.ds(0, rows // a), pl.ds(0, width)]
    raise ValueError(count)


UNITS = range(13)
GATHER = ("zyx", "zxy", "zyx", "xzy", "zxy", "yzx", "zxy", "zyx", "xzy", "yzx", "zyx", "zxy", "zxy")
SCATTER = ("zyx", "zyx", "zxy", "zxy", "xzy", "yzx", "zyx", "zxy", "yzx", "zxy", "yzx", "xzy", "zxy")
OUTER = ((0, 256), (256, 256), (512, 128), (640, 128))


LANDING = ("first", "third", "line")


def landing_shapes(i, pair, half, run):
    order = SCATTER[i]
    if i < 8:
        piece, strip, wide = (pair, half), (pair * NZ, half), (pair * NZ, 2 * half)
        double = (pair, 2 * half)
    else:
        size = OUTER[i - 8][1]
        piece, strip, wide = (run, size), (2, 2, run, size), (2, 2, 2 * run, size)
        double = (2 * run, size)
    if order[0] == "z":
        return (2,) + strip, strip, (NZ - 1,) + piece
    if order[0] == "x":
        return wide, piece, (NZ - 1,) + double
    return (2,) + strip, piece, (NZ - 1, 2) + piece


def mm(left, right):
    return jnp.dot(left, right, preferred_element_type=jnp.float32)


def mm_nt(left, right):
    return lax.dot_general(left, right, (((1,), (1,)), ((), ())), preferred_element_type=jnp.float32)


def mm_tn(left, right):
    return lax.dot_general(left, right, (((0,), (0,)), ((), ())), preferred_element_type=jnp.float32)


def eights(block):
    return jnp.sum(block.reshape(block.shape[0] // 8, 8, block.shape[1]), axis=0)


STEP = 64
F32, BF16 = jnp.float32, jnp.bfloat16


def layer_kernel(names, *refs):
    r = SimpleNamespace(**dict(zip(names, refs, strict=True)))
    net = Net()
    frame_count, width = r.frames.shape
    half = width // 2
    lead = r.wq.shape[0]
    pair = 2 * lead
    own_rows = pl.ds(pl.multiple_of(net.z * pair, 16), pair)
    own_cols = pl.ds(pl.multiple_of(net.x * half, LANES), half)
    w8, w2 = r.w8, r.w2
    g2, e12 = r.g2, r.e12

    x_in = pltpu.make_async_copy(r.frames, r.xbuf, r.isem.at[0])
    g_in = pltpu.make_async_copy(r.grad_out, r.gbuf, r.isem.at[1])
    net.greet()
    x_in.start()
    g_in.start()

    gather, scatter = [], []
    for i in UNITS:
        cols = OUTER[i - 8] if 8 <= i < 12 else None
        if i < 8:
            region, bulk = region_square(w8.at[i]), bulk_square(w8.at[i])
            to = region_square(w2.at[i // 2, i % 2]) if i < 3 else region
        elif cols:
            region, bulk, to = region_lead(w2, *cols), bulk_lead(w2, *cols), region_lead(g2, *cols)
        else:
            region, bulk = region_small(r.small), bulk_small(r.small)
        kind = 0 if i < 8 else 1 if cols else 2
        sems = r.gout.at[kind], r.gmate.at[kind], r.grecv.at[i]
        gather.append(Gather(net, region, GATHER[i], sems, bulk, r.gline.at[kind]).stages())
        if i < 12:
            landing = (getattr(r, f"{name}{i}") for name in LANDING)
            sems = r.sout.at[kind], r.smate.at[kind], r.srecv.at[i]
            scatter.append(Scatter(net, to, SCATTER[i], sems, *landing))

    def sent(ref, sem):
        pltpu.make_async_remote_copy(
            src_ref=ref, dst_ref=ref, send_sem=sem, recv_sem=r.grecv.at[0, 0], device_id=net.across("c"),
            device_id_type=MESH).wait_send()

    def mates_sent(mate):
        sent(w8.at[:, :, 0], mate.at[0])
        sent(w2.at[:, 0], mate.at[1])

    def shard(u):
        if u < 4:
            return (r.wq, r.wk, r.wv, r.wo)[u][...]
        return r.wi[:, (u - 4) * width:(u - 3) * width]

    def swap(u):
        return pltpu.make_async_remote_copy(
            src_ref=r.xs.at[u], dst_ref=r.xr.at[u], send_sem=r.xss.at[0], recv_sem=r.xrs.at[u],
            device_id=net.across("x"), device_id_type=MESH)

    def offer(u):
        v = shard(u).astype(F32)
        theirs = jnp.where(net.x == 0, v[:, half:], v[:, :half])
        r.xs[u] = jnp.concatenate([theirs, jnp.zeros((8, half), F32)], axis=0).astype(BF16)

    def merge(u):
        swap(u).wait_recv()
        v = shard(u).astype(F32)
        mine = jnp.where(net.x == 0, v[:, :half], v[:, half:])
        came = r.xr[u].astype(F32)[:lead]
        first, second = jnp.where(net.x == 0, mine, came), jnp.where(net.x == 0, came, mine)
        w8[u, net.y, net.c, own_rows, own_cols] = jnp.concatenate([first, second], axis=0).astype(BF16)

    def place():
        for k in range(8):
            offer(k)
        pack = r.pack
        pack[...] = jnp.zeros_like(pack)
        for row, one in enumerate((r.bq, None, r.bv, r.bo, r.g1, r.s1, r.b2, r.gg2, r.s2, r.bi1)):
            if one is not None:
                size = one.shape[0]
                pack[row:row + 1, :size] = one[...].astype(F32).reshape(1, size)
        r.small[net.y, net.c, net.z, net.x] = pack[...].astype(BF16)
        w2[net.y, net.c, lax.div(net.z, 2), lax.rem(net.z, 2), pl.ds(pl.multiple_of(net.x * 4 * lead, 16), 4 * lead), :] = (
            r.wouter[...])
        masks()
        turn()
        net.meet()
        for k in range(8):
            swap(k).start()

    l0 = r.lengths[0, 0]
    l1 = l0 + r.lengths[0, 1]
    vec, bi, gsm, cs = r.vec, r.bi, r.gsm, r.cs
    fa, q3 = r.fa, r.q3
    act, gp, act_t = r.act, r.gp, r.act_t

    def loop(body, step=STEP, total=frame_count):
        def one(i, carry):
            body(pl.ds(pl.multiple_of(i * step, step), step))
            return carry

        lax.fori_loop(0, total // step, one, 0)

    def groups(shape, dim, start=0):
        place = lax.broadcasted_iota(jnp.int32, shape, dim) + start
        return (place >= l0).astype(jnp.int32) + (place >= l1).astype(jnp.int32)

    def masks():
        shape = (frame_count, LANES)
        lane = lax.broadcasted_iota(jnp.int32, shape, 1)
        group = groups(shape, 0)
        for e in range(2):
            spare = lane - (1 - e) * (LANES // 2)
            inside = (spare >= 0) & (spare < 3)
            r.mq[e] = jnp.where(inside & (spare != group), -1e30, 0.0).astype(BF16)
            r.mk[e] = jnp.where(inside & (spare == group), 1.0, 0.0).astype(BF16)

    def vectors():
        got = r.small[...].reshape(32 * 16, LANES)
        lane = lax.broadcasted_iota(jnp.int32, (LANES, width), 0)
        col = lax.broadcasted_iota(jnp.int32, (LANES, width), 1)
        tile = jnp.where((lane < lead) & (lane == lax.rem(col, lead)), 1.0, 0.0).astype(BF16)
        wide = mm(got, tile).reshape(32, 16, width)
        owner = lax.broadcasted_iota(jnp.int32, wide.shape, 0)
        place = lax.div(lax.broadcasted_iota(jnp.int32, wide.shape, 2), lead)
        vec[...] = jnp.sum(jnp.where(owner == place, wide, 0.0), axis=0)
        inner = got.astype(F32).reshape(32, 16, LANES)[:, 9, :].astype(BF16)
        for c in range(4):
            lane = lax.broadcasted_iota(jnp.int32, (LANES, width), 0)
            col = lax.broadcasted_iota(jnp.int32, (LANES, width), 1) + c * width
            tile = jnp.where((lane < 4 * lead) & (lane == lax.rem(col, 4 * lead)), 1.0, 0.0).astype(BF16)
            wide = mm(inner, tile)
            owner = lax.broadcasted_iota(jnp.int32, wide.shape, 0)
            place = lax.div(lax.broadcasted_iota(jnp.int32, wide.shape, 1) + c * width, 4 * lead)
            bi[c] = jnp.sum(jnp.where(owner == place, wide, 0.0), axis=0, keepdims=True)

    def square(u):
        return w8[u].reshape(width, width)

    def project(u):
        rows = mm(r.xbuf[...], square(u)) + vec[pl.ds(u, 1), :]
        q3[u] = (rows * jnp.where(u == 0, 0.125, 1.0)).astype(BF16)

    def head_lanes(shape, e):
        return lax.div(lax.broadcasted_iota(jnp.int32, shape, 1), LANES // 2) == e

    ROWS = 256

    def attend(p):
        cols = pl.ds(pl.multiple_of(p * LANES, LANES), LANES)
        sides = []
        for e in range(2):
            mine = head_lanes((frame_count, LANES), e)
            keys = jnp.where(mine, q3[1, :, cols], r.mk[e])
            vals = jnp.where(mine, q3[2, :, cols], jnp.ones((), BF16))
            sides.append((keys, vals))
        for i in range(frame_count // ROWS):
            rows = pl.ds(i * ROWS, ROWS)
            outs = []
            for e in range(2):
                keys, vals = sides[e]
                mine = head_lanes((ROWS, LANES), e)
                query = jnp.where(mine, q3[0, rows, cols], r.mq[e, rows, :])
                scores = mm_nt(query, keys)
                top = jnp.max(scores, axis=1, keepdims=True)
                weights = jnp.exp(scores - top).astype(BF16)
                e12[2 * p + e, rows, :] = weights
                outs.append(mm(weights, vals))
            low = head_lanes((ROWS, LANES), 0)
            over = jnp.where(low, outs[0], outs[1])
            under = pltpu.roll(jnp.where(low, outs[1], outs[0]), LANES // 2, 1)
            inverse = 1.0 / under
            r.linv[rows, cols] = inverse
            r.ctx[rows, cols] = (over * inverse).astype(BF16)

    def norm_one():
        fa[...] = mm(r.ctx[...], square(3))
        r.ctx_t[...] = jnp.transpose(r.ctx[...]).reshape(r.ctx_t.shape)

        def body(rows):
            v = r.xbuf[rows, :].astype(F32) + fa[rows, :] + vec[3:4, :]
            center = v - jnp.mean(v, axis=1, keepdims=True)
            scale = lax.rsqrt(jnp.mean(center * center, axis=1, keepdims=True) + 1e-05)
            normed = center * scale
            r.n1[rows, :] = normed
            r.r1[rows, :] = jnp.broadcast_to(scale, (STEP, LANES))
            r.low[rows, :] = (normed * vec[4:5, :] + vec[5:6, :]).astype(BF16)

        loop(body)
        r.hid_t[...] = jnp.transpose(r.low[...]).reshape(r.hid_t.shape)

    def feed(c):
        fa[...] = mm(r.low[...], square(4 + c))

        def body(rows):
            v = fa[rows, :] + bi[c]
            phi = 0.5 + 0.5 * lax.erf(v * 0.7071067811865476)
            bell = jnp.exp(v * v * -0.5) * 0.3989422804014327
            act[c, rows, :] = (v * phi).astype(BF16)
            gp[c, rows, :] = (phi + v * bell).astype(BF16)

        loop(body, 32)
        act_t[lax.div(c, 2), lax.rem(c, 2)] = jnp.transpose(act[c])

    def block(ref, c):
        return ref[lax.div(c, 2), lax.rem(c, 2)].reshape(width, width)

    def feed_out(k):
        start, size = OUTER[k]
        cols = slice(start, start + size)
        total = None
        for c in range(4):
            one = mm(act[c], w2[c // 2, c % 2, :, :, :, cols].reshape(width, size))
            total = one if total is None else total + one
        fa[:, cols] = total

    def fold(slot, row):
        gsm[pl.ds(row, 1), :] = jnp.sum(cs[slot], axis=0, keepdims=True)

    def norm_two():
        g_in.wait()
        cs[...] = jnp.zeros_like(cs)

        def body(rows):
            hidden = r.n1[rows, :] * vec[4:5, :] + vec[5:6, :]
            v = hidden + fa[rows, :] + vec[6:7, :]
            center = v - jnp.mean(v, axis=1, keepdims=True)
            scale = lax.rsqrt(jnp.mean(center * center, axis=1, keepdims=True) + 1e-05)
            normed = center * scale
            place = lax.broadcasted_iota(jnp.int32, normed.shape, 0) + rows.start
            live = jnp.where(place < l1, 1.0, 0.0)
            r.xbuf[rows, :] = ((normed * vec[7:8, :] + vec[8:9, :]) * live).astype(BF16)
            top = r.gbuf[rows, :].astype(F32) * live
            e = top * vec[7:8, :]
            d = e - jnp.mean(e, axis=1, keepdims=True) - normed * jnp.mean(e * normed, axis=1, keepdims=True)
            d = d * scale
            r.d2[rows, :] = d
            low = d.astype(BF16)
            r.low[rows, :] = low
            cs[0] += eights(top * normed)
            cs[1] += eights(top)
            cs[2] += eights(low.astype(F32))

        loop(body)
        fold(0, 7)
        fold(1, 8)
        fold(2, 6)

    layer_out = pltpu.make_async_copy(r.xbuf, r.layer_out, r.isem.at[0])
    frames_out = pltpu.make_async_copy(r.gbuf, r.frames_grad, r.isem.at[1])

    def back_feed(c):
        fa[...] = mm_nt(r.low[...], block(w2, c))
        cs[0] = jnp.zeros_like(cs[0])

        def body(rows):
            low = (fa[rows, :] * gp[c, rows, :].astype(F32)).astype(BF16)
            gp[c, rows, :] = low
            cs[0] += eights(low.astype(F32))

        loop(body)
        fold(0, 9 + c)

    def grad_square(u, left, right, own):
        core = net.c if own else 1 - net.c
        to = w2.at[u // 2, u % 2] if u < 3 else w8.at[u]
        rows = mm(left[:, core].reshape(2 * pair * NZ, frame_count), right()).reshape(2, pair * NZ, width)
        if own:
            scatter[u].sibling_in().wait_recv()
            rows = rows + to[:, core].astype(F32)
        to[:, core] = rows.astype(BF16)

    def grad_outer(i, own):
        core = net.c if own else 1 - net.c
        start, size = OUTER[i - 8]
        cols = pl.ds(start, size)
        left = act_t[:, core].reshape(2 * width, frame_count)
        rows = mm(left, r.low[:, cols]).reshape((2,) + g2.shape[2:5] + (size,))
        if own:
            scatter[i].sibling_in().wait_recv()
            rows = rows + g2[:, core, :, :, :, cols].astype(F32)
        g2[:, core, :, :, :, cols] = rows.astype(BF16)

    def back_hidden(c):
        got = mm_nt(gp[c], square(4 + c))

        @pl.when(c == 0)
        def _():
            fa[...] = got

        @pl.when(c > 0)
        def _():
            fa[...] += got

    def back_norm_one():
        cs[...] = jnp.zeros_like(cs)

        def body(rows):
            d = r.d2[rows, :] + fa[rows, :]
            normed = r.n1[rows, :]
            e = d * vec[4:5, :]
            cs[0] += eights(d * normed)
            cs[1] += eights(d)
            d = e - jnp.mean(e, axis=1, keepdims=True) - normed * jnp.mean(e * normed, axis=1, keepdims=True)
            d = d * r.r1[rows, 0:1]
            r.d2[rows, :] = d
            low = d.astype(BF16)
            r.low[rows, :] = low
            cs[2] += eights(low.astype(F32))

        loop(body)
        fold(0, 4)
        fold(1, 5)
        fold(2, 3)

    def back_context():
        act[3] = mm_nt(r.low[...], square(3)).astype(BF16)

    def back_attend(p):
        cols = pl.ds(pl.multiple_of(p * LANES, LANES), LANES)
        shape = (frame_count, LANES)
        low = head_lanes(shape, 0)
        scaled = (act[3, :, cols].astype(F32) * r.linv[:, cols]).astype(BF16)
        product = scaled.astype(F32) * r.ctx[:, cols].astype(F32)
        lane = lax.broadcasted_iota(jnp.int32, shape, 1)
        k2, v2, q2 = q3[1, :, cols], q3[2, :, cols], q3[0, :, cols]
        dq, dk, dv = [], [], []
        for e in range(2):
            mine = head_lanes(shape, e)
            spare = lane - (1 - e) * (LANES // 2)
            dot = jnp.sum(jnp.where(mine, product, 0.0), axis=1, keepdims=True)
            high = dot.astype(BF16).astype(F32)
            extra = jnp.where(spare == 0, high, jnp.where(spare == 1, dot - high, 0.0)).astype(BF16)
            left = jnp.where(mine, scaled, extra)
            minus = jnp.where((spare == 0) | (spare == 1), -1.0, 0.0).astype(BF16)
            right = jnp.where(mine, v2, minus)
            for i in range(frame_count // ROWS):
                part = slice(i * ROWS, (i + 1) * ROWS)
                r.ds[e, part, :] = (e12[2 * p + e, part, :].astype(F32) * mm_nt(left[part], right)).astype(BF16)
            dq.append(mm(r.ds[e], k2))
            dk.append(mm_tn(r.ds[e], q2))
            dv.append(mm_tn(e12[2 * p + e], scaled))
        act[0, :, cols] = (jnp.where(low, dq[0], dq[1]) * 0.125).astype(BF16)
        act[1, :, cols] = jnp.where(low, dk[0], dk[1]).astype(BF16)
        act[2, :, cols] = jnp.where(low, dv[0], dv[1]).astype(BF16)

    def bias_sums():
        cs[...] = jnp.zeros_like(cs)

        def body(rows):
            cs[0] += eights(act[0, rows, :].astype(F32))
            cs[1] += eights(act[2, rows, :].astype(F32))

        loop(body)
        fold(0, 0)
        fold(1, 2)
        gsm[1:2, :] = jnp.zeros((1, width), F32)
        gsm[13:16, :] = jnp.zeros((3, width), F32)

    def back_frames(k):
        r.d2[...] += mm_nt(act[k], square(k))

    def frames_ready():
        layer_out.wait()

        def body(rows):
            r.gbuf[rows, :] = r.d2[rows, :].astype(BF16)

        loop(body)
        frames_out.start()

    def small_copy(k, device):
        return pltpu.make_async_remote_copy(
            src_ref=r.sm.at[k], dst_ref=r.sl.at[k], send_sem=r.sms.at[0], recv_sem=r.smr.at[k],
            device_id=device, device_id_type=MESH)

    def small_step(k):
        if k == 0:
            r.sm[0] = gsm[...].astype(BF16)
        else:
            r.sm[k] = (r.sm[k - 1].astype(F32) + r.sl[k - 1].astype(F32)).astype(BF16)
        if k < 3:
            small_copy(k, net.across("cyx"[k])).start()

    def small_wait(k):
        small_copy(k, net.across("cyx"[k])).wait_recv()

    def small_line(k):
        return pltpu.make_async_remote_copy(
            src_ref=r.sm.at[3], dst_ref=r.sl.at[2 + k], send_sem=r.sms.at[0], recv_sem=r.smr.at[3],
            device_id=net.dev(z=lax.rem(net.z + k, NZ)), device_id_type=MESH)

    def small_total():
        landed = r.sl.at[pl.ds(3, NZ - 1)]
        pltpu.make_async_remote_copy(
            src_ref=landed, dst_ref=landed, send_sem=r.sms.at[0], recv_sem=r.smr.at[3], device_id=net.across("c"),
            device_id_type=MESH).wait_recv()
        whole = sum((r.sl[k].astype(F32) for k in range(3, 6)), r.sm[3].astype(F32))
        index = (net.y * 2 + net.c) * 2 * NZ + net.z * 2 + net.x
        turned = pltpu.roll(whole, lax.rem(width - index * lead, width), 1)
        row = lax.broadcasted_iota(jnp.int32, (16, width), 0)
        block = lax.div(index, 8)
        inner = jnp.sum(jnp.where(row == 9 + block, whole, 0.0), axis=0, keepdims=True)
        inner = pltpu.roll(jnp.broadcast_to(inner, (8, width)), lax.rem(width - lax.rem(index, 8) * 4 * lead, width), 1)
        r.gsmall[0:8, :] = turned[0:8, :LANES]
        r.gsmall[8:16, :] = jnp.where(row[:8, :LANES] == 0, turned[8:9, :LANES], inner[:, :LANES])

    def swap_back(u):
        return pltpu.make_async_remote_copy(
            src_ref=r.ys.at[u], dst_ref=r.yr.at[u], send_sem=r.yss.at[0], recv_sem=r.yrs.at[0],
            device_id=net.across("x"), device_id_type=MESH)

    def out_of(u):
        if u < 4:
            return (r.gwq, r.gwk, r.gwv, r.gwo)[u], 0
        return r.gwi, (u - 4) * width

    def total_square(u):
        r.f8[...] = scatter[u].total()
        out, start = out_of(u)
        mine, theirs = pl.multiple_of(net.x * lead, 8), pl.multiple_of((1 - net.x) * lead, 8)
        r.ys[u] = jnp.concatenate([r.f8[pl.ds(theirs, lead), :], jnp.zeros((8, half), F32)], axis=0).astype(BF16)
        swap_back(u).start()
        out[:, pl.ds(pl.multiple_of(start + net.x * half, LANES), half)] = r.f8[pl.ds(mine, lead), :]

    def last():
        pltpu.make_async_remote_copy(
            src_ref=r.ys, dst_ref=r.yr, send_sem=r.yss.at[0], recv_sem=r.yrs.at[0], device_id=net.across("x"),
            device_id_type=MESH).wait_recv()
        for u in range(8):
            out, start = out_of(u)
            out[:, pl.ds(pl.multiple_of(start + (1 - net.x) * half, LANES), half)] = r.yr[u].astype(F32)[:lead]

    def total_outer(i):
        r.gwouter[:, pl.ds(*OUTER[i - 8])] = scatter[i].total()

    def unit(i, left=None, right=None):
        steps = SimpleNamespace(**gather[i])
        if i == len(UNITS) - 1:
            return steps
        way, square = scatter[i], i < 8

        def half_of(own):
            if square:
                grad_square(i, left, right, own)
            else:
                grad_outer(i, own)

        def away():
            half_of(False)
            way.sibling_out().start()

        def home():
            half_of(True)
            way.spread()

        steps.away, steps.home = away, home
        steps.t, steps.u, steps.v = way.fold_first, way.fold_second, way.fold_third
        if square:
            steps.p = functools.partial(merge, i)
            steps.x = functools.partial(total_square, i)
        else:
            steps.x = functools.partial(total_outer, i)
        return steps

    def give(k):
        pl.semaphore_signal(r.free.at[k], inc=1, device_id=net.across("c"), device_id_type=MESH)

    def take(k):
        pl.semaphore_wait(r.free.at[k], 1)

    def turn():
        x_in.wait()
        r.xt[...] = jnp.transpose(r.xbuf[...]).reshape(r.xt.shape)

    def gather_end():
        kinds = ((range(8), pair * half, half), (range(8, 12), lead * 4 * LANES, 2 * LANES), (range(12, 13), 16 * LANES, LANES))
        for kind, (units, count, run) in enumerate(kinds):
            flat = lines = 0
            for i in units:
                size = count * (OUTER[i - 8][1] // LANES if kind == 1 else 1)
                flat += size * (12 if GATHER[i][0] == "z" else 9)
                lines += size * (2 if GATHER[i][0] == "z" else 4)
            sent(stretch(e12, flat, run), r.gout.at[kind])
            inside = (net.z > 0) & (net.z < NZ - 1)
            for way, times in ((inside, 2), (jnp.logical_not(inside), 1)):
                pl.when(way)(functools.partial(sent, stretch(e12, lines * times, run), r.gline.at[kind]))
        mates_sent(r.gmate)
        sent(r.small.at[:, 0], r.gmate.at[2])

    def small(k):
        if k > 0:
            small_wait(k - 1)
        small_step(k)
        if k == 3:
            for one in range(1, NZ):
                small_line(one).start()

    def end():
        sent(stretch(e12, 8 * 15 * pair * half, half), r.sout.at[0])
        sent(stretch(e12, 15 * 4 * lead * width, 2 * LANES), r.sout.at[1])
        mates_sent(r.smate)
        sent(r.xs, r.xss.at[0])
        sent(r.ys, r.yss.at[0])
        sent(r.sl, r.sms.at[0])
        frames_out.wait()

    def rolled(count, body):
        def one(i, carry):
            body(i)
            return carry

        lax.fori_loop(0, count, one, 0)

    def go(*steps):
        for step in steps:
            step()

    q, k, v = (unit(u, r.xt, lambda u=u: act[u]) for u in range(3))
    o = unit(3, r.ctx_t, lambda: r.low[...])
    i0, i1, i2, i3 = (unit(4 + u, r.hid_t, lambda u=u: gp[u]) for u in range(4))
    w0, w1, w2_, w3 = (unit(8 + u) for u in range(4))
    s = unit(12)
    place()
    go(w3.a, w1.a, w3.b, s.a, q.p, q.a, w3.c, s.b, q.b, v.p, i1.p, i1.a)
    go(k.p, i0.p, k.a, q.c, v.a, w0.a, k.b, w3.d, s.c, k.c, w2_.a, i3.p)
    go(i0.a, q.d, o.p, o.a, i2.p, w3.e, s.d, v.b, i3.a, k.d, i2.a, s.e)
    go(i0.b, v.c, i0.c, o.b, w3.g, q.e, q.g, i2.b, s.g, k.e, i3.b, v.d)
    vectors()
    go(i1.b, i3.c)

    def project_run(i):
        project(i)

        @pl.when(i == 0)
        def _():
            go(k.g, o.c)

        @pl.when(i == 1)
        def _():
            go(i0.d, i2.c, v.e, w1.b, o.d, i1.c, v.g, i3.d)

    rolled(3, project_run)
    go(w2_.b)

    def attend_run(i):
        attend(i)

        @pl.when(i == 1)
        def _():
            go(w0.b, i1.d)

        @pl.when(i == 4)
        def _():
            go(w1.c, i2.d, i0.e, i3.e, w1.d, w2_.c, w0.c, o.e)

    rolled(6, attend_run)
    go(w0.d, i0.g, i1.e, o.g)
    norm_one()
    go(i2.e)

    def feed_run(i):
        feed(i)

        @pl.when(i == 0)
        def _():
            go(w2_.d, i1.g, i2.g)

        @pl.when(i == 1)
        def _():
            go(w1.e)

        @pl.when(i == 2)
        def _():
            go(i3.g, w0.e)

    rolled(4, feed_run)
    go(w2_.e, w1.g)
    feed_out(1)
    feed_out(3)
    go(w0.g)
    feed_out(0)
    go(w2_.g)
    feed_out(2)
    norm_two()
    go(w2_.away)
    gather_end()
    go(w3.away, w0.away, w1.away, w2_.home)

    def back_feed_run(i):
        back_feed(i)

        @pl.when(i == 1)
        def _():
            go(w3.home, w0.home)

        @pl.when(i == 2)
        def _():
            go(w2_.t, w1.home)

    rolled(4, back_feed_run)

    def back_hidden_run(i):
        back_hidden(i)

        @pl.when(i == 0)
        def _():
            go(w3.t)

    rolled(4, back_hidden_run)
    give(1)
    layer_out.start()
    take(1)
    go(i0.away, w1.t)
    give(0)
    go(i1.away, w0.t)
    back_norm_one()
    go(i0.home, i2.away, i1.home, i3.away)
    back_context()
    go(w1.u, w1.v)

    def back_attend_run(i):
        back_attend(i)

        @pl.when(i == 0)
        def _():
            give(2)
            take(2)
            go(i3.home, i2.home, o.away)

        @pl.when(i == 1)
        def _():
            take(0)

        @pl.when(i == 2)
        def _():
            go(i1.t, o.home)

        @pl.when(i == 3)
        def _():
            go(i0.t, i3.t, i2.t)

    rolled(6, back_attend_run)
    go(w1.x, q.away, o.t)

    def back_frames_run(i):
        back_frames(i)

        @pl.when(i == 0)
        def _():
            go(i2.u, v.away, q.home)
            bias_sums()
            go(v.home, k.away, i2.v, o.u, k.home, i3.u, i3.v, q.t, q.u, o.v, k.t, i0.u)
            go(q.v)
            small(0)
            go(v.t, w2_.u, i1.u, k.u, i2.x, i0.v, v.u, k.v)
            small(1)
            go(w3.u, i3.x)

        @pl.when(i == 1)
        def _():
            go(i1.v)
            small(2)
            go(v.v, w0.u, q.x, w3.v, i1.x)
            small(3)
            go(w2_.v, o.x, i0.x, w0.v, k.x, w2_.x, v.x, w0.x, w3.x)

    rolled(3, back_frames_run)
    frames_ready()
    small_total()
    last()
    end()


def kernel_device(
    frames, lengths, query_weight, query_bias, key_weight, value_weight, value_bias, output_weight, output_bias,
    first_gain, first_shift, inner_weight, inner_bias, outer_weight, outer_bias, second_gain, second_shift, grad_out,
):
    count, width = frames.shape
    lead = query_weight.shape[0]
    pair, half = 2 * lead, width // 2
    vmem, hbm = pl.BlockSpec(memory_space=pltpu.VMEM), pl.BlockSpec(memory_space=pl.ANY)
    smem = pl.BlockSpec(memory_space=pltpu.SMEM)
    args = dict(
        frames=(hbm, frames), grad_out=(hbm, grad_out), lengths=(smem, lengths), wq=(vmem, query_weight),
        wk=(vmem, key_weight), wv=(vmem, value_weight), wo=(vmem, output_weight), wi=(vmem, inner_weight),
        wouter=(vmem, outer_weight), bq=(vmem, query_bias), bv=(vmem, value_bias), bo=(vmem, output_bias),
        g1=(vmem, first_gain), s1=(vmem, first_shift), b2=(vmem, outer_bias), gg2=(vmem, second_gain),
        s2=(vmem, second_shift), bi1=(vmem, inner_bias))
    shape = jax.ShapeDtypeStruct
    outs = dict(
        layer_out=(hbm, shape((count, width), BF16)), frames_grad=(hbm, shape((count, width), BF16)),
        gwq=(vmem, shape((lead, width), F32)), gwk=(vmem, shape((lead, width), F32)),
        gwv=(vmem, shape((lead, width), F32)), gwo=(vmem, shape((lead, width), F32)),
        gwi=(vmem, shape(inner_weight.shape, F32)), gwouter=(vmem, shape(outer_weight.shape, F32)),
        gsmall=(vmem, shape((16, LANES), F32)))
    dma = pltpu.SemaphoreType.DMA
    big = (count, width)
    square = (2, 2, pair * NZ, width)
    turned = (2, 2, pair * NZ, count)
    lead_shape = (2, 2, 2, 2, 8 * lead, width)
    scratch = dict(
        w8=((8,) + square, BF16), w2=(lead_shape, BF16), g2=(lead_shape, BF16), small=((2, 2, NZ, 2, 16, LANES), BF16),
        pack=((16, LANES), F32), xs=((8, lead + 8, half), BF16), xr=((8, lead + 8, half), BF16),
        ys=((8, lead + 8, half), BF16), yr=((8, lead + 8, half), BF16), xbuf=(big, BF16), gbuf=(big, BF16), q3=((3,) + big, BF16),
        e12=((HEADS, count, count), BF16), linv=(big, F32), ctx=(big, BF16), xt=(turned, BF16), ctx_t=(turned, BF16),
        hid_t=(turned, BF16), low=(big, BF16), n1=(big, F32), r1=((count, LANES), F32), act=((4,) + big, BF16),
        gp=((4,) + big, BF16), act_t=((2, 2, width, count), BF16), fa=(big, F32), d2=(big, F32),
        ds=((2, count, count), BF16), mq=((2, count, LANES), BF16), mk=((2, count, LANES), BF16), vec=((16, width), F32),
        bi=((4, 1, width), F32), gsm=((16, width), F32), cs=((3, 8, width), F32), sm=((4, 16, width), BF16),
        sl=((6, 16, width), BF16), f8=((pair, half), F32))
    for i in range(12):
        for kind, size in zip(LANDING, landing_shapes(i, pair, half, 4 * lead), strict=True):
            scratch[f"{kind}{i}"] = (size, BF16)
    scratch = {k: pltpu.VMEM(*v) for k, v in scratch.items()}
    scratch.update(
        gout=dma((3,)), gline=dma((3,)), gmate=dma((3,)), grecv=dma((13, 5)), sout=dma((2,)), smate=dma((2,)), srecv=dma((12, 5)),
        xss=dma((1,)), xrs=dma((8,)), yss=dma((1,)), yrs=dma((1,)), sms=dma((1,)), smr=dma((4,)), isem=dma((2,)), free=pltpu.SemaphoreType.REGULAR((3,)))
    got = pl.pallas_call(
        functools.partial(layer_kernel, (*args, *outs, *scratch)),
        out_shape=[o[1] for o in outs.values()],
        in_specs=[a[0] for a in args.values()],
        out_specs=[o[0] for o in outs.values()],
        scratch_shapes=list(scratch.values()),
        compiler_params=pltpu.CompilerParams(collective_id=0, has_side_effects=True, vmem_limit_bytes=VMEM_BYTES),
    )(*(a[1] for a in args.values()))

    bias, wide = shape((lead,), F32), shape((4 * lead,), F32)
    vectors = {3: bias, 6: bias, 8: bias, 9: bias, 10: bias, 12: wide, 14: bias, 15: bias, 16: bias}
    row_of = {3: 0, 6: 2, 8: 3, 9: 4, 10: 5, 12: 9, 14: 6, 15: 7, 16: 8}
    places = [i for i in range(17) if i not in vectors]

    def publish(*refs):
        came, small, out = refs[:8], refs[8], refs[9:]
        for a, i in zip(came, places, strict=True):
            out[i][...] = a[...]
        for i, row in row_of.items():
            size = vectors[i].shape[0]
            out[i][...] = small[row:row + 1, :size].reshape(size)

    whole = dict(zip(places, (o[1] for o in list(outs.values())[:8]), strict=True))
    return tuple(pl.pallas_call(
        publish,
        out_shape=[vectors[i] if i in vectors else whole[i] for i in range(17)],
        in_specs=[vmem] * 9,
        out_specs=[vmem] * 17,
    )(*got))


VMEM_BYTES = 63 << 20


def solution(mesh):
    split = P(("dp", "fsdp"))
    rows = P(("dp", "fsdp"), None)
    in_specs = (
        rows, rows, rows, split, rows, rows, split, rows, split, split, split, rows, split, rows, split, split, split, rows,
    )
    out_specs = (
        rows, rows, rows, split, rows, rows, split, rows, split, split, split, rows, split, rows, split, split, split,
    )
    fits = mesh.shape["dp"] == 4 and mesh.shape["fsdp"] == 2 * NZ

    def per_device(frames, lengths, query_weight, *rest):
        lead, width = query_weight.shape
        good = fits and lead % 8 == 0 and 4 * lead <= LANES and width == 768
        run = kernel_device if good else general_device
        return run(frames, lengths, query_weight, *rest)

    return jax.shard_map(per_device, mesh=mesh, in_specs=in_specs, out_specs=out_specs, check_vma=False)
```

```python
import functools
from types import SimpleNamespace

import jax
import jax.numpy as jnp
from jax import lax
from jax.experimental import pallas as pl
from jax.experimental.pallas import tpu as pltpu
from jax.sharding import PartitionSpec as P

HEADS = 12


def layer_norm(values, gain_vec, shift_vec):
    center = values - jnp.mean(values, axis=-1, keepdims=True)
    spread = jnp.mean(center * center, axis=-1, keepdims=True)
    return center * lax.rsqrt(spread + 1e-05) * gain_vec + shift_vec


def exact_gelu(values):
    return jax.nn.gelu(values, approximate=False)


def matmul(left_side, right_side):
    return jnp.dot(left_side, right_side, preferred_element_type=jnp.float32)


def matmul_tn(left_side, right_side):
    return lax.dot_general(
        left_side, right_side, (((0,), (0,)), ((), ())), preferred_element_type=jnp.float32
    )


def matmul_nt(left_side, right_side):
    return lax.dot_general(
        left_side, right_side, (((1,), (1,)), ((), ())), preferred_element_type=jnp.float32
    )


def column_sums(values):
    return jnp.sum(values.astype(jnp.float32), axis=0)


def block_scores(query_block, key_heads, group_block, groups, score_scale):
    raw_scores = (
        jnp.einsum("qhd,khd->hqk", query_block, key_heads, preferred_element_type=jnp.float32)
        * score_scale
    )
    allowed = group_block[:, None] == groups[None, :]
    return jnp.where(allowed[None], raw_scores, -1e30)


def general_device(
    frames,
    lengths,
    query_weight,
    query_bias,
    key_weight,
    value_weight,
    value_bias,
    output_weight,
    output_bias,
    first_gain,
    first_shift,
    inner_weight,
    inner_bias,
    outer_weight,
    outer_bias,
    second_gain,
    second_shift,
    grad_out,
):
    frame_count = frames.shape[0]
    model_width = frames.shape[1]
    head_size = model_width // HEADS
    score_scale = head_size ** (-0.5)
    places = jnp.arange(frame_count, dtype=jnp.int32)
    bounds = jnp.stack([lengths[0, 0], lengths[0, 0] + lengths[0, 1]])
    groups = jnp.sum((places[:, None] >= bounds[None, :]).astype(jnp.int32), axis=1)
    live_mask = (places < bounds[-1]).astype(jnp.float32)
    gathered = (
        lax.all_gather(query_weight, ("dp", "fsdp"), axis=0, tiled=True),
        lax.all_gather(query_bias, ("dp", "fsdp"), axis=0, tiled=True),
        lax.all_gather(key_weight, ("dp", "fsdp"), axis=0, tiled=True),
        lax.all_gather(value_weight, ("dp", "fsdp"), axis=0, tiled=True),
        lax.all_gather(value_bias, ("dp", "fsdp"), axis=0, tiled=True),
        lax.all_gather(output_weight, ("dp", "fsdp"), axis=0, tiled=True),
        lax.all_gather(output_bias, ("dp", "fsdp"), axis=0, tiled=True),
        lax.all_gather(first_gain, ("dp", "fsdp"), axis=0, tiled=True),
        lax.all_gather(first_shift, ("dp", "fsdp"), axis=0, tiled=True),
        lax.all_gather(inner_weight, ("dp", "fsdp"), axis=0, tiled=True),
        lax.all_gather(inner_bias, ("dp", "fsdp"), axis=0, tiled=True),
        lax.all_gather(outer_weight, ("dp", "fsdp"), axis=0, tiled=True),
        lax.all_gather(outer_bias, ("dp", "fsdp"), axis=0, tiled=True),
        lax.all_gather(second_gain, ("dp", "fsdp"), axis=0, tiled=True),
        lax.all_gather(second_shift, ("dp", "fsdp"), axis=0, tiled=True),
    )
    (
        query_mat,
        query_vec,
        key_mat,
        value_mat,
        value_vec,
        output_mat,
        output_vec,
        first_scale,
        first_offset,
        inner_mat,
        inner_vec,
        outer_mat,
        outer_vec,
        second_scale,
        second_offset,
    ) = gathered
    query_rows = (matmul(frames, query_mat) + query_vec.astype(jnp.float32)).astype(jnp.bfloat16)
    key_rows = matmul(frames, key_mat).astype(jnp.bfloat16)
    value_rows = (matmul(frames, value_mat) + value_vec.astype(jnp.float32)).astype(jnp.bfloat16)
    query_heads = query_rows.reshape(frame_count, HEADS, head_size)
    key_heads = key_rows.reshape(frame_count, HEADS, head_size)
    value_heads = value_rows.reshape(frame_count, HEADS, head_size)
    scores = block_scores(query_heads, key_heads, groups, groups, score_scale)
    row_max = jnp.max(scores, axis=-1, keepdims=True)
    raw_weights = jnp.exp(scores - row_max)
    row_total = jnp.sum(raw_weights, axis=-1, keepdims=True)
    attn_prob = raw_weights / row_total
    log_totals = row_max + jnp.log(row_total)
    context_parts = jnp.einsum(
        "hqk,khd->qhd",
        attn_prob.astype(jnp.bfloat16),
        value_heads,
        preferred_element_type=jnp.float32,
    )
    context_rows = context_parts.reshape(frame_count, model_width).astype(jnp.bfloat16)
    frames_float = frames.astype(jnp.float32)
    resid_one = frames_float + matmul(context_rows, output_mat) + output_vec.astype(jnp.float32)
    hidden, first_pull = jax.vjp(
        layer_norm, resid_one, first_scale.astype(jnp.float32), first_offset.astype(jnp.float32)
    )
    hidden_low = hidden.astype(jnp.bfloat16)
    inner_pre = matmul(hidden_low, inner_mat) + inner_vec.astype(jnp.float32)
    active, gelu_pull = jax.vjp(exact_gelu, inner_pre)
    active_low = active.astype(jnp.bfloat16)
    outer_out = matmul(active_low, outer_mat) + outer_vec.astype(jnp.float32)
    normed_out, second_pull = jax.vjp(
        layer_norm,
        hidden + outer_out,
        second_scale.astype(jnp.float32),
        second_offset.astype(jnp.float32),
    )
    layer_out = (normed_out * live_mask[:, None]).astype(jnp.bfloat16)
    grad_top = grad_out.astype(jnp.float32) * live_mask[:, None]
    grad_two, second_gain_grad, second_shift_grad = second_pull(grad_top)
    grad_outer = grad_two.astype(jnp.bfloat16)
    outer_mat_grad = matmul_tn(active_low, grad_outer)
    outer_vec_grad = column_sums(grad_outer)
    (grad_inner,) = gelu_pull(matmul_nt(grad_outer, outer_mat))
    grad_inner_low = grad_inner.astype(jnp.bfloat16)
    inner_mat_grad = matmul_tn(hidden_low, grad_inner_low)
    inner_vec_grad = column_sums(grad_inner_low)
    grad_hidden = grad_two + matmul_nt(grad_inner_low, inner_mat)
    grad_one, first_gain_grad, first_shift_grad = first_pull(grad_hidden)
    grad_attn = grad_one.astype(jnp.bfloat16)
    output_mat_grad = matmul_tn(context_rows, grad_attn)
    output_vec_grad = column_sums(grad_attn)
    grad_context = (
        matmul_nt(grad_attn, output_mat).astype(jnp.bfloat16).reshape(frame_count, HEADS, head_size)
    )
    scores = block_scores(query_heads, key_heads, groups, groups, score_scale)
    attn_prob = jnp.exp(scores - log_totals)
    grad_prob = jnp.einsum(
        "qhd,khd->hqk", grad_context, value_heads, preferred_element_type=jnp.float32
    )
    inner_sum = jnp.sum(attn_prob * grad_prob, axis=-1, keepdims=True)
    grad_scores = (attn_prob * (grad_prob - inner_sum)).astype(jnp.bfloat16)
    query_grad_parts = (
        jnp.einsum("hqk,khd->qhd", grad_scores, key_heads, preferred_element_type=jnp.float32)
        * score_scale
    )
    key_grad_sum = (
        jnp.einsum("hqk,qhd->khd", grad_scores, query_heads, preferred_element_type=jnp.float32)
        * score_scale
    )
    value_grad_sum = jnp.einsum(
        "hqk,qhd->khd",
        attn_prob.astype(jnp.bfloat16),
        grad_context,
        preferred_element_type=jnp.float32,
    )
    grad_query = query_grad_parts.reshape(frame_count, model_width).astype(jnp.bfloat16)
    grad_key = key_grad_sum.reshape(frame_count, model_width).astype(jnp.bfloat16)
    grad_value = value_grad_sum.reshape(frame_count, model_width).astype(jnp.bfloat16)
    query_mat_grad = matmul_tn(frames, grad_query)
    query_vec_grad = column_sums(grad_query)
    key_mat_grad = matmul_tn(frames, grad_key)
    value_mat_grad = matmul_tn(frames, grad_value)
    value_vec_grad = column_sums(grad_value)
    frames_grad = (
        grad_one
        + matmul_nt(grad_query, query_mat)
        + matmul_nt(grad_key, key_mat)
        + matmul_nt(grad_value, value_mat)
    ).astype(jnp.bfloat16)
    shares = (
        lax.psum_scatter(query_mat_grad, ("dp", "fsdp"), scatter_dimension=0, tiled=True),
        lax.psum_scatter(query_vec_grad, ("dp", "fsdp"), scatter_dimension=0, tiled=True),
        lax.psum_scatter(key_mat_grad, ("dp", "fsdp"), scatter_dimension=0, tiled=True),
        lax.psum_scatter(value_mat_grad, ("dp", "fsdp"), scatter_dimension=0, tiled=True),
        lax.psum_scatter(value_vec_grad, ("dp", "fsdp"), scatter_dimension=0, tiled=True),
        lax.psum_scatter(output_mat_grad, ("dp", "fsdp"), scatter_dimension=0, tiled=True),
        lax.psum_scatter(output_vec_grad, ("dp", "fsdp"), scatter_dimension=0, tiled=True),
        lax.psum_scatter(first_gain_grad, ("dp", "fsdp"), scatter_dimension=0, tiled=True),
        lax.psum_scatter(first_shift_grad, ("dp", "fsdp"), scatter_dimension=0, tiled=True),
        lax.psum_scatter(inner_mat_grad, ("dp", "fsdp"), scatter_dimension=0, tiled=True),
        lax.psum_scatter(inner_vec_grad, ("dp", "fsdp"), scatter_dimension=0, tiled=True),
        lax.psum_scatter(outer_mat_grad, ("dp", "fsdp"), scatter_dimension=0, tiled=True),
        lax.psum_scatter(outer_vec_grad, ("dp", "fsdp"), scatter_dimension=0, tiled=True),
        lax.psum_scatter(second_gain_grad, ("dp", "fsdp"), scatter_dimension=0, tiled=True),
        lax.psum_scatter(second_shift_grad, ("dp", "fsdp"), scatter_dimension=0, tiled=True),
    )
    return (
        layer_out,
        frames_grad,
        shares[0],
        shares[1],
        shares[2],
        shares[3],
        shares[4],
        shares[5],
        shares[6],
        shares[7],
        shares[8],
        shares[9],
        shares[10],
        shares[11],
        shares[12],
        shares[13],
        shares[14],
    )


MESH = pl.DeviceIdType.MESH
NZ = 4
LANES = 128


class Net:
    def __init__(self):
        dp, fs = lax.axis_index("dp"), lax.axis_index("fsdp")
        self.y, self.c = lax.div(dp, 2), lax.rem(dp, 2)
        self.z, self.x = lax.div(fs, 2), lax.rem(fs, 2)

    def dev(self, y=None, c=None, z=None, x=None):
        y = self.y if y is None else y
        c = self.c if c is None else c
        z = self.z if z is None else z
        x = self.x if x is None else x
        return (y * 2 + c, z * 2 + x)

    def across(self, dim):
        if dim == "x":
            return self.dev(x=1 - self.x)
        if dim == "y":
            return self.dev(y=1 - self.y)
        return self.dev(c=1 - self.c)

    def greet(self):
        bar = pltpu.get_barrier_semaphore()

        def tell(device):
            pl.semaphore_signal(bar, inc=1, device_id=device, device_id_type=MESH)

        for dim in "xyc":
            tell(self.across(dim))
        for k in range(1, NZ):
            tell(self.dev(z=lax.rem(self.z + k, NZ)))

    def meet(self):
        pl.semaphore_wait(pltpu.get_barrier_semaphore(), 3 + NZ - 1)


class Way:
    def __init__(self, net, region, order, sems):
        self.net, self.region, self.order = net, region, order
        self.out, self.mate, self.recv = sems

    def copy(self, src, dst, slot, device, send=None):
        return pltpu.make_async_remote_copy(
            src_ref=src, dst_ref=dst, send_sem=self.out if send is None else send, recv_sem=self.recv.at[slot],
            device_id=device, device_id_type=MESH)

    def wait_for(self, ref, slot):
        self.copy(ref, ref, slot, self.net.across("c")).wait_recv()

    def part(self, have="", **at):
        n = self.net
        for d in "yzx":
            at.setdefault(d, None if d in have else getattr(n, d))
        return self.region(at["y"], n.c, at["z"], at["x"])

    def flip(self, *dims):
        return {d: 1 - getattr(self.net, d) for d in dims}

    def ahead(self, k):
        return lax.rem(self.net.z + k, NZ)


class Gather(Way):
    def __init__(self, net, region, order, sems, bulk, line_out):
        super().__init__(net, region, order, sems)
        self.bulk, self.line_out = bulk, line_out

    def lines_start(self, have):
        n = self.net
        part = self.part(have)
        inside = lax.rem(lax.div(n.z + 1, 2), 2)
        self.copy(part, part, 4 * (1 - inside), n.dev(z=self.ahead(2)), self.line_out).start()

        @pl.when(n.z < NZ - 1)
        def _():
            self.copy(part, part, 0, n.dev(z=n.z + 1), self.line_out).start()

        @pl.when(n.z > 0)
        def _():
            self.copy(part, part, 0, n.dev(z=n.z - 1), self.line_out).start()

    def lines_pass(self, have):
        n = self.net

        @pl.when((n.z > 0) & (n.z < NZ - 1))
        def _():
            part = self.part(have, z=(NZ - 1) * (2 - n.z))
            self.wait_for(part, 4)
            self.copy(part, part, 0, n.dev(z=(NZ - 1) * (n.z - 1)), self.line_out).start()

    def lines_wait(self, have):
        n = self.net
        times = 2 if have else 1

        @pl.when((n.z > 0) & (n.z < NZ - 1))
        def _():
            self.wait_for(self.bulk(times, 2), 0)

        @pl.when((n.z == 0) | (n.z == NZ - 1))
        def _():
            self.wait_for(self.bulk(times, 3), 0)

    def over(self, slot, d, have, **at):
        part = self.part(have, **at)
        return self.copy(part, part, slot, self.net.across(d))

    def sibling(self):
        part = self.region(None, self.net.c, None, None)
        return self.copy(part, part, 3, self.net.across("c"), self.mate)

    def stages(self):
        first, d2, d3 = self.order

        def spread():
            self.lines_wait("")
            self.over(1, d2, "z").start()
            self.over(2, d3, "z").start()

        def turn():
            self.over(1, d2, "z").wait_recv()
            self.over(2, d3, "z", **self.flip(d2)).start()

        def mate():
            self.wait_for(self.part((first + d2 if first == "z" else first + "z"), **self.flip(d3)), 2)
            self.sibling().start()

        def ready():
            self.sibling().wait_recv()

        if first == "z":
            start, onward = functools.partial(self.lines_start, ""), functools.partial(self.lines_pass, "")
            return dict(a=start, b=onward, c=spread, d=turn, e=mate, g=ready)

        def begin():
            self.over(1, first, "").start()

        def lines():
            self.over(1, first, "").wait_recv()
            self.lines_start(first)

        def cross():
            self.lines_wait(first)
            self.over(2, d3, first + "z").start()

        return dict(a=begin, b=lines, c=functools.partial(self.lines_pass, first), d=cross, e=mate, g=ready)


class Scatter(Way):
    def __init__(self, net, region, order, sems, first, third, line):
        super().__init__(net, region, order, sems)
        self.into_first, self.into_third, self.into_line = first, third, line
        self.inner = order[0] != "z"
        self.near = order[0] if self.inner else order[1]
        self.far = order[2]
        self.rest = self.near + "z" if self.inner else "z"

    def sibling(self, core):
        part = self.region(None, core, None, None)
        return self.copy(part, part, 4, self.net.across("c"), self.mate)

    def sibling_out(self):
        return self.sibling(1 - self.net.c)

    def sibling_in(self):
        return self.sibling(self.net.c)

    def first(self):
        if self.inner:
            return self.copy(self.part(self.rest, **self.flip(self.far)), self.into_first, 0, self.net.across(self.far))
        part = self.part("z", **self.flip(self.far, self.near))
        return self.copy(part, self.into_first.at[0], 0, self.net.across(self.far))

    def second(self):
        part = self.part("z", **self.flip(self.far))
        return self.copy(part, self.into_first.at[1], 1, self.net.across(self.far))

    def third(self):
        part = self.part("" if self.inner else "z", **self.flip(self.near))
        return self.copy(part, self.into_third, 2, self.net.across(self.near))

    def along(self, k):
        ahead = self.ahead(k)
        part = self.part(self.near if self.inner else "", z=ahead)
        return self.copy(part, self.into_line.at[k - 1], 3, self.net.dev(z=ahead))

    @staticmethod
    def add(part, *came):
        total = part[...].astype(jnp.float32)
        for one in came:
            total = total + one[...].astype(jnp.float32)
        part[...] = total.astype(part.dtype)

    def lines_start(self):
        for k in range(1, NZ):
            self.along(k).start()

    def lines_wait(self):
        self.wait_for(self.into_line, 3)
        return [self.into_line.at[k] for k in range(NZ - 1)]

    def spread(self):
        self.first().start()
        if not self.inner:
            self.second().start()

    def fold_first(self):
        self.first().wait_recv()
        if self.inner:
            self.add(self.part(self.rest), self.into_first)
            self.lines_start()
        else:
            self.add(self.part("z", **self.flip(self.near)), self.into_first.at[0])
            self.third().start()

    def fold_second(self):
        if self.inner:
            self.add(self.part(self.near), *self.lines_wait())
            self.third().start()
        else:
            self.second().wait_recv()
            self.add(self.part("z"), self.into_first.at[1])

    def fold_third(self):
        self.third().wait_recv()
        if not self.inner:
            self.add(self.part("z"), self.into_third)
            self.lines_start()

    def total(self):
        came = [self.into_third] if self.inner else self.lines_wait()
        out = self.part()[...].astype(jnp.float32)
        for one in came:
            out = out + one[...].astype(jnp.float32)
        return out


def region_square(ref):
    pair, half = ref.shape[2] // NZ, ref.shape[3] // 2

    def region(y, c, z, x):
        rows = pl.ds(0, pair * NZ) if z is None else pl.ds(pl.multiple_of(z * pair, 16), pair)
        cols = pl.ds(0, half * 2) if x is None else pl.ds(pl.multiple_of(x * half, LANES), half)
        return ref.at[pl.ds(0, 2) if y is None else y, c, rows, cols]

    return region


def region_lead(ref, start, size):
    run = ref.shape[4] // 2

    def region(y, c, z, x):
        rows = pl.ds(0, 2 * run) if x is None else pl.ds(pl.multiple_of(x * run, 16), run)
        high, low = (pl.ds(0, 2), pl.ds(0, 2)) if z is None else (lax.div(z, 2), lax.rem(z, 2))
        return ref.at[pl.ds(0, 2) if y is None else y, c, high, low, rows, pl.ds(start, size)]

    return region


def region_small(ref):
    def region(y, c, z, x):
        return ref.at[pl.ds(0, 2) if y is None else y, c, pl.ds(0, NZ) if z is None else z, pl.ds(0, 2) if x is None else x]

    return region


def bulk_square(ref):
    pair, half = ref.shape[2] // NZ, ref.shape[3] // 2
    return lambda times, k: ref.at[pl.ds(0, times), 0, pl.ds(0, k * pair), pl.ds(0, half)]


def bulk_lead(ref, start, size):
    run = ref.shape[4] // 2
    return lambda times, k: ref.at[0, 0, pl.ds(0, times), pl.ds(0, 2), pl.ds(0, k * run // 2), pl.ds(start, size)]


def bulk_small(ref):
    return lambda times, k: ref.at[0, 0, pl.ds(0, k), 0]


def stretch(ref, count, width):
    deep, tall, _ = ref.shape
    rows = count // width
    for a in range(deep, 0, -1):
        if rows % (16 * a) == 0 and rows // a <= tall:
            return ref.at[pl.ds(0, a), pl.ds(0, rows // a), pl.ds(0, width)]
    raise ValueError(count)


UNITS = range(13)
GATHER = ("zyx", "zxy", "zyx", "xzy", "zxy", "yzx", "zxy", "zyx", "xzy", "yzx", "zyx", "zxy", "zxy")
SCATTER = ("zyx", "zyx", "zxy", "zxy", "xzy", "yzx", "zyx", "zxy", "yzx", "zxy", "yzx", "xzy", "zxy")
OUTER = ((0, 256), (256, 256), (512, 128), (640, 128))


LANDING = ("first", "third", "line")


def landing_shapes(i, pair, half, run):
    order = SCATTER[i]
    if i < 8:
        piece, strip, wide = (pair, half), (pair * NZ, half), (pair * NZ, 2 * half)
        double = (pair, 2 * half)
    else:
        size = OUTER[i - 8][1]
        piece, strip, wide = (run, size), (2, 2, run, size), (2, 2, 2 * run, size)
        double = (2 * run, size)
    if order[0] == "z":
        return (2,) + strip, strip, (NZ - 1,) + piece
    if order[0] == "x":
        return wide, piece, (NZ - 1,) + double
    return (2,) + strip, piece, (NZ - 1, 2) + piece


def mm(left, right):
    return jnp.dot(left, right, preferred_element_type=jnp.float32)


def mm_nt(left, right):
    return lax.dot_general(left, right, (((1,), (1,)), ((), ())), preferred_element_type=jnp.float32)


def mm_tn(left, right):
    return lax.dot_general(left, right, (((0,), (0,)), ((), ())), preferred_element_type=jnp.float32)


def eights(block):
    return jnp.sum(block.reshape(block.shape[0] // 8, 8, block.shape[1]), axis=0)


STEP = 128
F32, BF16 = jnp.float32, jnp.bfloat16


def layer_kernel(names, *refs):
    r = SimpleNamespace(**dict(zip(names, refs, strict=True)))
    net = Net()
    frame_count, width = r.frames.shape
    half = width // 2
    lead = r.wq.shape[0]
    pair = 2 * lead
    own_rows = pl.ds(pl.multiple_of(net.z * pair, 16), pair)
    own_cols = pl.ds(pl.multiple_of(net.x * half, LANES), half)
    w8, w2 = r.w8, r.w2
    g2, e12 = r.g2, r.e12

    x_in = pltpu.make_async_copy(r.frames, r.xbuf, r.isem.at[0])
    g_in = pltpu.make_async_copy(r.grad_out, r.gbuf, r.isem.at[1])
    net.greet()
    x_in.start()
    g_in.start()

    gather, scatter = [], []
    for i in UNITS:
        cols = OUTER[i - 8] if 8 <= i < 12 else None
        if i < 8:
            region, bulk = region_square(w8.at[i]), bulk_square(w8.at[i])
            to = region_square(w2.at[i // 2, i % 2]) if i < 3 else region
        elif cols:
            region, bulk, to = region_lead(w2, *cols), bulk_lead(w2, *cols), region_lead(g2, *cols)
        else:
            region, bulk = region_small(r.small), bulk_small(r.small)
        kind = 0 if i < 8 else 1 if cols else 2
        sems = r.gout.at[kind], r.gmate.at[kind], r.grecv.at[i]
        gather.append(Gather(net, region, GATHER[i], sems, bulk, r.gline.at[kind]).stages())
        if i < 12:
            landing = (getattr(r, f"{name}{i}") for name in LANDING)
            sems = r.sout.at[kind], r.smate.at[kind], r.srecv.at[i]
            scatter.append(Scatter(net, to, SCATTER[i], sems, *landing))

    def sent(ref, sem):
        pltpu.make_async_remote_copy(
            src_ref=ref, dst_ref=ref, send_sem=sem, recv_sem=r.grecv.at[0, 0], device_id=net.across("c"),
            device_id_type=MESH).wait_send()

    def mates_sent(mate):
        sent(w8.at[:, :, 0], mate.at[0])
        sent(w2.at[:, 0], mate.at[1])

    def shard(u):
        if u < 4:
            return (r.wq, r.wk, r.wv, r.wo)[u][...]
        return r.wi[:, (u - 4) * width:(u - 3) * width]

    def swap(u):
        return pltpu.make_async_remote_copy(
            src_ref=r.xs.at[u], dst_ref=r.xr.at[u], send_sem=r.xss.at[0], recv_sem=r.xrs.at[u],
            device_id=net.across("x"), device_id_type=MESH)

    def offer(u):
        v = shard(u).astype(F32)
        theirs = jnp.where(net.x == 0, v[:, half:], v[:, :half])
        r.xs[u] = jnp.concatenate([theirs, jnp.zeros((8, half), F32)], axis=0).astype(BF16)

    def merge(u):
        swap(u).wait_recv()
        v = shard(u).astype(F32)
        mine = jnp.where(net.x == 0, v[:, :half], v[:, half:])
        came = r.xr[u].astype(F32)[:lead]
        first, second = jnp.where(net.x == 0, mine, came), jnp.where(net.x == 0, came, mine)
        w8[u, net.y, net.c, own_rows, own_cols] = jnp.concatenate([first, second], axis=0).astype(BF16)

    def place():
        for k in range(8):
            offer(k)
        pack = r.pack
        pack[...] = jnp.zeros_like(pack)
        for row, one in enumerate((r.bq, None, r.bv, r.bo, r.g1, r.s1, r.b2, r.gg2, r.s2, r.bi1)):
            if one is not None:
                size = one.shape[0]
                pack[row:row + 1, :size] = one[...].astype(F32).reshape(1, size)
        r.small[net.y, net.c, net.z, net.x] = pack[...].astype(BF16)
        w2[net.y, net.c, lax.div(net.z, 2), lax.rem(net.z, 2), pl.ds(pl.multiple_of(net.x * 4 * lead, 16), 4 * lead), :] = (
            r.wouter[...])
        masks()
        turn()
        net.meet()
        for k in range(8):
            swap(k).start()

    l0 = r.lengths[0, 0]
    l1 = l0 + r.lengths[0, 1]
    vec, bi, gsm, cs = r.vec, r.bi, r.gsm, r.cs
    fa, q3 = r.fa, r.q3
    act, gp, act_t = r.act, r.gp, r.act_t

    def loop(body, step=STEP, total=frame_count):
        def one(i, carry):
            body(pl.ds(pl.multiple_of(i * step, step), step))
            return carry

        lax.fori_loop(0, total // step, one, 0)

    def groups(shape, dim, start=0):
        place = lax.broadcasted_iota(jnp.int32, shape, dim) + start
        return (place >= l0).astype(jnp.int32) + (place >= l1).astype(jnp.int32)

    def masks():
        shape = (frame_count, LANES)
        lane = lax.broadcasted_iota(jnp.int32, shape, 1)
        group = groups(shape, 0)
        for e in range(2):
            spare = lane - (1 - e) * (LANES // 2)
            inside = (spare >= 0) & (spare < 3)
            r.mq[e] = jnp.where(inside & (spare != group), -1e30, 0.0).astype(BF16)
            r.mk[e] = jnp.where(inside & (spare == group), 1.0, 0.0).astype(BF16)

    def vectors():
        got = r.small[...].reshape(32 * 16, LANES)
        lane = lax.broadcasted_iota(jnp.int32, (LANES, width), 0)
        col = lax.broadcasted_iota(jnp.int32, (LANES, width), 1)
        tile = jnp.where((lane < lead) & (lane == lax.rem(col, lead)), 1.0, 0.0).astype(BF16)
        wide = mm(got, tile).reshape(32, 16, width)
        owner = lax.broadcasted_iota(jnp.int32, wide.shape, 0)
        place = lax.div(lax.broadcasted_iota(jnp.int32, wide.shape, 2), lead)
        vec[...] = jnp.sum(jnp.where(owner == place, wide, 0.0), axis=0)
        inner = got.astype(F32).reshape(32, 16, LANES)[:, 9, :].astype(BF16)
        for c in range(4):
            lane = lax.broadcasted_iota(jnp.int32, (LANES, width), 0)
            col = lax.broadcasted_iota(jnp.int32, (LANES, width), 1) + c * width
            tile = jnp.where((lane < 4 * lead) & (lane == lax.rem(col, 4 * lead)), 1.0, 0.0).astype(BF16)
            wide = mm(inner, tile)
            owner = lax.broadcasted_iota(jnp.int32, wide.shape, 0)
            place = lax.div(lax.broadcasted_iota(jnp.int32, wide.shape, 1) + c * width, 4 * lead)
            bi[c] = jnp.sum(jnp.where(owner == place, wide, 0.0), axis=0, keepdims=True)

    def square(u):
        return w8[u].reshape(width, width)

    def project(u):
        rows = mm(r.xbuf[...], square(u)) + vec[pl.ds(u, 1), :]
        q3[u] = (rows * jnp.where(u == 0, 0.125, 1.0)).astype(BF16)

    def head_lanes(shape, e):
        return lax.div(lax.broadcasted_iota(jnp.int32, shape, 1), LANES // 2) == e

    ROWS = 256

    def attend(p):
        cols = pl.ds(pl.multiple_of(p * LANES, LANES), LANES)
        sides = []
        for e in range(2):
            mine = head_lanes((frame_count, LANES), e)
            keys = jnp.where(mine, q3[1, :, cols], r.mk[e])
            vals = jnp.where(mine, q3[2, :, cols], jnp.ones((), BF16))
            sides.append((keys, vals))
        for i in range(frame_count // ROWS):
            rows = pl.ds(i * ROWS, ROWS)
            outs = []
            for e in range(2):
                keys, vals = sides[e]
                mine = head_lanes((ROWS, LANES), e)
                query = jnp.where(mine, q3[0, rows, cols], r.mq[e, rows, :])
                scores = mm_nt(query, keys)
                top = jnp.max(scores, axis=1, keepdims=True)
                weights = jnp.exp(scores - top).astype(BF16)
                e12[2 * p + e, rows, :] = weights
                outs.append(mm(weights, vals))
            low = head_lanes((ROWS, LANES), 0)
            over = jnp.where(low, outs[0], outs[1])
            under = pltpu.roll(jnp.where(low, outs[1], outs[0]), LANES // 2, 1)
            inverse = 1.0 / under
            r.linv[rows, cols] = inverse
            r.ctx[rows, cols] = (over * inverse).astype(BF16)

    def norm_one():
        fa[...] = mm(r.ctx[...], square(3))
        r.ctx_t[...] = jnp.transpose(r.ctx[...]).reshape(r.ctx_t.shape)

        def body(rows):
            v = r.xbuf[rows, :].astype(F32) + fa[rows, :] + vec[3:4, :]
            center = v - jnp.mean(v, axis=1, keepdims=True)
            scale = lax.rsqrt(jnp.mean(center * center, axis=1, keepdims=True) + 1e-05)
            normed = center * scale
            r.n1[rows, :] = normed
            r.r1[rows, :] = jnp.broadcast_to(scale, (STEP, LANES))
            r.low[rows, :] = (normed * vec[4:5, :] + vec[5:6, :]).astype(BF16)

        loop(body)
        r.hid_t[...] = jnp.transpose(r.low[...]).reshape(r.hid_t.shape)

    def feed(c):
        fa[...] = mm(r.low[...], square(4 + c))

        def body(rows):
            v = fa[rows, :] + bi[c]
            phi = 0.5 + 0.5 * lax.erf(v * 0.7071067811865476)
            bell = jnp.exp(v * v * -0.5) * 0.3989422804014327
            act[c, rows, :] = (v * phi).astype(BF16)
            gp[c, rows, :] = (phi + v * bell).astype(BF16)

        loop(body, 64)
        act_t[lax.div(c, 2), lax.rem(c, 2)] = jnp.transpose(act[c])

    def block(ref, c):
        return ref[lax.div(c, 2), lax.rem(c, 2)].reshape(width, width)

    def feed_out(k):
        start, size = OUTER[k]
        cols = slice(start, start + size)
        total = None
        for c in range(4):
            one = mm(act[c], w2[c // 2, c % 2, :, :, :, cols].reshape(width, size))
            total = one if total is None else total + one
        fa[:, cols] = total

    def fold(slot, row):
        gsm[pl.ds(row, 1), :] = jnp.sum(cs[slot], axis=0, keepdims=True)

    def norm_two():
        g_in.wait()
        cs[...] = jnp.zeros_like(cs)

        def body(rows):
            hidden = r.n1[rows, :] * vec[4:5, :] + vec[5:6, :]
            v = hidden + fa[rows, :] + vec[6:7, :]
            center = v - jnp.mean(v, axis=1, keepdims=True)
            scale = lax.rsqrt(jnp.mean(center * center, axis=1, keepdims=True) + 1e-05)
            normed = center * scale
            place = lax.broadcasted_iota(jnp.int32, normed.shape, 0) + rows.start
            live = jnp.where(place < l1, 1.0, 0.0)
            r.xbuf[rows, :] = ((normed * vec[7:8, :] + vec[8:9, :]) * live).astype(BF16)
            top = r.gbuf[rows, :].astype(F32) * live
            e = top * vec[7:8, :]
            d = e - jnp.mean(e, axis=1, keepdims=True) - normed * jnp.mean(e * normed, axis=1, keepdims=True)
            d = d * scale
            r.d2[rows, :] = d
            low = d.astype(BF16)
            r.low[rows, :] = low
            cs[0] += eights(top * normed)
            cs[1] += eights(top)
            cs[2] += eights(low.astype(F32))

        loop(body)
        fold(0, 7)
        fold(1, 8)
        fold(2, 6)

    layer_out = pltpu.make_async_copy(r.xbuf, r.layer_out, r.isem.at[0])
    frames_out = pltpu.make_async_copy(r.gbuf, r.frames_grad, r.isem.at[1])

    def back_feed(c):
        fa[...] = mm_nt(r.low[...], block(w2, c))
        cs[0] = jnp.zeros_like(cs[0])

        def body(rows):
            low = (fa[rows, :] * gp[c, rows, :].astype(F32)).astype(BF16)
            gp[c, rows, :] = low
            cs[0] += eights(low.astype(F32))

        loop(body)
        fold(0, 9 + c)

    def grad_square(u, left, right, own):
        core = net.c if own else 1 - net.c
        to = w2.at[u // 2, u % 2] if u < 3 else w8.at[u]
        rows = mm(left[:, core].reshape(2 * pair * NZ, frame_count), right()).reshape(2, pair * NZ, width)
        if own:
            scatter[u].sibling_in().wait_recv()
            rows = rows + to[:, core].astype(F32)
        to[:, core] = rows.astype(BF16)

    def grad_outer(i, own):
        core = net.c if own else 1 - net.c
        start, size = OUTER[i - 8]
        cols = pl.ds(start, size)
        left = act_t[:, core].reshape(2 * width, frame_count)
        rows = mm(left, r.low[:, cols]).reshape((2,) + g2.shape[2:5] + (size,))
        if own:
            scatter[i].sibling_in().wait_recv()
            rows = rows + g2[:, core, :, :, :, cols].astype(F32)
        g2[:, core, :, :, :, cols] = rows.astype(BF16)

    def back_hidden(c):
        got = mm_nt(gp[c], square(4 + c))

        @pl.when(c == 0)
        def _():
            fa[...] = got

        @pl.when(c > 0)
        def _():
            fa[...] += got

    def back_norm_one():
        cs[...] = jnp.zeros_like(cs)

        def body(rows):
            d = r.d2[rows, :] + fa[rows, :]
            normed = r.n1[rows, :]
            e = d * vec[4:5, :]
            cs[0] += eights(d * normed)
            cs[1] += eights(d)
            d = e - jnp.mean(e, axis=1, keepdims=True) - normed * jnp.mean(e * normed, axis=1, keepdims=True)
            d = d * r.r1[rows, 0:1]
            r.d2[rows, :] = d
            low = d.astype(BF16)
            r.low[rows, :] = low
            cs[2] += eights(low.astype(F32))

        loop(body)
        fold(0, 4)
        fold(1, 5)
        fold(2, 3)

    def back_context():
        act[3] = mm_nt(r.low[...], square(3)).astype(BF16)

    def back_attend(p):
        cols = pl.ds(pl.multiple_of(p * LANES, LANES), LANES)
        shape = (frame_count, LANES)
        low = head_lanes(shape, 0)
        scaled = (act[3, :, cols].astype(F32) * r.linv[:, cols]).astype(BF16)
        product = scaled.astype(F32) * r.ctx[:, cols].astype(F32)
        lane = lax.broadcasted_iota(jnp.int32, shape, 1)
        k2, v2, q2 = q3[1, :, cols], q3[2, :, cols], q3[0, :, cols]
        dq, dk, dv = [], [], []
        for e in range(2):
            mine = head_lanes(shape, e)
            spare = lane - (1 - e) * (LANES // 2)
            dot = jnp.sum(jnp.where(mine, product, 0.0), axis=1, keepdims=True)
            high = dot.astype(BF16).astype(F32)
            extra = jnp.where(spare == 0, high, jnp.where(spare == 1, dot - high, 0.0)).astype(BF16)
            left = jnp.where(mine, scaled, extra)
            minus = jnp.where((spare == 0) | (spare == 1), -1.0, 0.0).astype(BF16)
            right = jnp.where(mine, v2, minus)
            for i in range(frame_count // ROWS):
                part = slice(i * ROWS, (i + 1) * ROWS)
                r.ds[e, part, :] = (e12[2 * p + e, part, :].astype(F32) * mm_nt(left[part], right)).astype(BF16)
            dq.append(mm(r.ds[e], k2))
            dk.append(mm_tn(r.ds[e], q2))
            dv.append(mm_tn(e12[2 * p + e], scaled))
        act[0, :, cols] = (jnp.where(low, dq[0], dq[1]) * 0.125).astype(BF16)
        act[1, :, cols] = jnp.where(low, dk[0], dk[1]).astype(BF16)
        act[2, :, cols] = jnp.where(low, dv[0], dv[1]).astype(BF16)

    def bias_sums():
        cs[...] = jnp.zeros_like(cs)

        def body(rows):
            cs[0] += eights(act[0, rows, :].astype(F32))
            cs[1] += eights(act[2, rows, :].astype(F32))

        loop(body)
        fold(0, 0)
        fold(1, 2)
        gsm[1:2, :] = jnp.zeros((1, width), F32)
        gsm[13:16, :] = jnp.zeros((3, width), F32)

    def back_frames(k):
        r.d2[...] += mm_nt(act[k], square(k))

    def frames_ready():
        layer_out.wait()

        def body(rows):
            r.gbuf[rows, :] = r.d2[rows, :].astype(BF16)

        loop(body)
        frames_out.start()

    def small_copy(k, device):
        return pltpu.make_async_remote_copy(
            src_ref=r.sm.at[k], dst_ref=r.sl.at[k], send_sem=r.sms.at[0], recv_sem=r.smr.at[k],
            device_id=device, device_id_type=MESH)

    def small_step(k):
        if k == 0:
            r.sm[0] = gsm[...].astype(BF16)
        else:
            r.sm[k] = (r.sm[k - 1].astype(F32) + r.sl[k - 1].astype(F32)).astype(BF16)
        if k < 3:
            small_copy(k, net.across("cyx"[k])).start()

    def small_wait(k):
        small_copy(k, net.across("cyx"[k])).wait_recv()

    def small_line(k):
        return pltpu.make_async_remote_copy(
            src_ref=r.sm.at[3], dst_ref=r.sl.at[2 + k], send_sem=r.sms.at[0], recv_sem=r.smr.at[3],
            device_id=net.dev(z=lax.rem(net.z + k, NZ)), device_id_type=MESH)

    def small_total():
        landed = r.sl.at[pl.ds(3, NZ - 1)]
        pltpu.make_async_remote_copy(
            src_ref=landed, dst_ref=landed, send_sem=r.sms.at[0], recv_sem=r.smr.at[3], device_id=net.across("c"),
            device_id_type=MESH).wait_recv()
        whole = sum((r.sl[k].astype(F32) for k in range(3, 6)), r.sm[3].astype(F32))
        index = (net.y * 2 + net.c) * 2 * NZ + net.z * 2 + net.x
        turned = pltpu.roll(whole, lax.rem(width - index * lead, width), 1)
        row = lax.broadcasted_iota(jnp.int32, (16, width), 0)
        block = lax.div(index, 8)
        inner = jnp.sum(jnp.where(row == 9 + block, whole, 0.0), axis=0, keepdims=True)
        inner = pltpu.roll(jnp.broadcast_to(inner, (8, width)), lax.rem(width - lax.rem(index, 8) * 4 * lead, width), 1)
        r.gsmall[0:8, :] = turned[0:8, :LANES]
        r.gsmall[8:16, :] = jnp.where(row[:8, :LANES] == 0, turned[8:9, :LANES], inner[:, :LANES])

    def swap_back(u):
        return pltpu.make_async_remote_copy(
            src_ref=r.ys.at[u], dst_ref=r.yr.at[u], send_sem=r.yss.at[0], recv_sem=r.yrs.at[0],
            device_id=net.across("x"), device_id_type=MESH)

    def out_of(u):
        if u < 4:
            return (r.gwq, r.gwk, r.gwv, r.gwo)[u], 0
        return r.gwi, (u - 4) * width

    def total_square(u):
        r.f8[...] = scatter[u].total()
        out, start = out_of(u)
        mine, theirs = pl.multiple_of(net.x * lead, 8), pl.multiple_of((1 - net.x) * lead, 8)
        r.ys[u] = jnp.concatenate([r.f8[pl.ds(theirs, lead), :], jnp.zeros((8, half), F32)], axis=0).astype(BF16)
        swap_back(u).start()
        out[:, pl.ds(pl.multiple_of(start + net.x * half, LANES), half)] = r.f8[pl.ds(mine, lead), :]

    def last():
        pltpu.make_async_remote_copy(
            src_ref=r.ys, dst_ref=r.yr, send_sem=r.yss.at[0], recv_sem=r.yrs.at[0], device_id=net.across("x"),
            device_id_type=MESH).wait_recv()
        for u in range(8):
            out, start = out_of(u)
            out[:, pl.ds(pl.multiple_of(start + (1 - net.x) * half, LANES), half)] = r.yr[u].astype(F32)[:lead]

    def total_outer(i):
        r.gwouter[:, pl.ds(*OUTER[i - 8])] = scatter[i].total()

    def unit(i, left=None, right=None):
        steps = SimpleNamespace(**gather[i])
        if i == len(UNITS) - 1:
            return steps
        way, square = scatter[i], i < 8

        def half_of(own):
            if square:
                grad_square(i, left, right, own)
            else:
                grad_outer(i, own)

        def away():
            half_of(False)
            way.sibling_out().start()

        def home():
            half_of(True)
            way.spread()

        steps.away, steps.home = away, home
        steps.t, steps.u, steps.v = way.fold_first, way.fold_second, way.fold_third
        if square:
            steps.p = functools.partial(merge, i)
            steps.x = functools.partial(total_square, i)
        else:
            steps.x = functools.partial(total_outer, i)
        return steps

    def give(k):
        pl.semaphore_signal(r.free.at[k], inc=1, device_id=net.across("c"), device_id_type=MESH)

    def take(k):
        pl.semaphore_wait(r.free.at[k], 1)

    def turn():
        x_in.wait()
        r.xt[...] = jnp.transpose(r.xbuf[...]).reshape(r.xt.shape)

    def gather_end():
        kinds = ((range(8), pair * half, half), (range(8, 12), lead * 4 * LANES, 2 * LANES), (range(12, 13), 16 * LANES, LANES))
        for kind, (units, count, run) in enumerate(kinds):
            flat = lines = 0
            for i in units:
                size = count * (OUTER[i - 8][1] // LANES if kind == 1 else 1)
                flat += size * (12 if GATHER[i][0] == "z" else 9)
                lines += size * (2 if GATHER[i][0] == "z" else 4)
            sent(stretch(e12, flat, run), r.gout.at[kind])
            inside = (net.z > 0) & (net.z < NZ - 1)
            for way, times in ((inside, 2), (jnp.logical_not(inside), 1)):
                pl.when(way)(functools.partial(sent, stretch(e12, lines * times, run), r.gline.at[kind]))
        mates_sent(r.gmate)
        sent(r.small.at[:, 0], r.gmate.at[2])

    def small(k):
        if k > 0:
            small_wait(k - 1)
        small_step(k)
        if k == 3:
            for one in range(1, NZ):
                small_line(one).start()

    def end():
        sent(stretch(e12, 8 * 15 * pair * half, half), r.sout.at[0])
        sent(stretch(e12, 15 * 4 * lead * width, 2 * LANES), r.sout.at[1])
        mates_sent(r.smate)
        sent(r.xs, r.xss.at[0])
        sent(r.ys, r.yss.at[0])
        sent(r.sl, r.sms.at[0])
        frames_out.wait()

    def rolled(count, body):
        def one(i, carry):
            body(i)
            return carry

        lax.fori_loop(0, count, one, 0)

    def go(*steps):
        for step in steps:
            step()

    q, k, v = (unit(u, r.xt, lambda u=u: act[u]) for u in range(3))
    o = unit(3, r.ctx_t, lambda: r.low[...])
    i0, i1, i2, i3 = (unit(4 + u, r.hid_t, lambda u=u: gp[u]) for u in range(4))
    w0, w1, w2_, w3 = (unit(8 + u) for u in range(4))
    s = unit(12)
    place()
    go(w3.a, w1.a, w3.b, s.a, q.p, q.a, w3.c, s.b, q.b, v.p, i1.p, i1.a)
    go(k.p, i0.p, k.a, q.c, v.a, w0.a, k.b, w3.d, s.c, k.c, w2_.a, i3.p)
    go(i0.a, q.d, o.p, o.a, i2.p, w3.e, s.d, v.b, i3.a, k.d, i2.a, s.e)
    go(i0.b, v.c, i0.c, o.b, w3.g, q.e, q.g, i2.b, s.g, k.e, i3.b, v.d)
    vectors()
    go(i1.b, i3.c)

    def project_run(i):
        project(i)

        @pl.when(i == 0)
        def _():
            go(k.g, o.c)

        @pl.when(i == 1)
        def _():
            go(i0.d, i2.c, v.e, w1.b, o.d, i1.c, v.g, i3.d)

    rolled(3, project_run)
    go(w2_.b)

    def attend_run(i):
        attend(i)

        @pl.when(i == 1)
        def _():
            go(w0.b, i1.d)

        @pl.when(i == 4)
        def _():
            go(w1.c, i2.d, i0.e, i3.e, w1.d, w2_.c, w0.c, o.e)

    rolled(6, attend_run)
    go(w0.d, i0.g, i1.e, o.g)
    norm_one()
    go(i2.e)

    def feed_run(i):
        feed(i)

        @pl.when(i == 0)
        def _():
            go(w2_.d, i1.g, i2.g)

        @pl.when(i == 1)
        def _():
            go(w1.e)

        @pl.when(i == 2)
        def _():
            go(i3.g, w0.e)

    rolled(4, feed_run)
    go(w2_.e, w1.g)
    feed_out(1)
    feed_out(3)
    go(w0.g)
    feed_out(0)
    go(w2_.g)
    feed_out(2)
    norm_two()
    go(w2_.away)
    gather_end()
    go(w3.away, w0.away, w1.away, w2_.home)

    def back_feed_run(i):
        back_feed(i)

        @pl.when(i == 1)
        def _():
            go(w3.home, w0.home)

        @pl.when(i == 2)
        def _():
            go(w2_.t, w1.home)

    rolled(4, back_feed_run)

    def back_hidden_run(i):
        back_hidden(i)

        @pl.when(i == 0)
        def _():
            go(w3.t)

    rolled(4, back_hidden_run)
    give(1)
    layer_out.start()
    take(1)
    go(i0.away, w1.t)
    give(0)
    go(i1.away, w0.t)
    back_norm_one()
    go(i0.home, i2.away, i1.home, i3.away)
    back_context()
    go(w1.u, w1.v)

    def back_attend_run(i):
        back_attend(i)

        @pl.when(i == 0)
        def _():
            give(2)
            take(2)
            go(i3.home, i2.home, o.away)

        @pl.when(i == 1)
        def _():
            take(0)

        @pl.when(i == 2)
        def _():
            go(i1.t, o.home)

        @pl.when(i == 3)
        def _():
            go(i0.t, i3.t, i2.t)

    rolled(6, back_attend_run)
    go(w1.x, q.away, o.t)

    def back_frames_run(i):
        back_frames(i)

        @pl.when(i == 0)
        def _():
            go(i2.u, v.away, q.home)
            bias_sums()
            go(v.home, k.away, i2.v, o.u, k.home, i3.u, i3.v, q.t, q.u, o.v, k.t, i0.u)
            go(q.v)
            small(0)
            go(v.t, w2_.u, i1.u, k.u, i2.x, i0.v, v.u, k.v)
            small(1)
            go(w3.u, i3.x)

        @pl.when(i == 1)
        def _():
            go(i1.v)
            small(2)
            go(v.v, w0.u, q.x, w3.v, i1.x)
            small(3)
            go(w2_.v, o.x, i0.x, w0.v, k.x, w2_.x, v.x, w0.x, w3.x)

    rolled(3, back_frames_run)
    frames_ready()
    small_total()
    last()
    end()


def kernel_device(
    frames, lengths, query_weight, query_bias, key_weight, value_weight, value_bias, output_weight, output_bias,
    first_gain, first_shift, inner_weight, inner_bias, outer_weight, outer_bias, second_gain, second_shift, grad_out,
):
    count, width = frames.shape
    lead = query_weight.shape[0]
    pair, half = 2 * lead, width // 2
    vmem, hbm = pl.BlockSpec(memory_space=pltpu.VMEM), pl.BlockSpec(memory_space=pl.ANY)
    smem = pl.BlockSpec(memory_space=pltpu.SMEM)
    args = dict(
        frames=(hbm, frames), grad_out=(hbm, grad_out), lengths=(smem, lengths), wq=(vmem, query_weight),
        wk=(vmem, key_weight), wv=(vmem, value_weight), wo=(vmem, output_weight), wi=(vmem, inner_weight),
        wouter=(vmem, outer_weight), bq=(vmem, query_bias), bv=(vmem, value_bias), bo=(vmem, output_bias),
        g1=(vmem, first_gain), s1=(vmem, first_shift), b2=(vmem, outer_bias), gg2=(vmem, second_gain),
        s2=(vmem, second_shift), bi1=(vmem, inner_bias))
    shape = jax.ShapeDtypeStruct
    outs = dict(
        layer_out=(hbm, shape((count, width), BF16)), frames_grad=(hbm, shape((count, width), BF16)),
        gwq=(vmem, shape((lead, width), F32)), gwk=(vmem, shape((lead, width), F32)),
        gwv=(vmem, shape((lead, width), F32)), gwo=(vmem, shape((lead, width), F32)),
        gwi=(vmem, shape(inner_weight.shape, F32)), gwouter=(vmem, shape(outer_weight.shape, F32)),
        gsmall=(vmem, shape((16, LANES), F32)))
    dma = pltpu.SemaphoreType.DMA
    big = (count, width)
    square = (2, 2, pair * NZ, width)
    turned = (2, 2, pair * NZ, count)
    lead_shape = (2, 2, 2, 2, 8 * lead, width)
    scratch = dict(
        w8=((8,) + square, BF16), w2=(lead_shape, BF16), g2=(lead_shape, BF16), small=((2, 2, NZ, 2, 16, LANES), BF16),
        pack=((16, LANES), F32), xs=((8, lead + 8, half), BF16), xr=((8, lead + 8, half), BF16),
        ys=((8, lead + 8, half), BF16), yr=((8, lead + 8, half), BF16), xbuf=(big, BF16), gbuf=(big, BF16), q3=((3,) + big, BF16),
        e12=((HEADS, count, count), BF16), linv=(big, F32), ctx=(big, BF16), xt=(turned, BF16), ctx_t=(turned, BF16),
        hid_t=(turned, BF16), low=(big, BF16), n1=(big, F32), r1=((count, LANES), F32), act=((4,) + big, BF16),
        gp=((4,) + big, BF16), act_t=((2, 2, width, count), BF16), fa=(big, F32), d2=(big, F32),
        ds=((2, count, count), BF16), mq=((2, count, LANES), BF16), mk=((2, count, LANES), BF16), vec=((16, width), F32),
        bi=((4, 1, width), F32), gsm=((16, width), F32), cs=((3, 8, width), F32), sm=((4, 16, width), BF16),
        sl=((6, 16, width), BF16), f8=((pair, half), F32))
    for i in range(12):
        for kind, size in zip(LANDING, landing_shapes(i, pair, half, 4 * lead), strict=True):
            scratch[f"{kind}{i}"] = (size, BF16)
    scratch = {k: pltpu.VMEM(*v) for k, v in scratch.items()}
    scratch.update(
        gout=dma((3,)), gline=dma((3,)), gmate=dma((3,)), grecv=dma((13, 5)), sout=dma((2,)), smate=dma((2,)), srecv=dma((12, 5)),
        xss=dma((1,)), xrs=dma((8,)), yss=dma((1,)), yrs=dma((1,)), sms=dma((1,)), smr=dma((4,)), isem=dma((2,)), free=pltpu.SemaphoreType.REGULAR((3,)))
    got = pl.pallas_call(
        functools.partial(layer_kernel, (*args, *outs, *scratch)),
        out_shape=[o[1] for o in outs.values()],
        in_specs=[a[0] for a in args.values()],
        out_specs=[o[0] for o in outs.values()],
        scratch_shapes=list(scratch.values()),
        compiler_params=pltpu.CompilerParams(collective_id=0, has_side_effects=True, vmem_limit_bytes=VMEM_BYTES),
    )(*(a[1] for a in args.values()))

    bias, wide = shape((lead,), F32), shape((4 * lead,), F32)
    vectors = {3: bias, 6: bias, 8: bias, 9: bias, 10: bias, 12: wide, 14: bias, 15: bias, 16: bias}
    row_of = {3: 0, 6: 2, 8: 3, 9: 4, 10: 5, 12: 9, 14: 6, 15: 7, 16: 8}
    places = [i for i in range(17) if i not in vectors]

    def publish(*refs):
        came, small, out = refs[:8], refs[8], refs[9:]
        for a, i in zip(came, places, strict=True):
            out[i][...] = a[...]
        for i, row in row_of.items():
            size = vectors[i].shape[0]
            out[i][...] = small[row:row + 1, :size].reshape(size)

    whole = dict(zip(places, (o[1] for o in list(outs.values())[:8]), strict=True))
    return tuple(pl.pallas_call(
        publish,
        out_shape=[vectors[i] if i in vectors else whole[i] for i in range(17)],
        in_specs=[vmem] * 9,
        out_specs=[vmem] * 17,
    )(*got))


VMEM_BYTES = 63 << 20


def solution(mesh):
    split = P(("dp", "fsdp"))
    rows = P(("dp", "fsdp"), None)
    in_specs = (
        rows, rows, rows, split, rows, rows, split, rows, split, split, split, rows, split, rows, split, split, split, rows,
    )
    out_specs = (
        rows, rows, rows, split, rows, rows, split, rows, split, split, split, rows, split, rows, split, split, split,
    )
    fits = mesh.shape["dp"] == 4 and mesh.shape["fsdp"] == 2 * NZ

    def per_device(frames, lengths, query_weight, *rest):
        lead, width = query_weight.shape
        good = fits and lead % 8 == 0 and 4 * lead <= LANES and width == 768
        run = kernel_device if good else general_device
        return run(frames, lengths, query_weight, *rest)

    return jax.shard_map(per_device, mesh=mesh, in_specs=in_specs, out_specs=out_specs, check_vma=False)
```
